128 devices in a mesh: gx: 8 (over z_hi, y), gy: 16 (over x, z_lo, core).
Axes of the slice: x: 4, y: 4, z: 4 (z_hi: 2, z_lo: 2; z = z_hi * 2 + z_lo), core: 2. Of those that a mesh axis runs over, the one named last changes fastest.
Arguments:
- src_value: bfloat16 [32, 1048576], P(None, ('gx', 'gy')), may hold values from -6 to 6
- src_point: int32 [2, 1048576], P(None, ('gx', 'gy')), may hold values from 0 to 255
- src_owner: int32 [1048576, 1], P(('gx', 'gy')), may hold values from 0 to 127; in each aligned block of 8192 rows (0 to 8191, 8192 to 16383, ...) at most 128 rows name the same one
- translation: bfloat16 [11, 2, 2, 2, 4096], replicated, may hold values from -0.375 to 0.375
Outputs:
- box_weights: bfloat16 [128, 8, 16, 4096], P(None, 'gx', 'gy')
The draws below stay inside these ranges and needn't reach their ends.
Inputs may be any that keep to these rules, and one draw needn't show every extreme that they name: `src_owner`: among the sources listed on one device, at most 128 have the same owner, and exactly 128 do for some owner on some device.
All inputs are finite; a program needn't handle non-finite values.
Results may differ from the reference program's by a relative error of at most 0.023.
Values may be sent and summed in bfloat16 or wider, within the bound.
No kernel may reach another device: no remote copies, remote signals or barrier semaphores. Data moves between devices by JAX's collectives and lax.ppermute only.
A program may use at most 128 MiB of HBM per device.

```python
import math
import jax
import jax.numpy as jnp
import numpy as np
from jax import lax

QX = 8
R = 64
CH = 16
LEVX = 4
LB = 16
LAT = 16
CAP = 128
SRC_DEV = 8192
SOURCES = 1048576
LEVELS = 11
NXB = 128
NYB = 256
N_GX = 8
N_GY = 16


def set_ends(result, stream_key, least, high):
    spot = [jax.random.randint(jax.random.fold_in(stream_key, axis), (), 0, length) for axis, length in enumerate(result.shape)]
    main_axis = result.shape.index(max(result.shape))
    neighbour = spot[:main_axis] + [(spot[main_axis] + 1) % result.shape[main_axis]] + spot[main_axis + 1:]
    return result.at[tuple(spot)].set(least).at[tuple(neighbour)].set(high)


def block_levels(rng, shape, split, low, largest):
    level = 1.0
    for dim, shards_of in split:
        steps = jax.random.uniform(jax.random.fold_in(jax.random.fold_in(rng, 6), dim), (shards_of,), jnp.float32, low / len(split), largest / len(split))
        level = level * jnp.repeat(jnp.exp(steps), shape[dim] // shards_of).reshape((-1,) + (1,) * (len(shape) - 1 - dim))
    return level


def shared_out(key, own, number, rows, amount, top, most, skew):
    order = jax.random.permutation(key, amount)
    packed, common = load_shares(amount, rows * top, most, skew, True), load_shares(amount, rows * top, most, skew, False)
    places = jnp.arange(amount)

    def named(sizes, rotation):
        used = int((sizes > 0).sum())
        fixed = max(1, used // 4)
        moved = fixed + (places - fixed + rotation * (used - fixed)) % max(1, amount - fixed)
        return jnp.zeros((amount,), jnp.int32).at[order[jnp.where(places < fixed, places, moved)]].set(jnp.asarray(sizes, jnp.int32))

    sizes = jnp.where(number % 4 == 0, named(packed, number // 4), named(common, number - number // 4 - 1))
    mixed = jax.random.permutation(jax.random.fold_in(own, 3), amount)
    donor, receiver = mixed[0:amount // 2 * 2:2], mixed[1:amount // 2 * 2:2]
    slack = jnp.minimum(sizes[donor] - 1, most - sizes[receiver]) // 2
    slack = jnp.where((donor == order[0]) | (receiver == order[0]) | (sizes[receiver] == 0), 0, jnp.maximum(slack, 0))
    moved = jax.random.randint(jax.random.fold_in(own, 4), (amount // 2,), 0, 1 << 20) % (slack + 1)
    sizes = sizes.at[donor].add(-moved).at[receiver].add(moved)
    members = jnp.searchsorted(jnp.cumsum(sizes), jnp.arange(rows * top), side="right").astype(jnp.int32)
    listing = members.reshape(top, rows).T
    listing = listing[jax.random.permutation(jax.random.fold_in(own, 1), rows)]
    rotation = jax.random.randint(jax.random.fold_in(own, 2), (rows, 1), 0, top)
    return jnp.take_along_axis(listing, (jnp.arange(top)[None, :] + rotation) % top, axis=1)


def load_shares(count, total, reach, slope, full):
    portions = [(1 << 20) // math.isqrt(rank ** slope) + 1 for rank in range(1, count + 1)]
    largest = reach if full else min(reach, max(-(-total // count), total * portions[0] // sum(portions)))
    least = 1 if total - largest >= count - 1 else 0
    holding, surplus = [largest] + [least] * (count - 1), total - largest - least * (count - 1)
    while surplus > 0:
        movable = [i for i in range(1, count) if holding[i] < largest] or [i for i in range(1, count) if holding[i] < reach]
        whole, remaining = sum([portions[i] for i in movable]), surplus
        for i in movable:
            extra = min(reach - holding[i], max(1, remaining * portions[i] // whole), surplus)
            holding[i] = holding[i] + extra
            surplus = surplus - extra
    return np.array(holding)


def centred(own_key, shape, scale, most, shards=(), held_as=jnp.bfloat16):
    factor_of = block_levels(own_key, shape, shards, -0.22, 0.18) if shards else 1.0
    result = jax.random.normal(own_key, shape, jnp.float32) * scale * factor_of
    return jnp.minimum(jnp.maximum(result, -most), most).astype(held_as)


def setup_inputs(seed: int = 0) -> dict:
    arg_keys = jax.random.split(jax.random.key(seed), 5)
    src_value = centred(arg_keys[0], (2 * CH, SOURCES), 1.0, 6.0, ((1, 128),))
    src_point = set_ends(jax.random.randint(arg_keys[1], (2, SOURCES), 0, LB * LAT), jax.random.fold_in(arg_keys[1], 1), 0, (LB * LAT) - 1).astype(jnp.int32)
    src_owner_keys = jax.random.split(jax.random.fold_in(arg_keys[2], 1), SOURCES // SRC_DEV)
    src_owner_turns = jax.random.permutation(jax.random.fold_in(arg_keys[2], 3), SOURCES // SRC_DEV)
    src_owner = jax.vmap(lambda own, number: shared_out(jax.random.fold_in(arg_keys[2], 2), own, number, SRC_DEV, N_GX * N_GY, 1, CAP, 2))(src_owner_keys, src_owner_turns).reshape((SOURCES, 1))
    translation = centred(arg_keys[3], (LEVELS, 2, 2, 2, R * R), (4 * R) ** -0.5, 0.375)
    return dict(src_value=src_value, src_point=src_point, src_owner=src_owner, translation=translation)


phase_modulus = 61


def chebyshev(count):
    index = jnp.arange(count, dtype=jnp.float32)
    return 0.5 + 0.5 * jnp.cos(math.pi * (2.0 * index + 1.0) / (2.0 * count))


def lagrange(position, count):
    nodes = chebyshev(count)
    rows_out = []
    for first in range(count):
        term = jnp.ones_like(position)
        for second in range(count):
            if second != first:
                term = term * (position - nodes[second]) / (nodes[first] - nodes[second])
        rows_out.append(term)
    return jnp.stack(rows_out)


def phase_angle(parents, targets):
    product = (parents[:, None] * targets[None, :]) % phase_modulus
    return (2.0 * math.pi / phase_modulus) * product.astype(jnp.float32)


def rotate(values, angle):
    half = values.shape[0] // 2
    cosine = jnp.cos(angle)
    sine = jnp.sin(angle)
    upper = values[:half]
    lower = values[half:]
    return jnp.concatenate([upper * cosine - lower * sine, upper * sine + lower * cosine], axis=0).astype(jnp.bfloat16)


def block_matrix(translation, level):
    parts = translation[level].reshape(2, 2, 2, R, R)
    real_part = parts[:, :, 0]
    imag_part = parts[:, :, 1]
    top = jnp.concatenate([real_part, -imag_part], axis=3)
    bottom = jnp.concatenate([imag_part, real_part], axis=3)
    return jnp.concatenate([top, bottom], axis=2)


def level_x(weights, mats, offset):
    rows, sx, sy, tx, ty, fields = weights.shape
    pieces = weights.reshape(rows, sx // 2, 2, sy, tx, ty, fields).astype(jnp.float32)
    out = jnp.einsum('tcoi,ipcsxyh->opsxtyh', mats.astype(jnp.float32), pieces)
    out = out.reshape(rows, sx // 2, sy, 2 * tx, ty, fields)
    parents = offset * (sx // 2) + jnp.arange(sx // 2, dtype=jnp.int32)
    angle = phase_angle(parents, jnp.arange(2 * tx, dtype=jnp.int32))
    return rotate(out, angle[None, :, None, :, None, None])


def level_y(weights, mats, offset):
    rows, sx, sy, tx, ty, fields = weights.shape
    pieces = weights.reshape(rows, sx, sy // 2, 2, tx, ty, fields).astype(jnp.float32)
    out = jnp.einsum('tcoi,ispcxyh->ospxyth', mats.astype(jnp.float32), pieces)
    out = out.reshape(rows, sx, sy // 2, tx, 2 * ty, fields)
    parents = offset * (sy // 2) + jnp.arange(sy // 2, dtype=jnp.int32)
    angle = phase_angle(parents, jnp.arange(2 * ty, dtype=jnp.int32))
    return rotate(out, angle[None, None, :, None, :, None])


def reference(src_value, src_point, src_owner, translation):
    devices = N_GX * N_GY
    owner = src_owner[:, 0].reshape(devices, SRC_DEV)
    values = src_value.reshape(2 * CH, devices, SRC_DEV).transpose(1, 0, 2)
    points = src_point.reshape(2, devices, SRC_DEV).transpose(1, 0, 2)

    def absorb(carry, block):
        vals, pts, dest = block
        col_a = dest // N_GY
        col_b = dest % N_GY
        px = pts[0]
        py = pts[1]
        leaf_id = (col_a * LB + px // LAT) * NYB + col_b * LB + py // LAT
        u = ((px % LAT).astype(jnp.float32) + 0.5) / LAT
        v = ((py % LAT).astype(jnp.float32) + 0.5) / LAT
        weights_x = lagrange(u, QX)
        weights_y = lax.optimization_barrier(lagrange(v, QX).astype(jnp.bfloat16)).astype(jnp.float32)
        glob_x = col_a * (LB * LAT) + px
        glob_y = col_b * (LB * LAT) + py
        angle = (2.0 * math.pi / phase_modulus) * ((glob_x * glob_y) % phase_modulus).astype(jnp.float32)
        source = vals.astype(jnp.float32).reshape(2, CH, SRC_DEV)
        cosine = jnp.cos(angle)
        sine = jnp.sin(angle)
        charge = jnp.stack([cosine * source[0] - sine * source[1], sine * source[0] + cosine * source[1]])
        spread = weights_x[None, :, None, :] * charge[:, None, :, :]
        spread = lax.optimization_barrier(spread.astype(jnp.bfloat16)).astype(jnp.float32)
        contrib = spread[:, :, None, :, :] * weights_y[None, None, :, None, :]
        contrib = contrib.reshape(2 * R * CH, SRC_DEV).T
        return carry.at[leaf_id].add(contrib), None

    start = jnp.zeros((NXB * NYB, 2 * R * CH), jnp.float32)
    total, _ = lax.scan(absorb, start, (values, points, owner))
    weights = total.reshape(NXB, NYB, 2, QX, QX, CH).transpose(2, 3, 4, 0, 1, 5)
    weights = weights.reshape(2 * R, NXB, NYB, 1, 1, CH).astype(jnp.bfloat16)
    for step in range(LEVX):
        weights = level_x(weights, block_matrix(translation, 2 * step), 0)
        weights = level_y(weights, block_matrix(translation, 2 * step + 1), 0)
    weights = level_x(weights, block_matrix(translation, 2 * LEVX), 0)
    weights = level_y(weights, block_matrix(translation, 2 * LEVX + 1), 0)
    weights = level_x(weights, block_matrix(translation, 2 * LEVX + 2), 0)
    final = weights.reshape(2 * R, N_GX // 4, N_GY // 2, LB, 2, 2, LB, 2, CH)
    final = final.transpose(0, 1, 5, 4, 2, 7, 3, 6, 8)
    return final.reshape(2 * R, N_GX, N_GY, LB * LB * CH)
```

```python
import math

import jax
import jax.numpy as jnp
from jax import lax
from jax.experimental import pallas as pl
from jax.experimental.pallas import tpu as pltpu
from jax.sharding import PartitionSpec as P

QX = 8
R = 64
LEVX = 4
LB = 16
LAT = 16
CAP = 128

F32 = jnp.float32
BF16 = jnp.bfloat16
MODULUS = 61.0

ROUTE_STEP = 1024
ROUTE_BLOCK = 256
LEAF_SOURCES = 8
MIB = 1024 * 1024


def matmul_nt(lhs, rhs):
    return lax.dot_general(lhs, rhs, (((1,), (1,)), ((), ())), preferred_element_type=F32)


def unit_phase(product):
    rest = product - MODULUS * jnp.floor(product * (1.0 / MODULUS) + 0.5)
    x = rest * (math.pi / MODULUS)
    x2 = x * x
    s = x * (1.0 + x2 * (-1 / 6 + x2 * (1 / 120 + x2 * (-1 / 5040 + x2 * (1 / 362880 + x2 * (-1 / 39916800))))))
    c = 1.0 + x2 * (-1 / 2 + x2 * (1 / 24 + x2 * (-1 / 720 + x2 * (1 / 40320 + x2 * (-1 / 3628800)))))
    return 1.0 - 2.0 * s * s, 2.0 * s * c


def iota(shape, dim):
    return lax.broadcasted_iota(jnp.int32, shape, dim)


def reversed_bits(value, bits):
    out = 0
    for bit in range(bits):
        out |= (value >> bit & 1) << (bits - 1 - bit)
    return out


def nibble_reversed(value):
    return (value & 1) << 3 | (value & 2) << 1 | value >> 1 & 2 | value >> 3 & 1


def route_kernel(own_ref, point_ref, value_ref, send_ref, acc, carry, tri, points, left, right):
    step = pl.program_id(0)
    width = ROUTE_BLOCK

    @pl.when(step == 0)
    def _():
        acc[...] = jnp.zeros_like(acc)
        carry[...] = jnp.zeros_like(carry)
        earlier = (iota((width, width + 128), 0) < iota((width, width + 128), 1))
        earlier = earlier | (iota((width, width + 128), 1) >= width)
        tri[...] = jnp.where(earlier, 1.0, 0.0).astype(BF16)

    rows = iota((128, width), 0)
    for block in range(ROUTE_STEP // width):
        span = pl.ds(block * width, width)
        own = own_ref[0:1, span]
        hit = rows == own
        counts = jnp.dot(
            jnp.where(hit, 1.0, 0.0).astype(BF16), tri[...], preferred_element_type=F32
        )
        held = carry[...]
        before = counts[:, :width] + jnp.concatenate([held] * (width // 128), axis=1)
        rank = jnp.sum(jnp.where(hit, before, 0.0), axis=0, keepdims=True)
        carry[...] = held + counts[:, width:]

        sibling = own >> 4 & 3
        low = (own >> 6) * 16 + (own & 15)
        place = jnp.where(rows.astype(F32) == rank, 1.0, 0.0)
        for y in range(4):
            right[y * 128 : (y + 1) * 128, span] = jnp.where(sibling == y, place, 0.0).astype(BF16)

        px = point_ref[0:1, span]
        py = point_ref[1:2, span]
        big_x = (own >> 4) * (LB * LAT) + px
        big_y = (own & 15) * (LB * LAT) + py
        cosine, sine = unit_phase(big_x.astype(F32) * big_y.astype(F32))
        real = value_ref[0:16, span].astype(F32)
        imag = value_ref[16:32, span].astype(F32)
        turned_real = cosine * real - sine * imag
        turned_imag = sine * real + cosine * imag
        parts = []
        for group in range(4):
            parts.append(turned_real[4 * group : 4 * group + 4])
            parts.append(turned_imag[4 * group : 4 * group + 4])
        charge = jnp.concatenate(parts, axis=0).astype(BF16)
        box = (nibble_reversed(px >> 4) * 16 + nibble_reversed(py >> 4)).astype(F32)
        offset = ((px & 15) * 16 + (py & 15)).astype(F32)
        mine = jnp.where(iota((32, width), 0) == low, 1.0, 0.0)
        left[1024:1056, span] = (mine * box).astype(BF16)
        left[1056:1088, span] = (mine * offset).astype(BF16)
        for number in range(32):
            mask = jnp.where(low == number, 1.0, 0.0).astype(BF16)
            left[number * 32 : (number + 1) * 32, span] = charge * mask

    acc[...] += matmul_nt(left[...], right[...])

    @pl.when(step == pl.num_programs(0) - 1)
    def _():
        for y in range(4):
            points[y] = acc[1024:1088, y * 128 : (y + 1) * 128]

        def one(number, carried):
            high = number // 16
            gy = number % 16
            taken = [
                points[y, pl.ds(32 * kind + number, 1), :]
                for kind in range(2)
                for y in range(4)
            ]
            taken = jnp.concatenate(taken, axis=0).astype(BF16)
            for group in range(4):
                dest = high * 64 + group * 16 + gy
                base = pl.multiple_of(number * 32 + group * 8, 8)
                for y in range(4):
                    send_ref[dest, y] = acc[pl.ds(base, 8), y * 128 : (y + 1) * 128].astype(BF16)
                send_ref[dest, 4] = taken
            return carried

        lax.fori_loop(0, 32, one, 0)


def route(owner, point, value):
    sources = owner.shape[1]
    return pl.pallas_call(
        route_kernel,
        grid=(sources // ROUTE_STEP,),
        in_specs=[
            pl.BlockSpec((1, ROUTE_STEP), lambda i: (0, i)),
            pl.BlockSpec((2, ROUTE_STEP), lambda i: (0, i)),
            pl.BlockSpec((32, ROUTE_STEP), lambda i: (0, i)),
        ],
        out_specs=pl.BlockSpec((128, 5, 8, 128), lambda i: (0, 0, 0, 0)),
        out_shape=jax.ShapeDtypeStruct((128, 5, 8, 128), BF16),
        scratch_shapes=[
            pltpu.VMEM((1088, 512), F32),
            pltpu.VMEM((128, 128), F32),
            pltpu.VMEM((ROUTE_BLOCK, ROUTE_BLOCK + 128), BF16),
            pltpu.VMEM((4, 64, 128), F32),
            pltpu.VMEM((1088, ROUTE_STEP), BF16),
            pltpu.VMEM((512, ROUTE_STEP), BF16),
        ],
        compiler_params=pltpu.CompilerParams(vmem_limit_bytes=40 * MIB),
        name="route",
    )(owner, point, value)


def nodes_and_scales():
    nodes = [0.5 + 0.5 * math.cos(math.pi * (2 * a + 1) / (2 * QX)) for a in range(QX)]
    scales = []
    for a in range(QX):
        scale = 1.0
        for c in range(QX):
            if c != a:
                scale /= nodes[a] - nodes[c]
        scales.append(scale)
    return nodes, scales


def column(values, shape):
    row = iota(shape, 0)
    out = jnp.full(shape, values[0], F32)
    for index in range(1, len(values)):
        out = jnp.where(row == index, values[index], out)
    return out


def interpolation(position, nodes, scales):
    gap = position - nodes
    one = jnp.roll(gap, -1, axis=0)
    two = one * jnp.roll(one, -1, axis=0)
    four = two * jnp.roll(two, -2, axis=0)
    return scales * four * jnp.roll(two, -4, axis=0) * jnp.roll(one, -6, axis=0)


def turn(values, cosine, sine):
    return values * cosine + pltpu.roll(values, 64, axis=values.ndim - 1) * sine


def signs(shape):
    return jnp.where(iota(shape, len(shape) - 1) < 64, -1.0, 1.0)


def inner_kernel(
    where_ref, got_ref, mats_ref, out_ref, points, total, held, work, left0, right0, left1, right1
):
    row_high = where_ref[0]
    row_y = where_ref[1]
    chunk = LEAF_SOURCES
    chunks = 128 // chunk

    points[...] = got_ref[:, 4].astype(F32)
    total[...] = jnp.zeros_like(total)

    nodes, scales = nodes_and_scales()
    nodes = column(nodes, (8, 128))
    scales = column(scales, (8, 128))
    cells = iota((256, 128), 0).astype(F32)

    def build(turn_number, left, right):
        y = turn_number // chunks
        first = (turn_number % chunks) * chunk
        for i in range(chunk):
            span = pl.ds(i * 128, 128)
            source = first + i
            charge = got_ref[source, y].astype(F32)
            box = points[source, pl.ds(y, 1), :]
            offset = points[source, pl.ds(4 + y, 1), :]
            left[:, span] = jnp.where(cells == box, 1.0, 0.0).astype(BF16)
            coarse = jnp.floor(offset * (1.0 / 16))
            fine = offset - 16.0 * coarse
            over_x = interpolation((coarse + 0.5) * (1.0 / LAT), nodes, scales)
            over_y = interpolation((fine + 0.5) * (1.0 / LAT), nodes, scales)
            both = jnp.concatenate(
                [over_x[a : a + 1] * over_y for a in range(QX)], axis=0
            ).astype(BF16)
            for h in range(4):
                for part in range(2):
                    row = charge[part * 4 + h : part * 4 + h + 1].astype(BF16)
                    base = (h * 2 + part) * 64
                    right[base : base + 64, span] = both * row

    def product(turn_number, left, right):
        y = turn_number // chunks
        total[y] += matmul_nt(left[...], right[...])

    turns = 4 * chunks
    build(0, left0, right0)

    def pair(i, carried):
        build(2 * i + 1, left1, right1)
        product(2 * i, left0, right0)
        build(jnp.minimum(2 * i + 2, turns - 1), left0, right0)
        product(2 * i + 1, left1, right1)
        return carried

    lax.fori_loop(0, turns // 2, pair, 0)

    for y in range(4):
        for h in range(4):
            held[pl.ds(y * 4 + h, 256, stride=16), :] = total[y, :, h * 128 : (h + 1) * 128]
    for x in range(16):
        work[x] = held[x * 256 : (x + 1) * 256].astype(BF16).reshape(16, 16, 128)

    sign16 = signs((16, 128))
    member = (iota((16, 128), 0) >> 2).astype(F32)
    row_x = row_high.astype(F32) * 4.0 + member
    row_y_f = row_y.astype(F32)

    for depth in range(LEVX):
        below = LEVX - 1 - depth
        count = 2**below
        for axis in range(2):
            mats = mats_ref[2 * depth + axis]
            for high in range(2**depth):
                for low in range(count):
                    start = high << below + 1 | low
                    parent = reversed_bits(low, below)
                    ends = [start, start | 1 << below]
                    if axis == 0:
                        both = [work[e].reshape(256, 128) for e in ends]
                    else:
                        both = [work[:, e].reshape(256, 128) for e in ends]
                    made = matmul_nt(jnp.concatenate(both, axis=1), mats)
                    for t in range(2):
                        target = float(2 * high + t)
                        if axis == 0:
                            cosine, sine = unit_phase((row_x * float(count) + float(parent)) * target)
                        else:
                            cosine, sine = unit_phase(
                                jnp.full((16, 128), 1.0, F32)
                                * ((row_y_f * float(count) + float(parent)) * target)
                            )
                        piece = made[:, t * 128 : (t + 1) * 128].reshape(16, 16, 128)
                        piece = turn(piece, cosine[None], (sine * sign16)[None])
                        e = ends[t]
                        if axis == 0:
                            work[e] = piece.astype(BF16)
                        elif depth < LEVX - 1:
                            work[:, e] = piece.astype(BF16)
                        else:
                            for x in range(16):
                                held[(x * 16 + e) * 16 : (x * 16 + e + 1) * 16] = piece[x]

    key = iota((16, 8, 128), 0).astype(F32)
    sign8 = signs((16, 8, 128))
    mats = mats_ref[2 * LEVX]
    for pair_number in range(2):
        tables = []
        for t in range(2):
            parent = row_high.astype(F32) * 2.0 + float(pair_number)
            cosine, sine = unit_phase(parent * (2.0 * key + float(t)))
            tables.append((cosine[:, None], (sine * sign8)[:, None]))
        for h in range(4):
            both = [
                held[pl.ds((2 * pair_number + c) * 4 + h, 256, stride=16), :].astype(BF16)
                for c in range(2)
            ]
            made = matmul_nt(jnp.concatenate(both, axis=1), mats)
            for t in range(2):
                piece = made[:, t * 128 : (t + 1) * 128].reshape(16, 2, 8, 128)
                piece = turn(piece, *tables[t]).reshape(256, 128)
                out_ref[pair_number, t, h] = piece.astype(BF16)


def inner(where, got, mats):
    width = LEAF_SOURCES * 128
    vmem = pl.BlockSpec(memory_space=pltpu.VMEM)
    return pl.pallas_call(
        inner_kernel,
        in_specs=[pl.BlockSpec(memory_space=pltpu.SMEM), vmem, vmem],
        out_specs=vmem,
        out_shape=jax.ShapeDtypeStruct((2, 2, 4, 256, 128), BF16),
        scratch_shapes=[
            pltpu.VMEM((128, 8, 128), F32),
            pltpu.VMEM((4, 256, 512), F32),
            pltpu.VMEM((4096, 128), F32),
            pltpu.VMEM((16, 16, 16, 128), BF16),
            pltpu.VMEM((256, width), BF16),
            pltpu.VMEM((512, width), BF16),
            pltpu.VMEM((256, width), BF16),
            pltpu.VMEM((512, width), BF16),
        ],
        compiler_params=pltpu.CompilerParams(vmem_limit_bytes=48 * MIB),
        name="inner",
    )(where, got, mats)


def outer_kernel(where_ref, mine_ref, other_ref, mats_y_ref, mats_x_ref, out_ref, work):
    row_high = where_ref[0].astype(F32)
    row_y = where_ref[1]
    parent_y = (row_y >> 1).astype(F32)
    core = (row_y & 1).astype(F32)
    target = 2.0 * iota((16, 128), 0).astype(F32) + core
    cosine, sine = unit_phase(parent_y * target)
    table = (cosine[None], (sine * signs((16, 128)))[None])
    mats_y = mats_y_ref[...]
    mats_x = mats_x_ref[...]
    key = iota((16, 8, 128), 0).astype(F32)
    sign8 = signs((16, 8, 128))
    for t8 in range(2):
        tables = []
        for t in range(2):
            cosine, sine = unit_phase(row_high * (2.0 * (2.0 * key + float(t8)) + float(t)))
            tables.append((cosine[:, None], (sine * sign8)[:, None]))
        for h in range(4):
            both = []
            for c in range(2):
                pair = jnp.concatenate([mine_ref[c, t8, h], other_ref[c, t8, h]], axis=1)
                made = matmul_nt(pair, mats_y).reshape(16, 16, 128)
                both.append(turn(made, *table).reshape(256, 128).astype(BF16))
            made = matmul_nt(jnp.concatenate(both, axis=1), mats_x)
            for t in range(2):
                piece = made[:, t * 128 : (t + 1) * 128].reshape(16, 2, 8, 128)
                piece = turn(piece, *tables[t]).reshape(256, 128)
                out_ref[2 * t + t8, h] = piece.astype(BF16)


def outer(where, mine, other, mats_y, mats_x):
    vmem = pl.BlockSpec(memory_space=pltpu.VMEM)
    return pl.pallas_call(
        outer_kernel,
        in_specs=[pl.BlockSpec(memory_space=pltpu.SMEM), vmem, vmem, vmem, vmem],
        out_specs=vmem,
        out_shape=jax.ShapeDtypeStruct((4, 4, 256, 128), BF16),
        scratch_shapes=[pltpu.VMEM((8, 128), F32)],
        compiler_params=pltpu.CompilerParams(vmem_limit_bytes=40 * MIB),
        name="outer",
    )(where, mine, other, mats_y, mats_x)


def finish_kernel(got_ref, out_ref, held):
    for group in range(4):
        for h in range(4):
            held[pl.ds(group * 4 + h, 256, stride=16), :] = got_ref[group, h].astype(F32)
    for block in range(32):
        span = slice(block * 128, (block + 1) * 128)
        out_ref[:, span] = held[span].T.astype(BF16)


def finish(got):
    vmem = pl.BlockSpec(memory_space=pltpu.VMEM)
    return pl.pallas_call(
        finish_kernel,
        in_specs=[vmem],
        out_specs=vmem,
        out_shape=jax.ShapeDtypeStruct((128, 4096), BF16),
        scratch_shapes=[pltpu.VMEM((4096, 128), F32)],
        compiler_params=pltpu.CompilerParams(vmem_limit_bytes=40 * MIB),
        name="finish",
    )(got)


def block_matrices(translation):
    parts = translation.reshape(-1, 2, 2, 2, R, R)
    real = parts[:, :, :, 0]
    imag = parts[:, :, :, 1]
    top = jnp.stack([real, -imag], axis=4)
    bottom = jnp.stack([imag, real], axis=4)
    whole = jnp.stack([top, bottom], axis=2)
    whole = jnp.transpose(whole, (0, 1, 2, 4, 3, 5, 6))
    return whole.reshape(-1, 4 * R, 4 * R)


def body(src_value, src_point, src_owner, translation):
    row_x = lax.axis_index("gx")
    row_y = lax.axis_index("gy")
    where = jnp.stack([row_x >> 2, row_y]).astype(jnp.int32)
    mats = block_matrices(translation)

    send = route(src_owner.reshape(1, -1), src_point, src_value)
    got = lax.all_to_all(send, ("gx", "gy"), split_axis=0, concat_axis=0, tiled=True)
    mine = inner(where, got, mats)

    pairs = [(i, i ^ 1) for i in range(lax.axis_size("gy"))]
    other = lax.ppermute(mine, "gy", pairs)
    core = row_y & 1
    rows = lax.dynamic_slice_in_dim(mats[2 * LEVX + 1], core * 128, 128, axis=0)
    mats_y = jnp.where(
        core == 0, rows, jnp.concatenate([rows[:, 128:], rows[:, :128]], axis=1)
    )
    out = outer(where, mine, other, mats_y, mats[2 * LEVX + 2])
    groups = [[0, 1, 2, 3], [4, 5, 6, 7]]
    out = lax.all_to_all(
        out, "gx", split_axis=0, concat_axis=0, axis_index_groups=groups, tiled=True
    )
    return finish(out).reshape(128, 1, 1, 4096)


def solution(mesh):
    return jax.shard_map(
        body,
        mesh=mesh,
        in_specs=(P(None, ("gx", "gy")), P(None, ("gx", "gy")), P(("gx", "gy"), None), P()),
        out_specs=P(None, "gx", "gy", None),
        check_vma=False,
    )
```

```python
import functools
import math

import jax
import jax.numpy as jnp
from jax import lax
from jax.experimental import pallas as pl
from jax.experimental.pallas import tpu as pltpu
from jax.sharding import PartitionSpec as P

QX = 8
R = 64
LEVX = 4
LB = 16
LAT = 16
CAP = 128

F32 = jnp.float32
BF16 = jnp.bfloat16
MODULUS = 61.0
MIB = 1024 * 1024

BLOCK = 256
HALF = 2
RANK_UNROLL = 8
ROUTE_UNROLL = 4
POINT_UNROLL = 8
LEAF_UNROLL = 16


def matmul_nt(lhs, rhs):
    return lax.dot_general(lhs, rhs, (((1,), (1,)), ((), ())), preferred_element_type=F32)


def unit_phase(product):
    rest = product - MODULUS * jnp.floor(product * (1.0 / MODULUS) + 0.5)
    x = rest * (math.pi / MODULUS)
    x2 = x * x
    s = x * (1.0 + x2 * (-1 / 6 + x2 * (1 / 120 + x2 * (-1 / 5040 + x2 * (1 / 362880 + x2 * (-1 / 39916800))))))
    c = 1.0 + x2 * (-1 / 2 + x2 * (1 / 24 + x2 * (-1 / 720 + x2 * (1 / 40320 + x2 * (-1 / 3628800)))))
    return 1.0 - 2.0 * s * s, 2.0 * s * c


def cost(micros):
    return pl.CostEstimate(flops=int(micros * 1.0e9), bytes_accessed=0, transcendentals=0)


def iota(shape, dim):
    return lax.broadcasted_iota(jnp.int32, shape, dim)


def reversed_bits(value, bits):
    out = 0
    for bit in range(bits):
        out |= (value >> bit & 1) << (bits - 1 - bit)
    return out


def nibble_reversed(value):
    return (value & 1) << 3 | (value & 2) << 1 | value >> 1 & 2 | value >> 3 & 1


def one_hot(cells, row):
    return jnp.where(cells == row, jnp.ones((), BF16), jnp.zeros((), BF16))


def rank_sources(own_ref, point_ref, value_ref, rows_ref, charge_ref, tri, accs):
    width = BLOCK
    earlier = iota((width, width), 0) < iota((width, width), 1)
    tri[...] = jnp.where(earlier, 1.0, 0.0).astype(BF16)
    owners = iota((128, width), 0).astype(F32).astype(BF16)
    before_accs, whole_accs = accs[0::2], accs[1::2]

    pltpu.matmul_push_rhs(tri[...], 0, 0)
    pltpu.matmul_acc_lhs(before_accs[0], jnp.zeros((128, width), BF16), load_staged_rhs=0)
    pltpu.matmul_push_rhs(jnp.ones((width, width), BF16), 0, 1)
    pltpu.matmul_acc_lhs(whole_accs[0], jnp.zeros((128, width), BF16), load_staged_rhs=0)
    start = pltpu.matmul_pop(before_accs[0]) + pltpu.matmul_pop(whole_accs[0])

    def several(step, held):
        spans = [
            pl.ds(pl.multiple_of((step * RANK_UNROLL + u) * width, width), width)
            for u in range(RANK_UNROLL)
        ]
        hits = []
        for u, span in enumerate(spans):
            own = own_ref[0:1, span]
            hits.append(one_hot(owners, own.astype(F32).astype(BF16)))
            pltpu.matmul_acc_lhs(before_accs[u], hits[u])
            pltpu.matmul_acc_lhs(whole_accs[u], hits[u])
        for u, span in enumerate(spans):
            own = own_ref[0:1, span]
            px = point_ref[0:1, span]
            py = point_ref[1:2, span]
            rows_ref[2:3, span] = ((own >> 6) * 16 + (own & 15)).astype(F32)
            box = nibble_reversed(px >> 4) * 16 + nibble_reversed(py >> 4)
            rows_ref[3:4, span] = box.astype(F32)
            rows_ref[4:5, span] = ((px & 15) * 16 + (py & 15)).astype(F32)
            big_x = (own >> 4) * (LB * LAT) + px
            big_y = (own & 15) * (LB * LAT) + py
            cosine, sine = unit_phase(big_x.astype(F32) * big_y.astype(F32))
            real = value_ref[0:16, span].astype(F32)
            imag = value_ref[16:32, span].astype(F32)
            turned_real = cosine * real - sine * imag
            turned_imag = sine * real + cosine * imag
            parts = []
            for group in range(4):
                parts.append(turned_real[4 * group : 4 * group + 4])
                parts.append(turned_imag[4 * group : 4 * group + 4])
            charge_ref[:, span] = jnp.concatenate(parts, axis=0).astype(BF16)
        for u, span in enumerate(spans):
            before = pltpu.matmul_pop(before_accs[u]) + held
            held = held + pltpu.matmul_pop(whole_accs[u])
            rank = jnp.sum(hits[u].astype(F32) * before, axis=0, keepdims=True)
            sibling = own_ref[0:1, span] >> 4 & 3
            key = rank + (128 * (sibling & 1)).astype(F32)
            rows_ref[0:1, span] = jnp.where(sibling < 2, key, -1.0)
            rows_ref[1:2, span] = jnp.where(sibling < 2, -1.0, key)
        return held

    lax.fori_loop(0, own_ref.shape[1] // width // RANK_UNROLL, several, start)


def place_charges(rows_ref, charge_ref, hold, accs):
    blocks = charge_ref.shape[1] // BLOCK
    cells = iota((256, BLOCK), 0).astype(F32).astype(BF16)
    none = jnp.zeros((), BF16)

    def one(step, carried):
        for u in range(ROUTE_UNROLL):
            span = pl.ds(pl.multiple_of((step * ROUTE_UNROLL + u) * BLOCK, BLOCK), BLOCK)
            low = jnp.broadcast_to(rows_ref[2:3, span].astype(BF16), (32, BLOCK))
            charge = charge_ref[:, span]
            slots = [one_hot(cells, rows_ref[side : side + 1, span].astype(BF16)) for side in range(2)]
            for m in range(2):
                parts = [jnp.where(low == float(m * 16 + n), charge, none) for n in range(16)]
                parts = jnp.concatenate(parts, axis=0)
                for side in range(2):
                    pltpu.matmul_push_rhs(slots[side], side, m, transpose=True)
                    pltpu.matmul_acc_lhs(accs[2 * side + m], parts, load_staged_rhs=side)
        return carried

    lax.fori_loop(0, blocks // ROUTE_UNROLL, one, 0)
    for side in range(2):
        for m in range(2):
            hold[side, m, 0:512] = pltpu.matmul_pop(accs[2 * side + m])


def place_points(rows_ref, hold, accs):
    blocks = rows_ref.shape[1] // BLOCK
    cells = iota((256, BLOCK), 0).astype(F32).astype(BF16)
    lows = iota((32, BLOCK), 0).astype(F32).astype(BF16)
    none = jnp.zeros((), BF16)

    def one(step, carried):
        for u in range(POINT_UNROLL):
            span = pl.ds(pl.multiple_of((step * POINT_UNROLL + u) * BLOCK, BLOCK), BLOCK)
            mine = lows == rows_ref[2:3, span].astype(BF16)
            places = [
                jnp.where(mine, rows_ref[3 + kind : 4 + kind, span].astype(BF16), none)
                for kind in range(2)
            ]
            places = jnp.concatenate(places, axis=0)
            for side in range(2):
                slots = one_hot(cells, rows_ref[side : side + 1, span].astype(BF16))
                pltpu.matmul_push_rhs(slots, u % 2, side, transpose=True)
                pltpu.matmul_acc_lhs(accs[side], places, load_staged_rhs=u % 2)
        return carried

    lax.fori_loop(0, blocks // POINT_UNROLL, one, 0)
    for side in range(2):
        hold[side, 0, 512:576] = pltpu.matmul_pop(accs[side])


def route_kernel(own_ref, point_ref, value_ref, send_ref, rows_ref, charge_ref, tri, hold):
    pl.run_scoped(
        lambda *accs: rank_sources(own_ref, point_ref, value_ref, rows_ref, charge_ref, tri, accs),
        *[pltpu.ACC(number % 2)((128, 256), F32) for number in range(2 * RANK_UNROLL)],
    )
    pl.run_scoped(
        lambda *accs: place_points(rows_ref, hold, accs),
        *[pltpu.ACC(number % 2)((64, 256), F32) for number in range(2)],
    )
    pl.run_scoped(
        lambda *accs: place_charges(rows_ref, charge_ref, hold, accs),
        *[pltpu.ACC(number % 2)((512, 256), F32) for number in range(4)],
    )
    for number in range(32):
        first = number // 16 * 64 + number % 16
        row = number % 16 * 32
        for group in range(4):
            for y in range(4):
                tile = hold[
                    y // 2,
                    number // 16,
                    row + group * 8 : row + group * 8 + 8,
                    y % 2 * 128 : y % 2 * 128 + 128,
                ]
                send_ref[first + group * 16, y] = tile.astype(BF16)
        tile = [
            hold[y // 2, 0, pl.ds(512 + 32 * kind + number, 1), y % 2 * 128 : y % 2 * 128 + 128]
            for kind in range(2)
            for y in range(4)
        ]
        tile = jnp.concatenate(tile, axis=0).astype(BF16)
        for group in range(4):
            send_ref[first + group * 16, 4] = tile


def route(owner, point, value):
    sources = owner.shape[1]
    vmem = pl.BlockSpec(memory_space=pltpu.VMEM)
    return pl.pallas_call(
        route_kernel,
        in_specs=[vmem] * 3,
        out_specs=vmem,
        out_shape=jax.ShapeDtypeStruct((128, 5, 8, 128), BF16),
        scratch_shapes=[
            pltpu.VMEM((8, sources), F32),
            pltpu.VMEM((32, sources), BF16),
            pltpu.VMEM((BLOCK, BLOCK), BF16),
            pltpu.VMEM((2, 2, 576, 256), F32),
        ],
        compiler_params=pltpu.CompilerParams(vmem_limit_bytes=40 * MIB),
        cost_estimate=cost(15),
        name="route",
    )(owner, point, value)


def nodes_and_scales():
    nodes = [0.5 + 0.5 * math.cos(math.pi * (2 * a + 1) / (2 * QX)) for a in range(QX)]
    scales = []
    for a in range(QX):
        scale = 1.0
        for c in range(QX):
            if c != a:
                scale /= nodes[a] - nodes[c]
        scales.append(scale)
    return nodes, scales


def column(values, shape):
    row = iota(shape, 0)
    out = jnp.full(shape, values[0], F32)
    for index in range(1, len(values)):
        out = jnp.where(row == index, values[index], out)
    return out


def interpolation(position, nodes, scales):
    gap = position - nodes
    one = pltpu.roll(gap, 7, axis=0)
    two = one * pltpu.roll(one, 7, axis=0)
    four = two * pltpu.roll(two, 6, axis=0)
    return scales * four * pltpu.roll(two, 4, axis=0) * pltpu.roll(one, 2, axis=0)


def turn(values, cosine, sine):
    return values * cosine + pltpu.roll(values, 64, axis=values.ndim - 1) * sine


def signs(shape):
    return jnp.where(iota(shape, len(shape) - 1) < 64, -1.0, 1.0)


def level_matrix(mats_ref, level):
    return jnp.concatenate(
        [
            jnp.concatenate([mats_ref[level, t, 0], mats_ref[level, t, 1]], axis=1)
            for t in range(2)
        ],
        axis=0,
    )


def leaves_kernel(got_ref, out_ref, points):
    points[...] = got_ref[:, 4].astype(F32)
    nodes, scales = nodes_and_scales()
    nodes = column(nodes, (8, 128))
    scales = column(scales, (8, 128))
    cells = iota((256, 128), 0).astype(F32).astype(BF16)

    def operands(source, y):
        charge = got_ref[source, y].astype(F32)
        box = points[source, y : y + 1, :]
        offset = points[source, 4 + y : 5 + y, :]
        coarse = jnp.floor(offset * (1.0 / LAT))
        fine = offset - LAT * coarse
        over_x = interpolation((coarse + 0.5) * (1.0 / LAT), nodes, scales)
        over_y = interpolation((fine + 0.5) * (1.0 / LAT), nodes, scales)
        both = jnp.concatenate([over_x[a : a + 1] * over_y for a in range(QX)], axis=0)
        both = both.astype(BF16)
        rows = []
        for h in range(4):
            for part in range(2):
                at = part * 4 + h
                rows.append(both * charge[at : at + 1].astype(BF16))
        return one_hot(cells, box.astype(BF16)), jnp.concatenate(rows, axis=0)

    def run(*accs):
        for y in range(4):

            def one(step, carried):
                for u in range(LEAF_UNROLL):
                    for m in range(2):
                        source = (step * LEAF_UNROLL + u) * 4 + m * 2
                        boxes0, spread0 = operands(source, y)
                        boxes1, spread1 = operands(source + 1, y)
                        boxes = jnp.concatenate([boxes0, boxes1], axis=1)
                        spread = jnp.concatenate([spread0, spread1], axis=1)
                        pltpu.matmul_push_rhs(boxes, u % 2, m, transpose=True)
                        pltpu.matmul_acc_lhs(accs[m], spread, load_staged_rhs=u % 2)
                return carried

            lax.fori_loop(0, 32 // LEAF_UNROLL, one, 0)
            total = pltpu.matmul_pop(accs[0]) + pltpu.matmul_pop(accs[1])
            for h in range(4):
                out_ref[h // 2, y, h % 2] = total[h * 128 : (h + 1) * 128].T.astype(BF16)

    pl.run_scoped(run, pltpu.ACC(0)((512, 256), F32), pltpu.ACC(1)((512, 256), F32))


def leaves(got):
    vmem = pl.BlockSpec(memory_space=pltpu.VMEM)
    return pl.pallas_call(
        leaves_kernel,
        in_specs=[vmem],
        out_specs=vmem,
        out_shape=jax.ShapeDtypeStruct((2, 4, HALF, 256, 128), BF16),
        scratch_shapes=[pltpu.VMEM((128, 8, 128), F32)],
        compiler_params=pltpu.CompilerParams(vmem_limit_bytes=40 * MIB),
        cost_estimate=cost(19),
        name="leaves",
    )(got)


def inner_kernel(where_ref, leaf_ref, mats_ref, after_ref, out_ref, work):
    del after_ref
    for y in range(4):
        for h in range(HALF):
            work[pl.ds(y * HALF + h, 256, stride=8), :] = leaf_ref[0, y, h].astype(F32)
    pl.run_scoped(
        lambda *accs: inner_levels(where_ref, mats_ref, out_ref, work, accs),
        *[pltpu.ACC(number % 2)((256, 256), F32) for number in range(4)],
    )


def four_products(accs, lefts, right):
    for number, left in enumerate(lefts):
        pltpu.matmul_push_rhs(right, number // 2, number % 2, transpose=True)
        pltpu.matmul_acc_lhs(accs[number], left, load_staged_rhs=number // 2)


def inner_levels(where_ref, mats_ref, out_ref, work, accs):
    row_high = where_ref[0].astype(F32)
    row_y = where_ref[1].astype(F32)
    sign8 = signs((8, 128))
    row_x = row_high * 4.0 + (iota((8, 128), 0) // HALF).astype(F32)

    def box_rows(x, y):
        return pl.ds((x * 16 + y) * 8, 8)

    def line(axis, at):
        if axis == 0:
            return work[pl.ds(at * 128, 128), :].astype(BF16)
        return jnp.concatenate([work[box_rows(x, at), :] for x in range(16)], axis=0).astype(BF16)

    for depth in range(LEVX):
        below = LEVX - 1 - depth
        count = 2**below
        starts = [(high, low) for high in range(2**depth) for low in range(count)]
        for axis in range(2):
            lefts = []
            for number in range(4):
                first = [high << below + 1 | low for high, low in starts[2 * number : 2 * number + 2]]
                lefts.append(
                    jnp.concatenate(
                        [
                            jnp.concatenate([line(axis, s) for s in first], axis=0),
                            jnp.concatenate([line(axis, s | 1 << below) for s in first], axis=0),
                        ],
                        axis=1,
                    )
                )
            four_products(accs, lefts, level_matrix(mats_ref, 2 * depth + axis))
            for number in range(4):
                made = pltpu.matmul_pop(accs[number])
                for place in range(2):
                    high, low = starts[2 * number + place]
                    parent = float(reversed_bits(low, below))
                    for t in range(2):
                        target = float(2 * high + t)
                        if axis == 0:
                            angle = (row_x * float(count) + parent) * target
                        else:
                            angle = jnp.full((8, 128), (row_y * float(count) + parent) * target)
                        cosine, sine = unit_phase(angle)
                        piece = made[place * 128 : (place + 1) * 128, t * 128 : (t + 1) * 128]
                        piece = turn(piece.reshape(16, 8, 128), cosine[None], (sine * sign8)[None])
                        end = high << below + 1 | low | t << below
                        if axis == 0:
                            work[pl.ds(end * 128, 128), :] = piece.reshape(128, 128)
                        else:
                            for x in range(16):
                                work[box_rows(x, end), :] = piece[x]

    key = iota((16, 8, 128), 0).astype(F32)
    sign = signs((16, 8, 128))
    lefts = []
    for pair in range(2):
        for h in range(HALF):
            both = [
                work[pl.ds((2 * pair + c) * HALF + h, 256, stride=8), :].astype(BF16)
                for c in range(2)
            ]
            lefts.append(jnp.concatenate(both, axis=1))
    four_products(accs, lefts, level_matrix(mats_ref, 2 * LEVX))
    for pair in range(2):
        tables = []
        for t in range(2):
            cosine, sine = unit_phase((row_high * 2.0 + float(pair)) * (2.0 * key + float(t)))
            tables.append((cosine[:, None], (sine * sign)[:, None]))
        for h in range(HALF):
            made = pltpu.matmul_pop(accs[pair * HALF + h])
            for t in range(2):
                piece = made[:, t * 128 : (t + 1) * 128].reshape(16, 2, 8, 128)
                piece = turn(piece, *tables[t]).reshape(256, 128)
                out_ref[pair, t, h] = piece.astype(BF16)


def inner(half, where, leaf, mats, after):
    vmem = pl.BlockSpec(memory_space=pltpu.VMEM)
    chosen = pl.BlockSpec((1, 4, HALF, 256, 128), lambda i: (half, 0, 0, 0, 0))
    return pl.pallas_call(
        inner_kernel,
        grid=(1,),
        in_specs=[
            pl.BlockSpec(memory_space=pltpu.SMEM),
            chosen,
            vmem,
            pl.BlockSpec(memory_space=pl.ANY),
        ],
        out_specs=vmem,
        out_shape=jax.ShapeDtypeStruct((2, 2, HALF, 256, 128), BF16),
        scratch_shapes=[pltpu.VMEM((2048, 128), F32)],
        compiler_params=pltpu.CompilerParams(vmem_limit_bytes=40 * MIB),
        cost_estimate=cost(4),
        name="inner",
    )(where, leaf, mats, after)


def outer_kernel(where_ref, mine_ref, other_ref, mats_ref, *refs):
    outs, held = refs[:4], refs[4]
    row_high = where_ref[0].astype(F32)
    row_y = where_ref[1]
    own = where_ref[2]
    core = row_y & 1
    target = 2.0 * iota((16, 128), 0).astype(F32) + core.astype(F32)
    cosine, sine = unit_phase((row_y >> 1).astype(F32) * target)
    table = (cosine[None], (sine * signs((16, 128)))[None])
    mats_y = jnp.concatenate([mats_ref[0, core, core], mats_ref[0, core, 1 - core]], axis=1)
    mats_x = level_matrix(mats_ref, 1)
    key = iota((16, 8, 128), 0).astype(F32)
    sign = signs((16, 8, 128))
    for t8 in range(2):
        tables = []
        for t in range(2):
            cosine, sine = unit_phase(row_high * (2.0 * (2.0 * key + float(t8)) + float(t)))
            tables.append((cosine[:, None], (sine * sign)[:, None]))
        for h in range(HALF):
            both = []
            for c in range(2):
                pair = jnp.concatenate([mine_ref[c, t8, h], other_ref[c, t8, h]], axis=1)
                made = matmul_nt(pair, mats_y).reshape(16, 16, 128)
                both.append(turn(made, *table).reshape(256, 128).astype(BF16))
            made = matmul_nt(jnp.concatenate(both, axis=1), mats_x)
            for t in range(2):
                piece = made[:, t * 128 : (t + 1) * 128].reshape(16, 2, 8, 128)
                piece = turn(piece, *tables[t]).reshape(256, 128)
                held[2 * t + t8, h] = piece.astype(BF16)
    for shift in range(4):
        outs[shift][...] = held[(own + shift) & 3]


def outer(where, mine, other, mats):
    vmem = pl.BlockSpec(memory_space=pltpu.VMEM)
    return pl.pallas_call(
        outer_kernel,
        in_specs=[pl.BlockSpec(memory_space=pltpu.SMEM), vmem, vmem, vmem],
        out_specs=[vmem] * 4,
        out_shape=[jax.ShapeDtypeStruct((HALF, 256, 128), BF16)] * 4,
        scratch_shapes=[pltpu.VMEM((4, HALF, 256, 128), BF16)],
        compiler_params=pltpu.CompilerParams(vmem_limit_bytes=40 * MIB),
        cost_estimate=cost(3),
        name="outer",
    )(where, mine, other, mats)


def finish_kernel(where_ref, *refs):
    got, out_ref, taken, held = refs[:8], refs[8], refs[9], refs[10]
    own = where_ref[2]
    for half in range(2):
        for shift in range(4):
            taken[half, shift] = got[half * 4 + shift][...]
    for half in range(2):
        for group in range(4):
            for h in range(HALF):
                row = group * 4 + half * HALF + h
                piece = taken[half, (own - group) & 3, h]
                held[pl.ds(row, 256, stride=16), :] = piece.astype(F32)
    for block in range(32):
        span = slice(block * 128, (block + 1) * 128)
        out_ref[:, span] = held[span].T.astype(BF16)


def finish(where, got):
    vmem = pl.BlockSpec(memory_space=pltpu.VMEM)
    return pl.pallas_call(
        finish_kernel,
        in_specs=[pl.BlockSpec(memory_space=pltpu.SMEM)] + [vmem] * 8,
        out_specs=vmem,
        out_shape=jax.ShapeDtypeStruct((128, 4096), BF16),
        scratch_shapes=[
            pltpu.VMEM((2, 4, HALF, 256, 128), BF16),
            pltpu.VMEM((4096, 128), F32),
        ],
        compiler_params=pltpu.CompilerParams(vmem_limit_bytes=40 * MIB),
        cost_estimate=cost(3),
        name="finish",
    )(where, *got)


def block_matrices(translation):
    parts = translation.reshape(-1, 2, 2, 2, R, R)
    real = parts[:, :, :, 0]
    imag = parts[:, :, :, 1]
    top = jnp.concatenate([real, -imag], axis=-1)
    bottom = jnp.concatenate([imag, real], axis=-1)
    return jnp.concatenate([top, bottom], axis=-2)


def body(src_value, src_point, src_owner, translation):
    row_x = lax.axis_index("gx")
    row_y = lax.axis_index("gy")
    where = jnp.stack([row_x >> 2, row_y, row_x & 3]).astype(jnp.int32)

    send = route(src_owner.reshape(1, -1), src_point, src_value)
    got = lax.all_to_all(send, ("gx", "gy"), split_axis=0, concat_axis=0, tiled=True)
    mats = block_matrices(translation)
    inner_mats = mats[: 2 * LEVX + 1]
    outer_mats = mats[2 * LEVX + 1 :]
    leaf = leaves(got)
    cores = [(i, i ^ 1) for i in range(lax.axis_size("gy"))]
    after = where
    got = []
    for half in range(2):
        mine = inner(half, where, leaf, inner_mats, after)
        after = mine
        other = lax.ppermute(mine, "gy", cores)
        outs = outer(where, mine, other, outer_mats)
        got.append(outs[0])
        for shift in range(1, 4):
            pairs = [(i, i // 4 * 4 + (i + shift) % 4) for i in range(lax.axis_size("gx"))]
            got.append(lax.ppermute(outs[shift], "gx", pairs))
    return finish(where, got).reshape(128, 1, 1, 4096)


def solution(mesh):
    return jax.shard_map(
        body,
        mesh=mesh,
        in_specs=(P(None, ("gx", "gy")), P(None, ("gx", "gy")), P(("gx", "gy"), None), P()),
        out_specs=P(None, "gx", "gy", None),
        check_vma=False,
    )
```

```python
import functools
import math

import jax
import jax.numpy as jnp
from jax import lax
from jax.experimental import pallas as pl
from jax.experimental.pallas import tpu as pltpu
from jax.sharding import PartitionSpec as P

QX = 8
R = 64
LEVX = 4
LB = 16
LAT = 16
CAP = 128

F32 = jnp.float32
BF16 = jnp.bfloat16
MODULUS = 61.0
MIB = 1024 * 1024

BLOCK = 256
HALF = 2
RANK_UNROLL = 8
ROUTE_UNROLL = 8
LEAF_UNROLL = 32


def matmul_nt(lhs, rhs):
    return lax.dot_general(lhs, rhs, (((1,), (1,)), ((), ())), preferred_element_type=F32)


def unit_phase(product):
    rest = product - MODULUS * jnp.floor(product * (1.0 / MODULUS) + 0.5)
    x = rest * (math.pi / MODULUS)
    x2 = x * x
    s = x * (1.0 + x2 * (-1 / 6 + x2 * (1 / 120 + x2 * (-1 / 5040 + x2 * (1 / 362880 + x2 * (-1 / 39916800))))))
    c = 1.0 + x2 * (-1 / 2 + x2 * (1 / 24 + x2 * (-1 / 720 + x2 * (1 / 40320 + x2 * (-1 / 3628800)))))
    return 1.0 - 2.0 * s * s, 2.0 * s * c


def cost(micros):
    return pl.CostEstimate(flops=int(micros * 1.0e9), bytes_accessed=0, transcendentals=0)


def iota(shape, dim):
    return lax.broadcasted_iota(jnp.int32, shape, dim)


def reversed_bits(value, bits):
    out = 0
    for bit in range(bits):
        out |= (value >> bit & 1) << (bits - 1 - bit)
    return out


def nibble_reversed(value):
    return (value & 1) << 3 | (value & 2) << 1 | value >> 1 & 2 | value >> 3 & 1


def one_hot(cells, row):
    return jnp.where(cells == row, jnp.ones((), BF16), jnp.zeros((), BF16))


def rank_sources(own_ref, point_ref, value_ref, rows_ref, charge_ref, tri, accs):
    width = BLOCK
    owners = iota((128, width), 0).astype(F32).astype(BF16)
    before_accs, whole_accs = accs[0::2], accs[1::2]

    pltpu.matmul_push_rhs(tri[...], 0, 0)
    pltpu.matmul_acc_lhs(before_accs[0], jnp.zeros((128, width), BF16), load_staged_rhs=0)
    pltpu.matmul_push_rhs(jnp.ones((width, width), BF16), 0, 1)
    pltpu.matmul_acc_lhs(whole_accs[0], jnp.zeros((128, width), BF16), load_staged_rhs=0)
    start = pltpu.matmul_pop(before_accs[0]) + pltpu.matmul_pop(whole_accs[0])

    def several(step, held):
        spans = [
            pl.ds(pl.multiple_of((step * RANK_UNROLL + u) * width, width), width)
            for u in range(RANK_UNROLL)
        ]
        hits = []
        for u, span in enumerate(spans):
            own = own_ref[0:1, span]
            hits.append(one_hot(owners, own.astype(F32).astype(BF16)))
            pltpu.matmul_acc_lhs(before_accs[u], hits[u])
            pltpu.matmul_acc_lhs(whole_accs[u], hits[u])
        for u, span in enumerate(spans):
            own = own_ref[0:1, span]
            px = point_ref[0:1, span]
            py = point_ref[1:2, span]
            rows_ref[2:3, span] = ((own >> 6) * 16 + (own & 15)).astype(F32)
            box = nibble_reversed(px >> 4) * 16 + nibble_reversed(py >> 4)
            rows_ref[3:4, span] = box.astype(F32)
            rows_ref[4:5, span] = ((px & 15) * 16 + (py & 15)).astype(F32)
            big_x = (own >> 4) * (LB * LAT) + px
            big_y = (own & 15) * (LB * LAT) + py
            cosine, sine = unit_phase(big_x.astype(F32) * big_y.astype(F32))
            real = value_ref[0:16, span].astype(F32)
            imag = value_ref[16:32, span].astype(F32)
            turned_real = cosine * real - sine * imag
            turned_imag = sine * real + cosine * imag
            parts = []
            for group in range(4):
                parts.append(turned_real[4 * group : 4 * group + 4])
                parts.append(turned_imag[4 * group : 4 * group + 4])
            charge_ref[:, span] = jnp.concatenate(parts, axis=0).astype(BF16)
        for u, span in enumerate(spans):
            before = pltpu.matmul_pop(before_accs[u]) + held
            held = held + pltpu.matmul_pop(whole_accs[u])
            rank = jnp.sum(hits[u].astype(F32) * before, axis=0, keepdims=True)
            sibling = own_ref[0:1, span] >> 4 & 3
            key = rank + (128 * (sibling & 1)).astype(F32)
            rows_ref[0:1, span] = jnp.where(sibling < 2, key, -1.0)
            rows_ref[1:2, span] = jnp.where(sibling < 2, -1.0, key)
        return held

    lax.fori_loop(0, own_ref.shape[1] // width // RANK_UNROLL, several, start)


def place_sources(high, rows_ref, charge_ref, hold, accs):
    blocks = charge_ref.shape[1] // BLOCK
    cells = iota((256, BLOCK), 0).astype(F32).astype(BF16)
    lows = (iota((16, BLOCK), 0) + 16 * high).astype(F32).astype(BF16)
    none = jnp.zeros((), BF16)

    def one(step, carried):
        for u in range(ROUTE_UNROLL):
            span = pl.ds(pl.multiple_of((step * ROUTE_UNROLL + u) * BLOCK, BLOCK), BLOCK)
            row = rows_ref[2:3, span].astype(BF16)
            low = jnp.broadcast_to(row, (32, BLOCK))
            charge = charge_ref[:, span]
            parts = [jnp.where(low == float(high * 16 + n), charge, none) for n in range(16)]
            mine = lows == row
            for kind in range(2):
                parts.append(jnp.where(mine, rows_ref[3 + kind : 4 + kind, span].astype(BF16), none))
            parts = jnp.concatenate(parts, axis=0)
            for side in range(2):
                slots = one_hot(cells, rows_ref[side : side + 1, span].astype(BF16))
                pltpu.matmul_push_rhs(slots, u % 2, side, transpose=True)
                pltpu.matmul_acc_lhs(accs[side], parts, load_staged_rhs=u % 2)
        return carried

    lax.fori_loop(0, blocks // ROUTE_UNROLL, one, 0)
    for side in range(2):
        hold[high, side] = pltpu.matmul_pop(accs[side])


def route_kernel(
    own_hbm, point_hbm, value_hbm, send_ref, own, point, value, rows, charge, tri, hold, sems
):
    copies = [
        pltpu.make_async_copy(source, target, sems.at[number])
        for number, (source, target) in enumerate(
            ((own_hbm, own), (point_hbm, point), (value_hbm, value))
        )
    ]
    for copy in copies:
        copy.start()
    earlier = iota((BLOCK, BLOCK), 0) < iota((BLOCK, BLOCK), 1)
    tri[...] = jnp.where(earlier, 1.0, 0.0).astype(BF16)
    for copy in copies:
        copy.wait()
    pl.run_scoped(
        lambda *accs: rank_sources(own, point, value, rows, charge, tri, accs),
        *[pltpu.ACC(number % 2)((128, 256), F32) for number in range(2 * RANK_UNROLL)],
    )
    for high in range(2):
        pl.run_scoped(
            lambda *accs, high=high: place_sources(high, rows, charge, hold, accs),
            *[pltpu.ACC(number)((544, 256), F32) for number in range(2)],
        )
    for number in range(32):
        high, low = number // 16, number % 16
        first = high * 64 + low
        for group in range(4):
            at = low * 32 + group * 8
            for y in range(4):
                tile = hold[high, y // 2, at : at + 8, y % 2 * 128 : y % 2 * 128 + 128]
                send_ref[first + group * 16, y] = tile.astype(BF16)
        tile = [
            hold[high, y // 2, pl.ds(512 + 16 * kind + low, 1), y % 2 * 128 : y % 2 * 128 + 128]
            for kind in range(2)
            for y in range(4)
        ]
        tile = jnp.concatenate(tile, axis=0).astype(BF16)
        for group in range(4):
            send_ref[first + group * 16, 4] = tile


def route(owner, point, value):
    sources = owner.shape[1]
    vmem = pl.BlockSpec(memory_space=pltpu.VMEM)
    return pl.pallas_call(
        route_kernel,
        in_specs=[pl.BlockSpec(memory_space=pltpu.HBM)] * 3,
        out_specs=vmem,
        out_shape=jax.ShapeDtypeStruct((128, 5, 8, 128), BF16),
        scratch_shapes=[
            pltpu.VMEM((1, sources), jnp.int32),
            pltpu.VMEM((2, sources), jnp.int32),
            pltpu.VMEM((32, sources), BF16),
            pltpu.VMEM((8, sources), F32),
            pltpu.VMEM((32, sources), BF16),
            pltpu.VMEM((BLOCK, BLOCK), BF16),
            pltpu.VMEM((2, 2, 544, 256), F32),
            pltpu.SemaphoreType.DMA((3,)),
        ],
        compiler_params=pltpu.CompilerParams(vmem_limit_bytes=40 * MIB),
        cost_estimate=cost(15),
        name="route",
    )(owner, point, value)


def level_starts(depth):
    return [(high, low) for high in range(2**depth) for low in range(2 ** (LEVX - 1 - depth))]


def phases_kernel(
    where_ref, level_c, level_s, eight_c, eight_s, nine_c, nine_s, ten_c, ten_s
):
    row_high = where_ref[0].astype(F32)
    row_y = where_ref[1]
    sign = signs((8, 128))
    row_x = row_high * 4.0 + (iota((8, 128), 0) // HALF).astype(F32)
    flat_y = jnp.full((8, 128), row_y.astype(F32))
    for depth in range(LEVX):
        below = LEVX - 1 - depth
        for axis in range(2):
            row = (row_x, flat_y)[axis]
            for place, (high, low) in enumerate(level_starts(depth)):
                parent = row * float(2**below) + float(reversed_bits(low, below))
                for t in range(2):
                    cosine, sine = unit_phase(parent * float(2 * high + t))
                    level_c[2 * depth + axis, 2 * place + t] = cosine
                    level_s[2 * depth + axis, 2 * place + t] = sine * sign

    key = iota((16, 8, 128), 0).astype(F32)
    sign = signs((16, 8, 128))
    for pair in range(2):
        for t in range(2):
            cosine, sine = unit_phase((row_high * 2.0 + float(pair)) * (2.0 * key + float(t)))
            eight_c[pair, t] = cosine
            eight_s[pair, t] = sine * sign
            cosine, sine = unit_phase(row_high * (2.0 * (2.0 * key + float(pair)) + float(t)))
            ten_c[pair, t] = cosine
            ten_s[pair, t] = sine * sign

    core = (row_y & 1).astype(F32)
    target = 2.0 * iota((16, 128), 0).astype(F32) + core
    cosine, sine = unit_phase((row_y >> 1).astype(F32) * target)
    nine_c[...] = cosine
    nine_s[...] = sine * signs((16, 128))


def phases(where):
    shapes = [(8, 16, 8, 128), (2, 2, 16, 8, 128), (16, 128), (2, 2, 16, 8, 128)]
    return pl.pallas_call(
        phases_kernel,
        in_specs=[pl.BlockSpec(memory_space=pltpu.SMEM)],
        out_specs=[pl.BlockSpec(memory_space=pltpu.VMEM)] * 8,
        out_shape=[jax.ShapeDtypeStruct(shape, F32) for shape in shapes for _ in range(2)],
        compiler_params=pltpu.CompilerParams(vmem_limit_bytes=40 * MIB),
        cost_estimate=cost(2),
        name="phases",
    )(where)


def nodes_and_scales():
    nodes = [0.5 + 0.5 * math.cos(math.pi * (2 * a + 1) / (2 * QX)) for a in range(QX)]
    scales = []
    for a in range(QX):
        scale = 1.0
        for c in range(QX):
            if c != a:
                scale /= nodes[a] - nodes[c]
        scales.append(scale)
    return nodes, scales


def column(values, shape):
    row = iota(shape, 0)
    out = jnp.full(shape, values[0], F32)
    for index in range(1, len(values)):
        out = jnp.where(row == index, values[index], out)
    return out


def interpolation(position, nodes, scales):
    gap = position - nodes
    one = pltpu.roll(gap, 7, axis=0)
    two = one * pltpu.roll(one, 7, axis=0)
    four = two * pltpu.roll(two, 6, axis=0)
    return scales * four * pltpu.roll(two, 4, axis=0) * pltpu.roll(one, 2, axis=0)


def turn(values, cosine, sine):
    return values * cosine + pltpu.roll(values, 64, axis=values.ndim - 1) * sine


def signs(shape):
    return jnp.where(iota(shape, len(shape) - 1) < 64, -1.0, 1.0)


def level_matrix(mats_ref, level):
    return jnp.concatenate(
        [
            jnp.concatenate([mats_ref[level, t, 0], mats_ref[level, t, 1]], axis=1)
            for t in range(2)
        ],
        axis=0,
    )


def leaves_kernel(got_ref, out_ref, points):
    points[...] = got_ref[:, 4].astype(F32)
    nodes, scales = nodes_and_scales()
    nodes = column(nodes, (8, 128))
    scales = column(scales, (8, 128))
    cells = iota((256, 128), 0).astype(F32).astype(BF16)

    def operands(source, y):
        charge = got_ref[source, y].astype(F32)
        box = points[source, y : y + 1, :]
        offset = points[source, 4 + y : 5 + y, :]
        coarse = jnp.floor(offset * (1.0 / LAT))
        fine = offset - LAT * coarse
        over_x = interpolation((coarse + 0.5) * (1.0 / LAT), nodes, scales)
        over_y = interpolation((fine + 0.5) * (1.0 / LAT), nodes, scales)
        both = jnp.concatenate([over_x[a : a + 1] * over_y for a in range(QX)], axis=0)
        both = both.astype(BF16)
        rows = []
        for h in range(4):
            for part in range(2):
                at = part * 4 + h
                rows.append(both * charge[at : at + 1].astype(BF16))
        return one_hot(cells, box.astype(BF16)), jnp.concatenate(rows, axis=0)

    def run(*accs):
        for y in range(4):

            def one(step, carried):
                for u in range(LEAF_UNROLL):
                    for m in range(2):
                        source = (step * LEAF_UNROLL + u) * 4 + m * 2
                        boxes0, spread0 = operands(source, y)
                        boxes1, spread1 = operands(source + 1, y)
                        boxes = jnp.concatenate([boxes0, boxes1], axis=1)
                        spread = jnp.concatenate([spread0, spread1], axis=1)
                        pltpu.matmul_push_rhs(boxes, u % 2, m, transpose=True)
                        pltpu.matmul_acc_lhs(accs[m], spread, load_staged_rhs=u % 2)
                return carried

            lax.fori_loop(0, 32 // LEAF_UNROLL, one, 0)
            total = pltpu.matmul_pop(accs[0]) + pltpu.matmul_pop(accs[1])
            for h in range(4):
                out_ref[h // 2, y, h % 2] = total[h * 128 : (h + 1) * 128].T.astype(BF16)

    pl.run_scoped(run, pltpu.ACC(0)((512, 256), F32), pltpu.ACC(1)((512, 256), F32))


def leaves(got):
    vmem = pl.BlockSpec(memory_space=pltpu.VMEM)
    return pl.pallas_call(
        leaves_kernel,
        in_specs=[vmem],
        out_specs=vmem,
        out_shape=jax.ShapeDtypeStruct((2, 4, HALF, 256, 128), BF16),
        scratch_shapes=[pltpu.VMEM((128, 8, 128), F32)],
        compiler_params=pltpu.CompilerParams(vmem_limit_bytes=40 * MIB),
        cost_estimate=cost(19),
        name="leaves",
    )(got)


def inner_kernel(leaf_ref, mats_ref, level_c, level_s, eight_c, eight_s, out0, out1, work0, work1):
    works = (work0, work1)
    for half in range(2):
        for y in range(4):
            for h in range(HALF):
                piece = leaf_ref[half, y, h].astype(F32)
                works[half][pl.ds(y * HALF + h, 256, stride=8), :] = piece
    pl.run_scoped(
        lambda *accs: inner_levels(
            mats_ref, level_c, level_s, eight_c, eight_s, (out0, out1), works, accs
        ),
        *[pltpu.ACC(number % 2)((256, 256), F32) for number in range(8)],
    )


def four_products(accs, lefts, right, load):
    for number, left in enumerate(lefts):
        if load and number < 2:
            pltpu.matmul_push_rhs(right, 0, number, transpose=True)
            pltpu.matmul_acc_lhs(accs[number], left, load_staged_rhs=0)
        else:
            pltpu.matmul_acc_lhs(accs[number], left)


def box_rows(x, y):
    return pl.ds((x * 16 + y) * 8, 8)


def line(work, axis, at):
    if axis == 0:
        return work[pl.ds(at * 128, 128), :].astype(BF16)
    return jnp.concatenate([work[box_rows(x, at), :] for x in range(16)], axis=0).astype(BF16)


def inner_levels(mats_ref, level_c, level_s, eight_c, eight_s, outs, works, accs):
    for depth in range(LEVX):
        below = LEVX - 1 - depth
        starts = level_starts(depth)
        for axis in range(2):
            level = 2 * depth + axis
            right = level_matrix(mats_ref, level)
            for half, work in enumerate(works):
                lefts = []
                for number in range(4):
                    pair = starts[2 * number : 2 * number + 2]
                    first = [high << below + 1 | low for high, low in pair]
                    ends = [[line(work, axis, s | t << below) for s in first] for t in range(2)]
                    ends = [jnp.concatenate(end, axis=0) for end in ends]
                    lefts.append(jnp.concatenate(ends, axis=1))
                four_products(accs[4 * half : 4 * half + 4], lefts, right, half == 0)
            for half, work in enumerate(works):
                for number in range(4):
                    made = pltpu.matmul_pop(accs[4 * half + number])
                    for place in range(2):
                        high, low = starts[2 * number + place]
                        for t in range(2):
                            cosine = level_c[level, 4 * number + 2 * place + t]
                            sine = level_s[level, 4 * number + 2 * place + t]
                            piece = made[place * 128 : (place + 1) * 128, t * 128 : (t + 1) * 128]
                            piece = turn(piece.reshape(16, 8, 128), cosine[None], sine[None])
                            end = high << below + 1 | low | t << below
                            if axis == 0:
                                work[pl.ds(end * 128, 128), :] = piece.reshape(128, 128)
                            else:
                                for x in range(16):
                                    work[box_rows(x, end), :] = piece[x]

    right = level_matrix(mats_ref, 2 * LEVX)
    for half, work in enumerate(works):
        lefts = []
        for pair in range(2):
            for h in range(HALF):
                both = [
                    work[pl.ds((2 * pair + c) * HALF + h, 256, stride=8), :].astype(BF16)
                    for c in range(2)
                ]
                lefts.append(jnp.concatenate(both, axis=1))
        four_products(accs[4 * half : 4 * half + 4], lefts, right, half == 0)
    for half, out_ref in enumerate(outs):
        for pair in range(2):
            tables = [(eight_c[pair, t][:, None], eight_s[pair, t][:, None]) for t in range(2)]
            for h in range(HALF):
                made = pltpu.matmul_pop(accs[4 * half + pair * HALF + h])
                for t in range(2):
                    piece = made[:, t * 128 : (t + 1) * 128].reshape(16, 2, 8, 128)
                    piece = turn(piece, *tables[t]).reshape(256, 128)
                    out_ref[pair, t, h] = piece.astype(BF16)


def inner(leaf, mats, tables):
    vmem = pl.BlockSpec(memory_space=pltpu.VMEM)
    return pl.pallas_call(
        inner_kernel,
        in_specs=[vmem] * 6,
        out_specs=[vmem] * 2,
        out_shape=[jax.ShapeDtypeStruct((2, 2, HALF, 256, 128), BF16)] * 2,
        scratch_shapes=[pltpu.VMEM((2048, 128), F32)] * 2,
        compiler_params=pltpu.CompilerParams(vmem_limit_bytes=40 * MIB),
        cost_estimate=cost(6),
        name="inner",
    )(leaf, mats, *tables[:4])


def outer_kernel(
    where_ref, mine_ref, other_ref, mats_ref, nine_c, nine_s, ten_c, ten_s, after_ref, *refs
):
    del after_ref
    outs, held = refs[:4], refs[4]
    row_y = where_ref[1]
    own = where_ref[2]
    core = row_y & 1
    table = (nine_c[...][None], nine_s[...][None])
    mats_y = jnp.concatenate([mats_ref[0, core, core], mats_ref[0, core, 1 - core]], axis=1)
    mats_x = level_matrix(mats_ref, 1)
    for t8 in range(2):
        tables = [(ten_c[t8, t][:, None], ten_s[t8, t][:, None]) for t in range(2)]
        for h in range(HALF):
            both = []
            for c in range(2):
                pair = jnp.concatenate([mine_ref[c, t8, h], other_ref[c, t8, h]], axis=1)
                made = matmul_nt(pair, mats_y).reshape(16, 16, 128)
                both.append(turn(made, *table).reshape(256, 128).astype(BF16))
            made = matmul_nt(jnp.concatenate(both, axis=1), mats_x)
            for t in range(2):
                piece = made[:, t * 128 : (t + 1) * 128].reshape(16, 2, 8, 128)
                piece = turn(piece, *tables[t]).reshape(256, 128)
                held[2 * t + t8, h] = piece.astype(BF16)
    for shift in range(4):
        outs[shift][...] = held[(own + shift) & 3]


def outer(where, mine, other, mats, tables, after):
    vmem = pl.BlockSpec(memory_space=pltpu.VMEM)
    return pl.pallas_call(
        outer_kernel,
        in_specs=[pl.BlockSpec(memory_space=pltpu.SMEM)]
        + [vmem] * 7
        + [pl.BlockSpec(memory_space=pl.ANY)],
        out_specs=[vmem] * 4,
        out_shape=[jax.ShapeDtypeStruct((HALF, 256, 128), BF16)] * 4,
        scratch_shapes=[pltpu.VMEM((4, HALF, 256, 128), BF16)],
        compiler_params=pltpu.CompilerParams(vmem_limit_bytes=40 * MIB),
        cost_estimate=cost(3),
        name="outer",
    )(where, mine, other, mats, *tables[4:], after)


def finish_kernel(where_ref, *refs):
    got, out_ref, held = refs[:8], refs[8], refs[9]
    own = where_ref[2]
    for half in range(2):
        for shift in range(4):
            group = (own - shift) & 3
            for h in range(HALF):
                row = group * 4 + (half * HALF + h)
                held[pl.ds(row, 256, stride=16), :] = got[half * 4 + shift][h].astype(F32)
    for block in range(32):
        span = slice(block * 128, (block + 1) * 128)
        out_ref[:, span] = held[span].astype(BF16).T


def finish(where, got):
    vmem = pl.BlockSpec(memory_space=pltpu.VMEM)
    return pl.pallas_call(
        finish_kernel,
        in_specs=[pl.BlockSpec(memory_space=pltpu.SMEM)] + [vmem] * 8,
        out_specs=vmem,
        out_shape=jax.ShapeDtypeStruct((128, 4096), BF16),
        scratch_shapes=[pltpu.VMEM((4096, 128), F32)],
        compiler_params=pltpu.CompilerParams(vmem_limit_bytes=40 * MIB),
        cost_estimate=cost(3),
        name="finish",
    )(where, *got)


def block_matrices(translation):
    parts = translation.reshape(-1, 2, 2, 2, R, R)
    real = parts[:, :, :, 0]
    imag = parts[:, :, :, 1]
    top = jnp.concatenate([real, -imag], axis=-1)
    bottom = jnp.concatenate([imag, real], axis=-1)
    return jnp.concatenate([top, bottom], axis=-2)


def body(src_value, src_point, src_owner, translation):
    row_x = lax.axis_index("gx")
    row_y = lax.axis_index("gy")
    where = jnp.stack([row_x >> 2, row_y, row_x & 3]).astype(jnp.int32)

    send = route(src_owner.reshape(1, -1), src_point, src_value)
    got = lax.all_to_all(send, ("gx", "gy"), split_axis=0, concat_axis=0, tiled=True)
    mats = block_matrices(translation)
    inner_mats = mats[: 2 * LEVX + 1]
    outer_mats = mats[2 * LEVX + 1 :]
    leaf = leaves(got)
    cores = [(i, i ^ 1) for i in range(lax.axis_size("gy"))]
    tables = phases(where)
    last = where
    got = []
    for mine in inner(leaf, inner_mats, tables):
        other = lax.ppermute(mine, "gy", cores)
        outs = outer(where, mine, other, outer_mats, tables, last)
        last = outs[0]
        got.append(outs[0])
        for shift in range(1, 4):
            pairs = [(i, i // 4 * 4 + (i + shift) % 4) for i in range(lax.axis_size("gx"))]
            got.append(lax.ppermute(outs[shift], "gx", pairs))
    return finish(where, got).reshape(128, 1, 1, 4096)


def solution(mesh):
    return jax.shard_map(
        body,
        mesh=mesh,
        in_specs=(P(None, ("gx", "gy")), P(None, ("gx", "gy")), P(("gx", "gy"), None), P()),
        out_specs=P(None, "gx", "gy", None),
        check_vma=False,
    )
```

```python
import functools
import math

import jax
import jax.numpy as jnp
from jax import lax
from jax.experimental import pallas as pl
from jax.experimental.pallas import tpu as pltpu
from jax.sharding import PartitionSpec as P

QX = 8
R = 64
LEVX = 4
LB = 16
LAT = 16
CAP = 128

F32 = jnp.float32
BF16 = jnp.bfloat16
MODULUS = 61.0
MIB = 1024 * 1024

BLOCK = 256
HALF = 2
RANK_UNROLL = 8
ROUTE_UNROLL = 8


def matmul_nt(lhs, rhs):
    return lax.dot_general(lhs, rhs, (((1,), (1,)), ((), ())), preferred_element_type=F32)


def unit_phase(product):
    rest = product - MODULUS * jnp.floor(product * (1.0 / MODULUS) + 0.5)
    x = rest * (math.pi / MODULUS)
    x2 = x * x
    s = x * (1.0 + x2 * (-1 / 6 + x2 * (1 / 120 + x2 * (-1 / 5040 + x2 * (1 / 362880 + x2 * (-1 / 39916800))))))
    c = 1.0 + x2 * (-1 / 2 + x2 * (1 / 24 + x2 * (-1 / 720 + x2 * (1 / 40320 + x2 * (-1 / 3628800)))))
    return 1.0 - 2.0 * s * s, 2.0 * s * c


def cost(micros):
    return pl.CostEstimate(flops=int(micros * 1.0e9), bytes_accessed=0, transcendentals=0)


def iota(shape, dim):
    return lax.broadcasted_iota(jnp.int32, shape, dim)


def reversed_bits(value, bits):
    out = 0
    for bit in range(bits):
        out |= (value >> bit & 1) << (bits - 1 - bit)
    return out


def nibble_reversed(value):
    return (value & 1) << 3 | (value & 2) << 1 | value >> 1 & 2 | value >> 3 & 1


def one_hot(cells, row):
    return jnp.where(cells == row, jnp.ones((), BF16), jnp.zeros((), BF16))


def rank_sources(own_ref, point_ref, value_ref, rows_ref, charge_ref, tri, accs):
    width = BLOCK
    owners = iota((128, width), 0).astype(F32).astype(BF16)
    before_accs, whole_accs = accs[0::2], accs[1::2]

    pltpu.matmul_push_rhs(tri[...], 0, 0)
    pltpu.matmul_acc_lhs(before_accs[0], jnp.zeros((128, width), BF16), load_staged_rhs=0)
    pltpu.matmul_push_rhs(jnp.ones((width, width), BF16), 0, 1)
    pltpu.matmul_acc_lhs(whole_accs[0], jnp.zeros((128, width), BF16), load_staged_rhs=0)
    start = pltpu.matmul_pop(before_accs[0]) + pltpu.matmul_pop(whole_accs[0])

    def several(step, held):
        spans = [
            pl.ds(pl.multiple_of((step * RANK_UNROLL + u) * width, width), width)
            for u in range(RANK_UNROLL)
        ]
        hits = []
        for u, span in enumerate(spans):
            own = own_ref[0:1, span]
            hits.append(one_hot(owners, own.astype(F32).astype(BF16)))
            pltpu.matmul_acc_lhs(before_accs[u], hits[u])
            pltpu.matmul_acc_lhs(whole_accs[u], hits[u])
        for u, span in enumerate(spans):
            own = own_ref[0:1, span]
            px = point_ref[0:1, span]
            py = point_ref[1:2, span]
            rows_ref[2:3, span] = ((own >> 6) * 16 + (own & 15)).astype(F32)
            box = nibble_reversed(px >> 4) * 16 + nibble_reversed(py >> 4)
            rows_ref[3:4, span] = box.astype(F32)
            rows_ref[4:5, span] = ((px & 15) * 16 + (py & 15)).astype(F32)
            big_x = (own >> 4) * (LB * LAT) + px
            big_y = (own & 15) * (LB * LAT) + py
            cosine, sine = unit_phase(big_x.astype(F32) * big_y.astype(F32))
            real = value_ref[0:16, span].astype(F32)
            imag = value_ref[16:32, span].astype(F32)
            turned_real = cosine * real - sine * imag
            turned_imag = sine * real + cosine * imag
            parts = []
            for group in range(4):
                parts.append(turned_real[4 * group : 4 * group + 4])
                parts.append(turned_imag[4 * group : 4 * group + 4])
            charge_ref[:, span] = jnp.concatenate(parts, axis=0).astype(BF16)
        for u, span in enumerate(spans):
            before = pltpu.matmul_pop(before_accs[u]) + held
            held = held + pltpu.matmul_pop(whole_accs[u])
            rank = jnp.sum(hits[u].astype(F32) * before, axis=0, keepdims=True)
            sibling = own_ref[0:1, span] >> 4 & 3
            key = rank + (128 * (sibling & 1)).astype(F32)
            rows_ref[0:1, span] = jnp.where(sibling < 2, key, -1.0)
            rows_ref[1:2, span] = jnp.where(sibling < 2, -1.0, key)
        return held

    lax.fori_loop(0, own_ref.shape[1] // width // RANK_UNROLL, several, start)


def place_sources(high, rows_ref, charge_ref, hold, accs):
    blocks = charge_ref.shape[1] // BLOCK
    cells = iota((256, BLOCK), 0).astype(F32).astype(BF16)
    lows = (iota((16, BLOCK), 0) + 16 * high).astype(F32).astype(BF16)
    none = jnp.zeros((), BF16)

    def one(step, carried):
        for u in range(ROUTE_UNROLL):
            span = pl.ds(pl.multiple_of((step * ROUTE_UNROLL + u) * BLOCK, BLOCK), BLOCK)
            row = rows_ref[2:3, span].astype(BF16)
            low = jnp.broadcast_to(row, (32, BLOCK))
            charge = charge_ref[:, span]
            parts = [jnp.where(low == float(high * 16 + n), charge, none) for n in range(16)]
            mine = lows == row
            for kind in range(2):
                parts.append(jnp.where(mine, rows_ref[3 + kind : 4 + kind, span].astype(BF16), none))
            parts = jnp.concatenate(parts, axis=0)
            for side in range(2):
                slots = one_hot(cells, rows_ref[side : side + 1, span].astype(BF16))
                pltpu.matmul_push_rhs(slots, u % 2, side, transpose=True)
                pltpu.matmul_acc_lhs(accs[side], parts, load_staged_rhs=u % 2)
        return carried

    lax.fori_loop(0, blocks // ROUTE_UNROLL, one, 0)
    for side in range(2):
        hold[high, side] = pltpu.matmul_pop(accs[side])


def route_kernel(
    own_hbm, point_hbm, value_hbm, send_ref, own, point, value, rows, charge, tri, hold, sems
):
    copies = [
        pltpu.make_async_copy(source, target, sems.at[number])
        for number, (source, target) in enumerate(
            ((own_hbm, own), (point_hbm, point), (value_hbm, value))
        )
    ]
    for copy in copies:
        copy.start()
    earlier = iota((BLOCK, BLOCK), 0) < iota((BLOCK, BLOCK), 1)
    tri[...] = jnp.where(earlier, 1.0, 0.0).astype(BF16)
    for copy in copies:
        copy.wait()
    pl.run_scoped(
        lambda *accs: rank_sources(own, point, value, rows, charge, tri, accs),
        *[pltpu.ACC(number % 2)((128, 256), F32) for number in range(2 * RANK_UNROLL)],
    )
    for high in range(2):
        pl.run_scoped(
            lambda *accs, high=high: place_sources(high, rows, charge, hold, accs),
            *[pltpu.ACC(number)((544, 256), F32) for number in range(2)],
        )
    for number in range(32):
        high, low = number // 16, number % 16
        first = high * 64 + low
        for group in range(4):
            at = low * 32 + group * 8
            for y in range(4):
                tile = hold[high, y // 2, at : at + 8, y % 2 * 128 : y % 2 * 128 + 128]
                send_ref[first + group * 16, y] = tile.astype(BF16)
        tile = [
            hold[high, y // 2, pl.ds(512 + 16 * kind + low, 1), y % 2 * 128 : y % 2 * 128 + 128]
            for kind in range(2)
            for y in range(4)
        ]
        tile = jnp.concatenate(tile, axis=0).astype(BF16)
        for group in range(4):
            send_ref[first + group * 16, 4] = tile


def route(owner, point, value):
    sources = owner.shape[1]
    vmem = pl.BlockSpec(memory_space=pltpu.VMEM)
    return pl.pallas_call(
        route_kernel,
        in_specs=[pl.BlockSpec(memory_space=pltpu.HBM)] * 3,
        out_specs=vmem,
        out_shape=jax.ShapeDtypeStruct((128, 5, 8, 128), BF16),
        scratch_shapes=[
            pltpu.VMEM((1, sources), jnp.int32),
            pltpu.VMEM((2, sources), jnp.int32),
            pltpu.VMEM((32, sources), BF16),
            pltpu.VMEM((8, sources), F32),
            pltpu.VMEM((32, sources), BF16),
            pltpu.VMEM((BLOCK, BLOCK), BF16),
            pltpu.VMEM((2, 2, 544, 256), F32),
            pltpu.SemaphoreType.DMA((3,)),
        ],
        compiler_params=pltpu.CompilerParams(vmem_limit_bytes=60 * MIB),
        cost_estimate=cost(15),
        name="route",
    )(owner, point, value)


def level_starts(depth):
    return [(high, low) for high in range(2**depth) for low in range(2 ** (LEVX - 1 - depth))]


def phases_kernel(
    where_ref, level_c, level_s, eight_c, eight_s, nine_c, nine_s, ten_c, ten_s
):
    row_high = where_ref[0].astype(F32)
    row_y = where_ref[1]
    sign = signs((8, 128))
    row_x = row_high * 4.0 + (iota((8, 128), 0) // HALF).astype(F32)
    flat_y = jnp.full((8, 128), row_y.astype(F32))
    for depth in range(LEVX):
        below = LEVX - 1 - depth
        for axis in range(2):
            row = (row_x, flat_y)[axis]
            for place, (high, low) in enumerate(level_starts(depth)):
                parent = row * float(2**below) + float(reversed_bits(low, below))
                for t in range(2):
                    cosine, sine = unit_phase(parent * float(2 * high + t))
                    level_c[2 * depth + axis, 2 * place + t] = cosine
                    level_s[2 * depth + axis, 2 * place + t] = sine * sign

    key = iota((16, 8, 128), 0).astype(F32)
    sign = signs((16, 8, 128))
    for pair in range(2):
        for t in range(2):
            cosine, sine = unit_phase((row_high * 2.0 + float(pair)) * (2.0 * key + float(t)))
            eight_c[pair, t] = cosine
            eight_s[pair, t] = sine * sign
            cosine, sine = unit_phase(row_high * (2.0 * (2.0 * key + float(pair)) + float(t)))
            ten_c[pair, t] = cosine
            ten_s[pair, t] = sine * sign

    core = (row_y & 1).astype(F32)
    target = 2.0 * iota((16, 128), 0).astype(F32) + core
    cosine, sine = unit_phase((row_y >> 1).astype(F32) * target)
    nine_c[...] = cosine
    nine_s[...] = sine * signs((16, 128))


def phases(where):
    shapes = [(8, 16, 8, 128), (2, 2, 16, 8, 128), (16, 128), (2, 2, 16, 8, 128)]
    return pl.pallas_call(
        phases_kernel,
        in_specs=[pl.BlockSpec(memory_space=pltpu.SMEM)],
        out_specs=[pl.BlockSpec(memory_space=pltpu.VMEM)] * 8,
        out_shape=[jax.ShapeDtypeStruct(shape, F32) for shape in shapes for _ in range(2)],
        compiler_params=pltpu.CompilerParams(vmem_limit_bytes=40 * MIB),
        cost_estimate=cost(2),
        name="phases",
    )(where)


def nodes_and_scales():
    nodes = [0.5 + 0.5 * math.cos(math.pi * (2 * a + 1) / (2 * QX)) for a in range(QX)]
    scales = []
    for a in range(QX):
        scale = 1.0
        for c in range(QX):
            if c != a:
                scale /= nodes[a] - nodes[c]
        scales.append(scale)
    return nodes, scales


def column(values, shape):
    row = iota(shape, 0)
    out = jnp.full(shape, values[0], F32)
    for index in range(1, len(values)):
        out = jnp.where(row == index, values[index], out)
    return out


def interpolation(position, nodes, scales):
    gap = position - nodes
    one = pltpu.roll(gap, 7, axis=0)
    two = one * pltpu.roll(one, 7, axis=0)
    four = two * pltpu.roll(two, 6, axis=0)
    return scales * four * pltpu.roll(two, 4, axis=0) * pltpu.roll(one, 2, axis=0)


def turn(values, cosine, sine):
    return values * cosine + pltpu.roll(values, 64, axis=values.ndim - 1) * sine


def signs(shape):
    return jnp.where(iota(shape, len(shape) - 1) < 64, -1.0, 1.0)


def level_matrix(mats_ref, level):
    return jnp.concatenate(
        [
            jnp.concatenate([mats_ref[level, t, 0], mats_ref[level, t, 1]], axis=1)
            for t in range(2)
        ],
        axis=0,
    )


def leaves_kernel(got_ref, out_ref, points):
    points[...] = got_ref[:, 4].astype(F32)
    nodes, scales = nodes_and_scales()
    nodes = column(nodes, (8, 128))
    scales = column(scales, (8, 128))
    cells = iota((256, 128), 0).astype(F32).astype(BF16)

    def operands(source, y):
        charge = got_ref[source, y].astype(F32)
        box = points[source, y : y + 1, :]
        offset = points[source, 4 + y : 5 + y, :]
        coarse = jnp.floor(offset * (1.0 / LAT))
        fine = offset - LAT * coarse
        over_x = interpolation((coarse + 0.5) * (1.0 / LAT), nodes, scales)
        over_y = interpolation((fine + 0.5) * (1.0 / LAT), nodes, scales)
        both = jnp.concatenate([over_x[a : a + 1] * over_y for a in range(QX)], axis=0)
        both = both.astype(BF16)
        rows = []
        for h in range(4):
            for part in range(2):
                at = part * 4 + h
                rows.append(both * charge[at : at + 1].astype(BF16))
        return one_hot(cells, box.astype(BF16)), jnp.concatenate(rows, axis=0)

    def run(*accs):
        for y in range(4):

            for step in range(32):
                for m in range(2):
                    source = step * 4 + m * 2
                    boxes0, spread0 = operands(source, y)
                    boxes1, spread1 = operands(source + 1, y)
                    boxes = jnp.concatenate([boxes0, boxes1], axis=1)
                    spread = jnp.concatenate([spread0, spread1], axis=1)
                    pltpu.matmul_push_rhs(boxes, step % 2, m, transpose=True)
                    pltpu.matmul_acc_lhs(accs[m], spread, load_staged_rhs=step % 2)
            total = pltpu.matmul_pop(accs[0]) + pltpu.matmul_pop(accs[1])
            for h in range(4):
                rows = pl.ds(y * HALF + h % HALF, 256, stride=8)
                out_ref[h // HALF, rows, :] = total[h * 128 : (h + 1) * 128].T

    pl.run_scoped(run, pltpu.ACC(0)((512, 256), F32), pltpu.ACC(1)((512, 256), F32))


def leaves(got):
    vmem = pl.BlockSpec(memory_space=pltpu.VMEM)
    return pl.pallas_call(
        leaves_kernel,
        in_specs=[vmem],
        out_specs=vmem,
        out_shape=jax.ShapeDtypeStruct((2, 2048, 128), F32),
        scratch_shapes=[pltpu.VMEM((128, 8, 128), F32)],
        compiler_params=pltpu.CompilerParams(vmem_limit_bytes=40 * MIB),
        cost_estimate=cost(19),
        name="leaves",
    )(got)


def inner_kernel(leaf_ref, mats_ref, level_c, level_s, eight_c, eight_s, out0, out1, work0, work1):
    tables = (level_c, level_s, eight_c, eight_s)

    def run(*accs):
        halves = [
            (leaf_ref.at[0], work0, out0, accs[:4]),
            (leaf_ref.at[1], work1, out1, accs[4:]),
        ]
        for number, (leaf, _, _, own) in enumerate(halves):
            level_products(0, mats_ref, leaf, own, number == 0)
        for level in range(2 * LEVX):
            for number, (_, work, _, own) in enumerate(halves):
                level_turns(level, tables, work, own)
                if level < 2 * LEVX - 1:
                    level_products(level + 1, mats_ref, work, own, number == 0)
                else:
                    eighth_products(mats_ref, work, own, number == 0)
        for _, _, out, own in halves:
            eighth_turns(tables, out, own)

    pl.run_scoped(run, *[pltpu.ACC(number % 2)((256, 256), F32) for number in range(8)])


def four_products(accs, lefts, level, mats_ref, load):
    for number, left in enumerate(lefts):
        if load and number < 2:
            right = level_matrix(mats_ref, level)
            pltpu.matmul_push_rhs(right, level % 2, number, transpose=True)
            pltpu.matmul_acc_lhs(accs[number], left, load_staged_rhs=level % 2)
        else:
            pltpu.matmul_acc_lhs(accs[number], left)


def box_rows(x, y):
    return pl.ds((x * 16 + y) * 8, 8)


def line(work, level, at):
    if level % 2 == 0:
        return work[pl.ds(at * 128, 128), :].astype(BF16)
    return jnp.concatenate([work[box_rows(x, at), :] for x in range(16)], axis=0).astype(BF16)


def level_products(level, mats_ref, work, accs, load):
    below = LEVX - 1 - level // 2
    starts = [high << below + 1 | low for high, low in level_starts(level // 2)]
    lefts = []
    for number in range(4):
        first = starts[2 * number : 2 * number + 2]
        ends = [[line(work, level, s | t << below) for s in first] for t in range(2)]
        ends = [jnp.concatenate(end, axis=0) for end in ends]
        lefts.append(jnp.concatenate(ends, axis=1))
    four_products(accs, lefts, level, mats_ref, load)


def level_turns(level, tables, work, accs):
    level_c, level_s = tables[:2]
    below = LEVX - 1 - level // 2
    starts = [high << below + 1 | low for high, low in level_starts(level // 2)]
    for number in range(4):
        made = pltpu.matmul_pop(accs[number])
        for place in range(2):
            at = 2 * number + place
            for t in range(2):
                piece = made[place * 128 : (place + 1) * 128, t * 128 : (t + 1) * 128]
                cosine, sine = level_c[level, 2 * at + t], level_s[level, 2 * at + t]
                piece = turn(piece.reshape(16, 8, 128), cosine[None], sine[None])
                end = starts[at] | t << below
                if level % 2 == 0:
                    work[pl.ds(end * 128, 128), :] = piece.reshape(128, 128)
                else:
                    for x in range(16):
                        work[box_rows(x, end), :] = piece[x]


def eighth_products(mats_ref, work, accs, load):
    lefts = []
    for pair in range(2):
        for h in range(HALF):
            both = [
                work[pl.ds((2 * pair + c) * HALF + h, 256, stride=8), :].astype(BF16)
                for c in range(2)
            ]
            lefts.append(jnp.concatenate(both, axis=1))
    four_products(accs, lefts, 2 * LEVX, mats_ref, load)


def eighth_turns(tables, out_ref, accs):
    eight_c, eight_s = tables[2:]
    for pair in range(2):
        for h in range(HALF):
            made = pltpu.matmul_pop(accs[pair * HALF + h])
            for t in range(2):
                piece = made[:, t * 128 : (t + 1) * 128].reshape(16, 2, 8, 128)
                piece = turn(piece, eight_c[pair, t][:, None], eight_s[pair, t][:, None])
                out_ref[pair, t, h] = piece.reshape(256, 128).astype(BF16)


def inner(leaf, mats, tables):
    vmem = pl.BlockSpec(memory_space=pltpu.VMEM)
    return pl.pallas_call(
        inner_kernel,
        in_specs=[vmem] * 6,
        out_specs=[vmem] * 2,
        out_shape=[jax.ShapeDtypeStruct((2, 2, HALF, 256, 128), BF16)] * 2,
        scratch_shapes=[pltpu.VMEM((2048, 128), F32)] * 2,
        compiler_params=pltpu.CompilerParams(vmem_limit_bytes=40 * MIB),
        cost_estimate=cost(5),
        name="inner",
    )(leaf, mats, *tables[:4])


def outer_kernel(
    where_ref, mine_ref, other_ref, mats_ref, nine_c, nine_s, ten_c, ten_s, after_ref, *refs
):
    del after_ref
    outs, held = refs[:4], refs[4]
    row_y = where_ref[1]
    own = where_ref[2]
    core = row_y & 1
    table = (nine_c[...][None], nine_s[...][None])
    mats_y = jnp.concatenate([mats_ref[0, core, core], mats_ref[0, core, 1 - core]], axis=1)
    mats_x = level_matrix(mats_ref, 1)
    for t8 in range(2):
        tables = [(ten_c[t8, t][:, None], ten_s[t8, t][:, None]) for t in range(2)]
        for h in range(HALF):
            both = []
            for c in range(2):
                pair = jnp.concatenate([mine_ref[c, t8, h], other_ref[c, t8, h]], axis=1)
                made = matmul_nt(pair, mats_y).reshape(16, 16, 128)
                both.append(turn(made, *table).reshape(256, 128).astype(BF16))
            made = matmul_nt(jnp.concatenate(both, axis=1), mats_x)
            for t in range(2):
                piece = made[:, t * 128 : (t + 1) * 128].reshape(16, 2, 8, 128)
                piece = turn(piece, *tables[t]).reshape(256, 128)
                held[2 * t + t8, h] = piece.astype(BF16)
    for shift in range(4):
        outs[shift][...] = held[(own + shift) & 3]


def outer(where, mine, other, mats, tables, after):
    vmem = pl.BlockSpec(memory_space=pltpu.VMEM)
    return pl.pallas_call(
        outer_kernel,
        in_specs=[pl.BlockSpec(memory_space=pltpu.SMEM)]
        + [vmem] * 7
        + [pl.BlockSpec(memory_space=pl.ANY)],
        out_specs=[vmem] * 4,
        out_shape=[jax.ShapeDtypeStruct((HALF, 256, 128), BF16)] * 4,
        scratch_shapes=[pltpu.VMEM((4, HALF, 256, 128), BF16)],
        compiler_params=pltpu.CompilerParams(vmem_limit_bytes=40 * MIB),
        cost_estimate=cost(3),
        name="outer",
    )(where, mine, other, mats, *tables[4:], after)


def finish_kernel(where_ref, *refs):
    got, out_ref, held = refs[:8], refs[8], refs[9]
    own = where_ref[2]
    for half in range(2):
        for shift in range(4):
            group = (own - shift) & 3
            for h in range(HALF):
                row = group * 4 + (half * HALF + h)
                held[pl.ds(row, 256, stride=16), :] = got[half * 4 + shift][h].astype(F32)
    for block in range(32):
        span = slice(block * 128, (block + 1) * 128)
        out_ref[:, span] = held[span].astype(BF16).T


def finish(where, got):
    vmem = pl.BlockSpec(memory_space=pltpu.VMEM)
    return pl.pallas_call(
        finish_kernel,
        in_specs=[pl.BlockSpec(memory_space=pltpu.SMEM)] + [vmem] * 8,
        out_specs=vmem,
        out_shape=jax.ShapeDtypeStruct((128, 4096), BF16),
        scratch_shapes=[pltpu.VMEM((4096, 128), F32)],
        compiler_params=pltpu.CompilerParams(vmem_limit_bytes=40 * MIB),
        cost_estimate=cost(3),
        name="finish",
    )(where, *got)


def block_matrices(translation):
    parts = translation.reshape(-1, 2, 2, 2, R, R)
    real = parts[:, :, :, 0]
    imag = parts[:, :, :, 1]
    top = jnp.concatenate([real, -imag], axis=-1)
    bottom = jnp.concatenate([imag, real], axis=-1)
    return jnp.concatenate([top, bottom], axis=-2)


def body(src_value, src_point, src_owner, translation):
    row_x = lax.axis_index("gx")
    row_y = lax.axis_index("gy")
    where = jnp.stack([row_x >> 2, row_y, row_x & 3]).astype(jnp.int32)

    send = route(src_owner.reshape(1, -1), src_point, src_value)
    got = lax.all_to_all(send, ("gx", "gy"), split_axis=0, concat_axis=0, tiled=True)
    mats = block_matrices(translation)
    inner_mats = mats[: 2 * LEVX + 1]
    outer_mats = mats[2 * LEVX + 1 :]
    leaf = leaves(got)
    cores = [(i, i ^ 1) for i in range(lax.axis_size("gy"))]
    tables = phases(where)
    last = where
    got = []
    for mine in inner(leaf, inner_mats, tables):
        other = lax.ppermute(mine, "gy", cores)
        outs = outer(where, mine, other, outer_mats, tables, last)
        last = outs[0]
        got.append(outs[0])
        for shift in range(1, 4):
            pairs = [(i, i // 4 * 4 + (i + shift) % 4) for i in range(lax.axis_size("gx"))]
            got.append(lax.ppermute(outs[shift], "gx", pairs))
    return finish(where, got).reshape(128, 1, 1, 4096)


def solution(mesh):
    return jax.shard_map(
        body,
        mesh=mesh,
        in_specs=(P(None, ("gx", "gy")), P(None, ("gx", "gy")), P(("gx", "gy"), None), P()),
        out_specs=P(None, "gx", "gy", None),
        check_vma=False,
    )
```

```python
import functools
import math

import jax
import jax.numpy as jnp
from jax import lax
from jax.experimental import pallas as pl
from jax.experimental.pallas import tpu as pltpu
from jax.sharding import PartitionSpec as P

QX = 8
R = 64
LEVX = 4
LB = 16
LAT = 16
CAP = 128

F32 = jnp.float32
BF16 = jnp.bfloat16
MODULUS = 61.0
MIB = 1024 * 1024

BLOCK = 256
HALF = 2
RANK_UNROLL = 8
ROUTE_UNROLL = 8


def matmul_nt(lhs, rhs):
    return lax.dot_general(lhs, rhs, (((1,), (1,)), ((), ())), preferred_element_type=F32)


def unit_phase(product):
    rest = product - MODULUS * jnp.floor(product * (1.0 / MODULUS) + 0.5)
    x = rest * (math.pi / MODULUS)
    x2 = x * x
    s = x * (1.0 + x2 * (-1 / 6 + x2 * (1 / 120 + x2 * (-1 / 5040 + x2 * (1 / 362880 + x2 * (-1 / 39916800))))))
    c = 1.0 + x2 * (-1 / 2 + x2 * (1 / 24 + x2 * (-1 / 720 + x2 * (1 / 40320 + x2 * (-1 / 3628800)))))
    return 1.0 - 2.0 * s * s, 2.0 * s * c


def cost(micros):
    return pl.CostEstimate(flops=int(micros * 1.0e9), bytes_accessed=0, transcendentals=0)


def iota(shape, dim):
    return lax.broadcasted_iota(jnp.int32, shape, dim)


def reversed_bits(value, bits):
    out = 0
    for bit in range(bits):
        out |= (value >> bit & 1) << (bits - 1 - bit)
    return out


def nibble_reversed(value):
    return (value & 1) << 3 | (value & 2) << 1 | value >> 1 & 2 | value >> 3 & 1


def one_hot(cells, row):
    return jnp.where(cells == row, jnp.ones((), BF16), jnp.zeros((), BF16))


def rank_sources(own_ref, point_ref, value_ref, rows_ref, charge_ref, tri, accs):
    width = BLOCK
    owners = iota((128, width), 0).astype(F32).astype(BF16)
    before_accs, whole_accs = accs[0::2], accs[1::2]

    pltpu.matmul_push_rhs(tri[...], 0, 0)
    pltpu.matmul_acc_lhs(before_accs[0], jnp.zeros((128, width), BF16), load_staged_rhs=0)
    pltpu.matmul_push_rhs(jnp.ones((width, width), BF16), 0, 1)
    pltpu.matmul_acc_lhs(whole_accs[0], jnp.zeros((128, width), BF16), load_staged_rhs=0)
    start = pltpu.matmul_pop(before_accs[0]) + pltpu.matmul_pop(whole_accs[0])

    def several(step, held):
        spans = [
            pl.ds(pl.multiple_of((step * RANK_UNROLL + u) * width, width), width)
            for u in range(RANK_UNROLL)
        ]
        hits = []
        for u, span in enumerate(spans):
            own = own_ref[0:1, span]
            hits.append(one_hot(owners, own.astype(F32).astype(BF16)))
            pltpu.matmul_acc_lhs(before_accs[u], hits[u])
            pltpu.matmul_acc_lhs(whole_accs[u], hits[u])
        for u, span in enumerate(spans):
            own = own_ref[0:1, span]
            px = point_ref[0:1, span]
            py = point_ref[1:2, span]
            rows_ref[2:3, span] = ((own >> 6) * 16 + (own & 15)).astype(F32)
            box = nibble_reversed(px >> 4) * 16 + nibble_reversed(py >> 4)
            rows_ref[3:4, span] = box.astype(F32)
            rows_ref[4:5, span] = ((px & 15) * 16 + (py & 15)).astype(F32)
            big_x = (own >> 4) * (LB * LAT) + px
            big_y = (own & 15) * (LB * LAT) + py
            cosine, sine = unit_phase(big_x.astype(F32) * big_y.astype(F32))
            real = value_ref[0:16, span].astype(F32)
            imag = value_ref[16:32, span].astype(F32)
            turned_real = cosine * real - sine * imag
            turned_imag = sine * real + cosine * imag
            parts = []
            for group in range(4):
                parts.append(turned_real[4 * group : 4 * group + 4])
                parts.append(turned_imag[4 * group : 4 * group + 4])
            charge_ref[:, span] = jnp.concatenate(parts, axis=0).astype(BF16)
        for u, span in enumerate(spans):
            before = pltpu.matmul_pop(before_accs[u]) + held
            held = held + pltpu.matmul_pop(whole_accs[u])
            rank = jnp.sum(hits[u].astype(F32) * before, axis=0, keepdims=True)
            sibling = own_ref[0:1, span] >> 4 & 3
            key = rank + (128 * (sibling & 1)).astype(F32)
            rows_ref[0:1, span] = jnp.where(sibling < 2, key, -1.0)
            rows_ref[1:2, span] = jnp.where(sibling < 2, -1.0, key)
        return held

    lax.fori_loop(0, own_ref.shape[1] // width // RANK_UNROLL, several, start)


def place_sources(high, rows_ref, charge_ref, hold, accs):
    blocks = charge_ref.shape[1] // BLOCK
    cells = iota((256, BLOCK), 0).astype(F32).astype(BF16)
    lows = (iota((16, BLOCK), 0) + 16 * high).astype(F32).astype(BF16)
    none = jnp.zeros((), BF16)

    def one(step, carried):
        for u in range(ROUTE_UNROLL):
            span = pl.ds(pl.multiple_of((step * ROUTE_UNROLL + u) * BLOCK, BLOCK), BLOCK)
            row = rows_ref[2:3, span].astype(BF16)
            low = jnp.broadcast_to(row, (32, BLOCK))
            charge = charge_ref[:, span]
            parts = [jnp.where(low == float(high * 16 + n), charge, none) for n in range(16)]
            mine = lows == row
            for kind in range(2):
                parts.append(jnp.where(mine, rows_ref[3 + kind : 4 + kind, span].astype(BF16), none))
            parts = jnp.concatenate(parts, axis=0)
            for side in range(2):
                slots = one_hot(cells, rows_ref[side : side + 1, span].astype(BF16))
                pltpu.matmul_push_rhs(slots, u % 2, side, transpose=True)
                pltpu.matmul_acc_lhs(accs[side], parts, load_staged_rhs=u % 2)
        return carried

    lax.fori_loop(0, blocks // ROUTE_UNROLL, one, 0)
    for side in range(2):
        hold[high, side] = pltpu.matmul_pop(accs[side])


def route_kernel(
    own_hbm, point_hbm, value_hbm, send_ref, own, point, value, rows, charge, tri, hold, sems
):
    copies = [
        pltpu.make_async_copy(source, target, sems.at[number])
        for number, (source, target) in enumerate(
            ((own_hbm, own), (point_hbm, point), (value_hbm, value))
        )
    ]
    for copy in copies:
        copy.start()
    earlier = iota((BLOCK, BLOCK), 0) < iota((BLOCK, BLOCK), 1)
    tri[...] = jnp.where(earlier, 1.0, 0.0).astype(BF16)
    for copy in copies:
        copy.wait()
    pl.run_scoped(
        lambda *accs: rank_sources(own, point, value, rows, charge, tri, accs),
        *[pltpu.ACC(number % 2)((128, 256), F32) for number in range(2 * RANK_UNROLL)],
    )
    for high in range(2):
        pl.run_scoped(
            lambda *accs, high=high: place_sources(high, rows, charge, hold, accs),
            *[pltpu.ACC(number)((544, 256), F32) for number in range(2)],
        )
    for number in range(32):
        high, low = number // 16, number % 16
        first = high * 64 + low
        for group in range(4):
            at = low * 32 + group * 8
            for y in range(4):
                tile = hold[high, y // 2, at : at + 8, y % 2 * 128 : y % 2 * 128 + 128]
                send_ref[first + group * 16, y] = tile.astype(BF16)
        tile = [
            hold[high, y // 2, pl.ds(512 + 16 * kind + low, 1), y % 2 * 128 : y % 2 * 128 + 128]
            for kind in range(2)
            for y in range(4)
        ]
        tile = jnp.concatenate(tile, axis=0).astype(BF16)
        for group in range(4):
            send_ref[first + group * 16, 4] = tile


def route(owner, point, value):
    sources = owner.shape[1]
    vmem = pl.BlockSpec(memory_space=pltpu.VMEM)
    return pl.pallas_call(
        route_kernel,
        in_specs=[pl.BlockSpec(memory_space=pltpu.HBM)] * 3,
        out_specs=vmem,
        out_shape=jax.ShapeDtypeStruct((128, 5, 8, 128), BF16),
        scratch_shapes=[
            pltpu.VMEM((1, sources), jnp.int32),
            pltpu.VMEM((2, sources), jnp.int32),
            pltpu.VMEM((32, sources), BF16),
            pltpu.VMEM((8, sources), F32),
            pltpu.VMEM((32, sources), BF16),
            pltpu.VMEM((BLOCK, BLOCK), BF16),
            pltpu.VMEM((2, 2, 544, 256), F32),
            pltpu.SemaphoreType.DMA((3,)),
        ],
        compiler_params=pltpu.CompilerParams(vmem_limit_bytes=60 * MIB),
        cost_estimate=cost(15),
        name="route",
    )(owner, point, value)


def level_starts(depth):
    return [(high, low) for high in range(2**depth) for low in range(2 ** (LEVX - 1 - depth))]


def phases_kernel(
    where_ref, level_c, level_s, eight_c, eight_s, nine_c, nine_s, ten_c, ten_s
):
    row_high = where_ref[0].astype(F32)
    row_y = where_ref[1]
    sign = signs((8, 128))
    row_x = row_high * 4.0 + (iota((8, 128), 0) // HALF).astype(F32)
    flat_y = jnp.full((8, 128), row_y.astype(F32))
    for depth in range(LEVX):
        below = LEVX - 1 - depth
        for axis in range(2):
            row = (row_x, flat_y)[axis]
            for place, (high, low) in enumerate(level_starts(depth)):
                parent = row * float(2**below) + float(reversed_bits(low, below))
                for t in range(2):
                    cosine, sine = unit_phase(parent * float(2 * high + t))
                    level_c[2 * depth + axis, 2 * place + t] = cosine
                    level_s[2 * depth + axis, 2 * place + t] = sine * sign

    key = iota((16, 8, 128), 0).astype(F32)
    sign = signs((16, 8, 128))
    for pair in range(2):
        for t in range(2):
            cosine, sine = unit_phase((row_high * 2.0 + float(pair)) * (2.0 * key + float(t)))
            eight_c[pair, t] = cosine
            eight_s[pair, t] = sine * sign
            cosine, sine = unit_phase(row_high * (2.0 * (2.0 * key + float(pair)) + float(t)))
            ten_c[pair, t] = cosine
            ten_s[pair, t] = sine * sign

    core = (row_y & 1).astype(F32)
    target = 2.0 * iota((16, 128), 0).astype(F32) + core
    cosine, sine = unit_phase((row_y >> 1).astype(F32) * target)
    nine_c[...] = cosine
    nine_s[...] = sine * signs((16, 128))


def phases(where):
    shapes = [(8, 16, 8, 128), (2, 2, 16, 8, 128), (16, 128), (2, 2, 16, 8, 128)]
    return pl.pallas_call(
        phases_kernel,
        in_specs=[pl.BlockSpec(memory_space=pltpu.SMEM)],
        out_specs=[pl.BlockSpec(memory_space=pltpu.VMEM)] * 8,
        out_shape=[jax.ShapeDtypeStruct(shape, F32) for shape in shapes for _ in range(2)],
        compiler_params=pltpu.CompilerParams(vmem_limit_bytes=40 * MIB),
        cost_estimate=cost(2),
        name="phases",
    )(where)


def nodes_and_scales():
    nodes = [0.5 + 0.5 * math.cos(math.pi * (2 * a + 1) / (2 * QX)) for a in range(QX)]
    scales = []
    for a in range(QX):
        scale = 1.0
        for c in range(QX):
            if c != a:
                scale /= nodes[a] - nodes[c]
        scales.append(scale)
    return nodes, scales


def column(values, shape):
    row = iota(shape, 0)
    out = jnp.full(shape, values[0], F32)
    for index in range(1, len(values)):
        out = jnp.where(row == index, values[index], out)
    return out


def interpolation(position, nodes, scales):
    gap = position - nodes
    one = pltpu.roll(gap, 7, axis=0)
    two = one * pltpu.roll(one, 7, axis=0)
    four = two * pltpu.roll(two, 6, axis=0)
    return scales * four * pltpu.roll(two, 4, axis=0) * pltpu.roll(one, 2, axis=0)


def swapped_parts(matrix):
    blocks = [matrix[row : row + 64] for row in range(0, matrix.shape[0], 64)]
    order = [number ^ 1 for number in range(len(blocks))]
    return jnp.concatenate([blocks[number] for number in order], axis=0)


def signs(shape):
    return jnp.where(iota(shape, len(shape) - 1) < 64, -1.0, 1.0)


def level_matrix(mats_ref, level):
    return jnp.concatenate(
        [
            jnp.concatenate([mats_ref[level, t, 0], mats_ref[level, t, 1]], axis=1)
            for t in range(2)
        ],
        axis=0,
    )


def leaves_kernel(got_ref, out_ref, points):
    points[...] = got_ref[:, 4].astype(F32)
    nodes, scales = nodes_and_scales()
    nodes = column(nodes, (8, 128))
    scales = column(scales, (8, 128))
    cells = iota((256, 128), 0).astype(F32).astype(BF16)

    def operands(source, y):
        charge = got_ref[source, y].astype(F32)
        box = points[source, y : y + 1, :]
        offset = points[source, 4 + y : 5 + y, :]
        coarse = jnp.floor(offset * (1.0 / LAT))
        fine = offset - LAT * coarse
        over_x = interpolation((coarse + 0.5) * (1.0 / LAT), nodes, scales)
        over_y = interpolation((fine + 0.5) * (1.0 / LAT), nodes, scales)
        both = jnp.concatenate([over_x[a : a + 1] * over_y for a in range(QX)], axis=0)
        both = both.astype(BF16)
        rows = []
        for h in range(4):
            for part in range(2):
                at = part * 4 + h
                rows.append(both * charge[at : at + 1].astype(BF16))
        return one_hot(cells, box.astype(BF16)), jnp.concatenate(rows, axis=0)

    def run(*accs):
        for y in range(4):

            for step in range(32):
                for m in range(2):
                    source = step * 4 + m * 2
                    boxes0, spread0 = operands(source, y)
                    boxes1, spread1 = operands(source + 1, y)
                    boxes = jnp.concatenate([boxes0, boxes1], axis=1)
                    spread = jnp.concatenate([spread0, spread1], axis=1)
                    pltpu.matmul_push_rhs(boxes, step % 2, m, transpose=True)
                    pltpu.matmul_acc_lhs(accs[m], spread, load_staged_rhs=step % 2)
            total = pltpu.matmul_pop(accs[0]) + pltpu.matmul_pop(accs[1])
            for h in range(4):
                rows = pl.ds(y * HALF + h % HALF, 256, stride=8)
                out_ref[h // HALF, rows, :] = total[h * 128 : (h + 1) * 128].T

    pl.run_scoped(run, pltpu.ACC(0)((512, 256), F32), pltpu.ACC(1)((512, 256), F32))


def leaves(got):
    vmem = pl.BlockSpec(memory_space=pltpu.VMEM)
    return pl.pallas_call(
        leaves_kernel,
        in_specs=[vmem],
        out_specs=vmem,
        out_shape=jax.ShapeDtypeStruct((2, 2048, 128), F32),
        scratch_shapes=[pltpu.VMEM((128, 8, 128), F32)],
        compiler_params=pltpu.CompilerParams(vmem_limit_bytes=40 * MIB),
        cost_estimate=cost(19),
        name="leaves",
    )(got)


def inner_kernel(leaf_ref, mats_ref, level_c, level_s, eight_c, eight_s, out0, out1, work0, work1):
    tables = (level_c, level_s, eight_c, eight_s)
    works, outs = (work0, work1), (out0, out1)
    stages = [
        (level, half, number)
        for level in range(2 * LEVX + 1)
        for half in range(2)
        for number in range(2)
    ]

    def run(*accs):
        def start(at):
            level, half, number = stages[at]
            work = leaf_ref.at[half] if level == 0 else works[half]
            if level < 2 * LEVX:
                lefts = level_lefts(level, work, number)
            else:
                lefts = eighth_lefts(work, number)
            own = accs[at % 2 * 4 : at % 2 * 4 + 4]
            first = half == 0 and number == 0
            if first:
                right = level_matrix(mats_ref, level)
                pltpu.matmul_push_rhs(right, level % 2, 0, transpose=True)
                pltpu.matmul_push_rhs(swapped_parts(right), level % 2, 1, transpose=True)
            for place, left in enumerate(lefts):
                for m in range(2):
                    if place == 0 or m == at % 2:
                        load = level % 2 if first and place == 0 else None
                        pltpu.matmul_acc_lhs(own[2 * place + m], left, load_staged_rhs=load)

        def finish(at):
            level, half, number = stages[at]
            own = accs[at % 2 * 4 : at % 2 * 4 + 4]
            for place in range(2):
                both = place == 0
                made = pltpu.matmul_pop(own[2 * place]) if both or at % 2 == 0 else None
                other = pltpu.matmul_pop(own[2 * place + 1]) if both or at % 2 == 1 else None
                if level < 2 * LEVX:
                    level_turns(level, tables, works[half], 2 * number + place, made, other)
                else:
                    eighth_turns(tables, outs[half], number, place, made, other)

        start(0)
        start(1)
        for at in range(len(stages)):
            finish(at)
            if at + 2 < len(stages):
                start(at + 2)

    pl.run_scoped(run, *[pltpu.ACC(number % 2)((256, 256), F32) for number in range(8)])


def box_rows(x, y):
    return pl.ds((x * 16 + y) * 8, 8)


def line(work, level, at):
    if level % 2 == 0:
        return work[pl.ds(at * 128, 128), :].astype(BF16)
    return jnp.concatenate([work[box_rows(x, at), :] for x in range(16)], axis=0).astype(BF16)


def level_lefts(level, work, half):
    below = LEVX - 1 - level // 2
    starts = [high << below + 1 | low for high, low in level_starts(level // 2)]
    lefts = []
    for number in range(2 * half, 2 * half + 2):
        first = starts[2 * number : 2 * number + 2]
        ends = [[line(work, level, s | t << below) for s in first] for t in range(2)]
        ends = [jnp.concatenate(end, axis=0) for end in ends]
        lefts.append(jnp.concatenate(ends, axis=1))
    return lefts


def two_forms(made, other, chosen):
    if made is None:
        other = other[chosen]
        return pltpu.roll(other, 64, axis=1), other
    made = made[chosen]
    return made, pltpu.roll(made, 64, axis=1) if other is None else other[chosen]


def level_turns(level, tables, work, number, made, other):
    level_c, level_s = tables[:2]
    below = LEVX - 1 - level // 2
    starts = [high << below + 1 | low for high, low in level_starts(level // 2)]
    for place in range(2):
        at = 2 * number + place
        for t in range(2):
            chosen = (slice(place * 128, place * 128 + 128), slice(t * 128, t * 128 + 128))
            cosine, sine = level_c[level, 2 * at + t], level_s[level, 2 * at + t]
            plain, swapped = two_forms(made, other, chosen)
            piece = plain.reshape(16, 8, 128) * cosine[None]
            piece = piece + swapped.reshape(16, 8, 128) * sine[None]
            end = starts[at] | t << below
            if level % 2 == 0:
                work[pl.ds(end * 128, 128), :] = piece.reshape(128, 128)
            else:
                for x in range(16):
                    work[box_rows(x, end), :] = piece[x]


def eighth_lefts(work, pair):
    lefts = []
    for h in range(HALF):
        both = [
            work[pl.ds((2 * pair + c) * HALF + h, 256, stride=8), :].astype(BF16) for c in range(2)
        ]
        lefts.append(jnp.concatenate(both, axis=1))
    return lefts


def eighth_turns(tables, out_ref, pair, h, made, other):
    eight_c, eight_s = tables[2:]
    for t in range(2):
        chosen = (slice(None), slice(t * 128, t * 128 + 128))
        plain, swapped = two_forms(made, other, chosen)
        piece = plain.reshape(16, 2, 8, 128) * eight_c[pair, t][:, None]
        piece = piece + swapped.reshape(16, 2, 8, 128) * eight_s[pair, t][:, None]
        out_ref[pair, t, h] = piece.reshape(256, 128).astype(BF16)


def inner(leaf, mats, tables):
    vmem = pl.BlockSpec(memory_space=pltpu.VMEM)
    return pl.pallas_call(
        inner_kernel,
        in_specs=[vmem] * 6,
        out_specs=[vmem] * 2,
        out_shape=[jax.ShapeDtypeStruct((2, 2, HALF, 256, 128), BF16)] * 2,
        scratch_shapes=[pltpu.VMEM((2048, 128), F32)] * 2,
        compiler_params=pltpu.CompilerParams(vmem_limit_bytes=40 * MIB),
        cost_estimate=cost(5),
        name="inner",
    )(leaf, mats, *tables[:4])


def outer_kernel(
    where_ref, mine_ref, other_ref, mats_ref, nine_c, nine_s, ten_c, ten_s, after_ref, *refs
):
    del after_ref
    outs, held = refs[:4], refs[4]
    row_y = where_ref[1]
    own = where_ref[2]
    core = row_y & 1
    table = (nine_c[...][None], nine_s[...][None])
    mats_y = jnp.concatenate([mats_ref[0, core, core], mats_ref[0, core, 1 - core]], axis=1)
    mats_y = jnp.concatenate([mats_y, swapped_parts(mats_y)], axis=0)
    mats_x = level_matrix(mats_ref, 1)
    mats_x = jnp.concatenate([mats_x, swapped_parts(mats_x)], axis=0)
    for t8 in range(2):
        tables = [(ten_c[t8, t][:, None], ten_s[t8, t][:, None]) for t in range(2)]
        for h in range(HALF):
            both = []
            for c in range(2):
                pair = jnp.concatenate([mine_ref[c, t8, h], other_ref[c, t8, h]], axis=1)
                made = matmul_nt(pair, mats_y)
                piece = made[:, :128].reshape(16, 16, 128) * table[0]
                piece = piece + made[:, 128:].reshape(16, 16, 128) * table[1]
                both.append(piece.reshape(256, 128).astype(BF16))
            made = matmul_nt(jnp.concatenate(both, axis=1), mats_x)
            for t in range(2):
                plain = made[:, t * 128 : t * 128 + 128].reshape(16, 2, 8, 128)
                other = made[:, t * 128 + 256 : t * 128 + 384].reshape(16, 2, 8, 128)
                piece = plain * tables[t][0] + other * tables[t][1]
                held[2 * t + t8, h] = piece.reshape(256, 128).astype(BF16)
    for shift in range(4):
        outs[shift][...] = held[(own + shift) & 3]


def outer(where, mine, other, mats, tables, after):
    vmem = pl.BlockSpec(memory_space=pltpu.VMEM)
    return pl.pallas_call(
        outer_kernel,
        in_specs=[pl.BlockSpec(memory_space=pltpu.SMEM)]
        + [vmem] * 7
        + [pl.BlockSpec(memory_space=pl.ANY)],
        out_specs=[vmem] * 4,
        out_shape=[jax.ShapeDtypeStruct((HALF, 256, 128), BF16)] * 4,
        scratch_shapes=[pltpu.VMEM((4, HALF, 256, 128), BF16)],
        compiler_params=pltpu.CompilerParams(vmem_limit_bytes=40 * MIB),
        cost_estimate=cost(3),
        name="outer",
    )(where, mine, other, mats, *tables[4:], after)


def finish_kernel(where_ref, *refs):
    got, out_ref, held = refs[:8], refs[8], refs[9]
    own = where_ref[2]
    for half in range(2):
        for shift in range(4):
            group = (own - shift) & 3
            for h in range(HALF):
                row = group * 4 + (half * HALF + h)
                held[pl.ds(row, 256, stride=16), :] = got[half * 4 + shift][h].astype(F32)
    for block in range(32):
        span = slice(block * 128, (block + 1) * 128)
        out_ref[:, span] = held[span].astype(BF16).T


def finish(where, got):
    vmem = pl.BlockSpec(memory_space=pltpu.VMEM)
    return pl.pallas_call(
        finish_kernel,
        in_specs=[pl.BlockSpec(memory_space=pltpu.SMEM)] + [vmem] * 8,
        out_specs=vmem,
        out_shape=jax.ShapeDtypeStruct((128, 4096), BF16),
        scratch_shapes=[pltpu.VMEM((4096, 128), F32)],
        compiler_params=pltpu.CompilerParams(vmem_limit_bytes=40 * MIB),
        cost_estimate=cost(3),
        name="finish",
    )(where, *got)


def block_matrices(translation):
    parts = translation.reshape(-1, 2, 2, 2, R, R)
    real = parts[:, :, :, 0]
    imag = parts[:, :, :, 1]
    top = jnp.concatenate([real, -imag], axis=-1)
    bottom = jnp.concatenate([imag, real], axis=-1)
    return jnp.concatenate([top, bottom], axis=-2)


def body(src_value, src_point, src_owner, translation):
    row_x = lax.axis_index("gx")
    row_y = lax.axis_index("gy")
    where = jnp.stack([row_x >> 2, row_y, row_x & 3]).astype(jnp.int32)

    send = route(src_owner.reshape(1, -1), src_point, src_value)
    got = lax.all_to_all(send, ("gx", "gy"), split_axis=0, concat_axis=0, tiled=True)
    mats = block_matrices(translation)
    inner_mats = mats[: 2 * LEVX + 1]
    outer_mats = mats[2 * LEVX + 1 :]
    leaf = leaves(got)
    cores = [(i, i ^ 1) for i in range(lax.axis_size("gy"))]
    tables = phases(where)
    last = where
    got = []
    for mine in inner(leaf, inner_mats, tables):
        other = lax.ppermute(mine, "gy", cores)
        outs = outer(where, mine, other, outer_mats, tables, last)
        last = outs[0]
        got.append(outs[0])
        for shift in range(1, 4):
            pairs = [(i, i // 4 * 4 + (i + shift) % 4) for i in range(lax.axis_size("gx"))]
            got.append(lax.ppermute(outs[shift], "gx", pairs))
    return finish(where, got).reshape(128, 1, 1, 4096)


def solution(mesh):
    return jax.shard_map(
        body,
        mesh=mesh,
        in_specs=(P(None, ("gx", "gy")), P(None, ("gx", "gy")), P(("gx", "gy"), None), P()),
        out_specs=P(None, "gx", "gy", None),
        check_vma=False,
    )
```

```python
import functools
import math

import jax
import jax.numpy as jnp
from jax import lax
from jax.experimental import pallas as pl
from jax.experimental.pallas import tpu as pltpu
from jax.sharding import PartitionSpec as P

QX = 8
R = 64
LEVX = 4
LB = 16
LAT = 16
CAP = 128

F32 = jnp.float32
BF16 = jnp.bfloat16
MODULUS = 61.0
MIB = 1024 * 1024

BLOCK = 256
HALF = 2
RANK_UNROLL = 8
ROUTE_UNROLL = 32


def matmul_nt(lhs, rhs):
    return lax.dot_general(lhs, rhs, (((1,), (1,)), ((), ())), preferred_element_type=F32)


def unit_phase(product):
    rest = product - MODULUS * jnp.floor(product * (1.0 / MODULUS) + 0.5)
    x = rest * (math.pi / MODULUS)
    x2 = x * x
    s = x * (1.0 + x2 * (-1 / 6 + x2 * (1 / 120 + x2 * (-1 / 5040 + x2 * (1 / 362880 + x2 * (-1 / 39916800))))))
    c = 1.0 + x2 * (-1 / 2 + x2 * (1 / 24 + x2 * (-1 / 720 + x2 * (1 / 40320 + x2 * (-1 / 3628800)))))
    return 1.0 - 2.0 * s * s, 2.0 * s * c


def cost(micros):
    return pl.CostEstimate(flops=int(micros * 1.0e9), bytes_accessed=0, transcendentals=0)


def iota(shape, dim):
    return lax.broadcasted_iota(jnp.int32, shape, dim)


def reversed_bits(value, bits):
    out = 0
    for bit in range(bits):
        out |= (value >> bit & 1) << (bits - 1 - bit)
    return out


def nibble_reversed(value):
    return (value & 1) << 3 | (value & 2) << 1 | value >> 1 & 2 | value >> 3 & 1


def one_hot(cells, row):
    return jnp.where(cells == row, jnp.ones((), BF16), jnp.zeros((), BF16))


def rank_sources(own_ref, point_ref, value_ref, rows_ref, charge_ref, tri, accs):
    width = BLOCK
    owners = iota((128, width), 0).astype(F32).astype(BF16)
    before_accs, whole_accs = accs[0::2], accs[1::2]

    pltpu.matmul_push_rhs(tri[...], 0, 0)
    pltpu.matmul_acc_lhs(before_accs[0], jnp.zeros((128, width), BF16), load_staged_rhs=0)
    pltpu.matmul_push_rhs(jnp.ones((width, width), BF16), 0, 1)
    pltpu.matmul_acc_lhs(whole_accs[0], jnp.zeros((128, width), BF16), load_staged_rhs=0)
    start = pltpu.matmul_pop(before_accs[0]) + pltpu.matmul_pop(whole_accs[0])

    def several(step, held):
        spans = [
            pl.ds(pl.multiple_of((step * RANK_UNROLL + u) * width, width), width)
            for u in range(RANK_UNROLL)
        ]
        hits = []
        for u, span in enumerate(spans):
            own = own_ref[0:1, span]
            hits.append(one_hot(owners, own.astype(F32).astype(BF16)))
            pltpu.matmul_acc_lhs(before_accs[u], hits[u])
            pltpu.matmul_acc_lhs(whole_accs[u], hits[u])
        for u, span in enumerate(spans):
            own = own_ref[0:1, span]
            px = point_ref[0:1, span]
            py = point_ref[1:2, span]
            rows_ref[2:3, span] = ((own >> 6) * 16 + (own & 15)).astype(F32)
            box = nibble_reversed(px >> 4) * 16 + nibble_reversed(py >> 4)
            rows_ref[3:4, span] = box.astype(F32)
            rows_ref[4:5, span] = ((px & 15) * 16 + (py & 15)).astype(F32)
            big_x = (own >> 4) * (LB * LAT) + px
            big_y = (own & 15) * (LB * LAT) + py
            cosine, sine = unit_phase(big_x.astype(F32) * big_y.astype(F32))
            real = value_ref[0:16, span].astype(F32)
            imag = value_ref[16:32, span].astype(F32)
            turned_real = cosine * real - sine * imag
            turned_imag = sine * real + cosine * imag
            parts = []
            for group in range(4):
                parts.append(turned_real[4 * group : 4 * group + 4])
                parts.append(turned_imag[4 * group : 4 * group + 4])
            charge_ref[:, span] = jnp.concatenate(parts, axis=0).astype(BF16)
        for u, span in enumerate(spans):
            before = pltpu.matmul_pop(before_accs[u]) + held
            held = held + pltpu.matmul_pop(whole_accs[u])
            rank = jnp.sum(hits[u].astype(F32) * before, axis=0, keepdims=True)
            sibling = own_ref[0:1, span] >> 4 & 3
            key = rank + (128 * (sibling & 1)).astype(F32)
            rows_ref[0:1, span] = jnp.where(sibling < 2, key, -1.0)
            rows_ref[1:2, span] = jnp.where(sibling < 2, -1.0, key)
        return held

    lax.fori_loop(0, own_ref.shape[1] // width // RANK_UNROLL, several, start)


def place_sources(high, rows_ref, charge_ref, hold, accs):
    blocks = charge_ref.shape[1] // BLOCK
    cells = iota((256, BLOCK), 0).astype(F32).astype(BF16)
    lows = (iota((16, BLOCK), 0) + 16 * high).astype(F32).astype(BF16)
    none = jnp.zeros((), BF16)

    def one(step, carried):
        for u in range(ROUTE_UNROLL):
            span = pl.ds(pl.multiple_of((step * ROUTE_UNROLL + u) * BLOCK, BLOCK), BLOCK)
            row = rows_ref[2:3, span].astype(BF16)
            low = jnp.broadcast_to(row, (32, BLOCK))
            charge = charge_ref[:, span]
            parts = [jnp.where(low == float(high * 16 + n), charge, none) for n in range(16)]
            mine = lows == row
            for kind in range(2):
                parts.append(jnp.where(mine, rows_ref[3 + kind : 4 + kind, span].astype(BF16), none))
            parts = jnp.concatenate(parts, axis=0)
            for side in range(2):
                slots = one_hot(cells, rows_ref[side : side + 1, span].astype(BF16))
                pltpu.matmul_push_rhs(slots, u % 2, side, transpose=True)
                pltpu.matmul_acc_lhs(accs[side], parts, load_staged_rhs=u % 2)
        return carried

    lax.fori_loop(0, blocks // ROUTE_UNROLL, one, 0)
    for side in range(2):
        hold[high, side] = pltpu.matmul_pop(accs[side])


def route_kernel(
    own_hbm, point_hbm, value_hbm, send_ref, own, point, value, rows, charge, tri, hold, sems
):
    copies = [
        pltpu.make_async_copy(source, target, sems.at[number])
        for number, (source, target) in enumerate(
            ((own_hbm, own), (point_hbm, point), (value_hbm, value))
        )
    ]
    for copy in copies:
        copy.start()
    earlier = iota((BLOCK, BLOCK), 0) < iota((BLOCK, BLOCK), 1)
    tri[...] = jnp.where(earlier, 1.0, 0.0).astype(BF16)
    for copy in copies:
        copy.wait()
    pl.run_scoped(
        lambda *accs: rank_sources(own, point, value, rows, charge, tri, accs),
        *[pltpu.ACC(number % 2)((128, 256), F32) for number in range(2 * RANK_UNROLL)],
    )
    for high in range(2):
        pl.run_scoped(
            lambda *accs, high=high: place_sources(high, rows, charge, hold, accs),
            *[pltpu.ACC(number)((544, 256), F32) for number in range(2)],
        )
    for number in range(32):
        high, low = number // 16, number % 16
        first = high * 64 + low
        for group in range(4):
            at = low * 32 + group * 8
            for y in range(4):
                tile = hold[high, y // 2, at : at + 8, y % 2 * 128 : y % 2 * 128 + 128]
                send_ref[first + group * 16, y] = tile.astype(BF16)
        tile = [
            hold[high, y // 2, pl.ds(512 + 16 * kind + low, 1), y % 2 * 128 : y % 2 * 128 + 128]
            for kind in range(2)
            for y in range(4)
        ]
        tile = jnp.concatenate(tile, axis=0).astype(BF16)
        for group in range(4):
            send_ref[first + group * 16, 4] = tile


def route(owner, point, value):
    sources = owner.shape[1]
    vmem = pl.BlockSpec(memory_space=pltpu.VMEM)
    return pl.pallas_call(
        route_kernel,
        in_specs=[pl.BlockSpec(memory_space=pltpu.HBM)] * 3,
        out_specs=vmem,
        out_shape=jax.ShapeDtypeStruct((128, 5, 8, 128), BF16),
        scratch_shapes=[
            pltpu.VMEM((1, sources), jnp.int32),
            pltpu.VMEM((2, sources), jnp.int32),
            pltpu.VMEM((32, sources), BF16),
            pltpu.VMEM((8, sources), F32),
            pltpu.VMEM((32, sources), BF16),
            pltpu.VMEM((BLOCK, BLOCK), BF16),
            pltpu.VMEM((2, 2, 544, 256), F32),
            pltpu.SemaphoreType.DMA((3,)),
        ],
        compiler_params=pltpu.CompilerParams(vmem_limit_bytes=60 * MIB),
        cost_estimate=cost(15),
        name="route",
    )(owner, point, value)


def level_starts(depth):
    return [(high, low) for high in range(2**depth) for low in range(2 ** (LEVX - 1 - depth))]


def phases_kernel(
    where_ref, level_c, level_s, eight_c, eight_s, nine_c, nine_s, ten_c, ten_s
):
    row_high = where_ref[0].astype(F32)
    row_y = where_ref[1]
    sign = signs((8, 128))
    row_x = row_high * 4.0 + (iota((8, 128), 0) // HALF).astype(F32)
    flat_y = jnp.full((8, 128), row_y.astype(F32))
    for depth in range(LEVX):
        below = LEVX - 1 - depth
        for axis in range(2):
            row = (row_x, flat_y)[axis]
            for place, (high, low) in enumerate(level_starts(depth)):
                parent = row * float(2**below) + float(reversed_bits(low, below))
                for t in range(2):
                    cosine, sine = unit_phase(parent * float(2 * high + t))
                    level_c[2 * depth + axis, 2 * place + t] = cosine
                    level_s[2 * depth + axis, 2 * place + t] = sine * sign

    key = iota((16, 8, 128), 0).astype(F32)
    sign = signs((16, 8, 128))
    for pair in range(2):
        for t in range(2):
            cosine, sine = unit_phase((row_high * 2.0 + float(pair)) * (2.0 * key + float(t)))
            eight_c[pair, t] = cosine
            eight_s[pair, t] = sine * sign
            cosine, sine = unit_phase(row_high * (2.0 * (2.0 * key + float(pair)) + float(t)))
            ten_c[pair, t] = cosine
            ten_s[pair, t] = sine * sign

    core = (row_y & 1).astype(F32)
    target = 2.0 * iota((16, 128), 0).astype(F32) + core
    cosine, sine = unit_phase((row_y >> 1).astype(F32) * target)
    nine_c[...] = cosine
    nine_s[...] = sine * signs((16, 128))


def phases(where):
    shapes = [(8, 16, 8, 128), (2, 2, 16, 8, 128), (16, 128), (2, 2, 16, 8, 128)]
    return pl.pallas_call(
        phases_kernel,
        in_specs=[pl.BlockSpec(memory_space=pltpu.SMEM)],
        out_specs=[pl.BlockSpec(memory_space=pltpu.VMEM)] * 8,
        out_shape=[jax.ShapeDtypeStruct(shape, F32) for shape in shapes for _ in range(2)],
        compiler_params=pltpu.CompilerParams(vmem_limit_bytes=40 * MIB),
        cost_estimate=cost(2),
        name="phases",
    )(where)


def nodes_and_scales():
    nodes = [0.5 + 0.5 * math.cos(math.pi * (2 * a + 1) / (2 * QX)) for a in range(QX)]
    scales = []
    for a in range(QX):
        scale = 1.0
        for c in range(QX):
            if c != a:
                scale /= nodes[a] - nodes[c]
        scales.append(scale)
    return nodes, scales


def column(values, shape):
    row = iota(shape, 0)
    out = jnp.full(shape, values[0], F32)
    for index in range(1, len(values)):
        out = jnp.where(row == index, values[index], out)
    return out


def interpolation(position, nodes, scales):
    gap = position - nodes
    one = pltpu.roll(gap, 7, axis=0)
    two = one * pltpu.roll(one, 7, axis=0)
    four = two * pltpu.roll(two, 6, axis=0)
    return scales * four * pltpu.roll(two, 4, axis=0) * pltpu.roll(one, 2, axis=0)


def swapped_parts(matrix):
    blocks = [matrix[row : row + 64] for row in range(0, matrix.shape[0], 64)]
    order = [number ^ 1 for number in range(len(blocks))]
    return jnp.concatenate([blocks[number] for number in order], axis=0)


def signs(shape):
    return jnp.where(iota(shape, len(shape) - 1) < 64, -1.0, 1.0)


def level_matrix(mats_ref, level):
    return jnp.concatenate(
        [
            jnp.concatenate([mats_ref[level, t, 0], mats_ref[level, t, 1]], axis=1)
            for t in range(2)
        ],
        axis=0,
    )


def leaves_kernel(got_ref, out_ref, points):
    points[...] = got_ref[:, 4].astype(F32)
    nodes, scales = nodes_and_scales()
    nodes = column(nodes, (8, 128))
    scales = column(scales, (8, 128))
    cells = iota((256, 128), 0).astype(F32).astype(BF16)

    def operands(source, y):
        charge = got_ref[source, y].astype(F32)
        box = points[source, y : y + 1, :]
        offset = points[source, 4 + y : 5 + y, :]
        coarse = jnp.floor(offset * (1.0 / LAT))
        fine = offset - LAT * coarse
        over_x = interpolation((coarse + 0.5) * (1.0 / LAT), nodes, scales)
        over_y = interpolation((fine + 0.5) * (1.0 / LAT), nodes, scales)
        both = jnp.concatenate([over_x[a : a + 1] * over_y for a in range(QX)], axis=0)
        both = both.astype(BF16)
        rows = []
        for h in range(4):
            for part in range(2):
                at = part * 4 + h
                rows.append(both * charge[at : at + 1].astype(BF16))
        return one_hot(cells, box.astype(BF16)), jnp.concatenate(rows, axis=0)

    def run(*accs):
        for y in range(4):

            for step in range(32):
                for m in range(2):
                    source = step * 4 + m * 2
                    boxes0, spread0 = operands(source, y)
                    boxes1, spread1 = operands(source + 1, y)
                    boxes = jnp.concatenate([boxes0, boxes1], axis=1)
                    spread = jnp.concatenate([spread0, spread1], axis=1)
                    pltpu.matmul_push_rhs(boxes, step % 2, m, transpose=True)
                    pltpu.matmul_acc_lhs(accs[m], spread, load_staged_rhs=step % 2)
            total = pltpu.matmul_pop(accs[0]) + pltpu.matmul_pop(accs[1])
            for h in range(4):
                rows = pl.ds(y * HALF + h % HALF, 256, stride=8)
                out_ref[h // HALF, rows, :] = total[h * 128 : (h + 1) * 128].T

    pl.run_scoped(run, pltpu.ACC(0)((512, 256), F32), pltpu.ACC(1)((512, 256), F32))


def leaves(got):
    vmem = pl.BlockSpec(memory_space=pltpu.VMEM)
    return pl.pallas_call(
        leaves_kernel,
        in_specs=[vmem],
        out_specs=vmem,
        out_shape=jax.ShapeDtypeStruct((2, 2048, 128), F32),
        scratch_shapes=[pltpu.VMEM((128, 8, 128), F32)],
        compiler_params=pltpu.CompilerParams(vmem_limit_bytes=40 * MIB),
        cost_estimate=cost(19),
        name="leaves",
    )(got)


def inner_kernel(leaf_ref, mats_ref, level_c, level_s, eight_c, eight_s, out0, out1, work0, work1):
    tables = (level_c, level_s, eight_c, eight_s)
    works, outs = (work0, work1), (out0, out1)
    stages = [
        (level, half, number)
        for level in range(2 * LEVX + 1)
        for half in range(2)
        for number in range(2)
    ]

    def run(*accs):
        def start(at):
            level, half, number = stages[at]
            work = leaf_ref.at[half] if level == 0 else works[half]
            if level < 2 * LEVX:
                lefts = level_lefts(level, work, number)
            else:
                lefts = eighth_lefts(work, number)
            own = accs[at % 2 * 4 : at % 2 * 4 + 4]
            first = half == 0 and number == 0
            if first:
                right = level_matrix(mats_ref, level)
                pltpu.matmul_push_rhs(right, level % 2, 0, transpose=True)
                pltpu.matmul_push_rhs(swapped_parts(right), level % 2, 1, transpose=True)
            for place, left in enumerate(lefts):
                for m in range(2):
                    if place == 0 or m == at % 2:
                        load = level % 2 if first and place == 0 else None
                        pltpu.matmul_acc_lhs(own[2 * place + m], left, load_staged_rhs=load)

        def finish(at):
            level, half, number = stages[at]
            own = accs[at % 2 * 4 : at % 2 * 4 + 4]
            for place in range(2):
                both = place == 0
                made = pltpu.matmul_pop(own[2 * place]) if both or at % 2 == 0 else None
                other = pltpu.matmul_pop(own[2 * place + 1]) if both or at % 2 == 1 else None
                if level < 2 * LEVX:
                    level_turns(level, tables, works[half], 2 * number + place, made, other)
                else:
                    eighth_turns(tables, outs[half], number, place, made, other)

        start(0)
        start(1)
        for at in range(len(stages)):
            finish(at)
            if at + 2 < len(stages):
                start(at + 2)

    pl.run_scoped(run, *[pltpu.ACC(number % 2)((256, 256), F32) for number in range(8)])


def box_rows(x, y):
    return pl.ds((x * 16 + y) * 8, 8)


def line(work, level, at):
    if level % 2 == 0:
        return work[pl.ds(at * 128, 128), :].astype(BF16)
    return jnp.concatenate([work[box_rows(x, at), :] for x in range(16)], axis=0).astype(BF16)


def level_lefts(level, work, half):
    below = LEVX - 1 - level // 2
    starts = [high << below + 1 | low for high, low in level_starts(level // 2)]
    lefts = []
    for number in range(2 * half, 2 * half + 2):
        first = starts[2 * number : 2 * number + 2]
        ends = [[line(work, level, s | t << below) for s in first] for t in range(2)]
        ends = [jnp.concatenate(end, axis=0) for end in ends]
        lefts.append(jnp.concatenate(ends, axis=1))
    return lefts


def two_forms(made, other, chosen):
    if made is None:
        other = other[chosen]
        return pltpu.roll(other, 64, axis=1), other
    made = made[chosen]
    return made, pltpu.roll(made, 64, axis=1) if other is None else other[chosen]


def level_turns(level, tables, work, number, made, other):
    level_c, level_s = tables[:2]
    below = LEVX - 1 - level // 2
    starts = [high << below + 1 | low for high, low in level_starts(level // 2)]
    for place in range(2):
        at = 2 * number + place
        for t in range(2):
            chosen = (slice(place * 128, place * 128 + 128), slice(t * 128, t * 128 + 128))
            cosine, sine = level_c[level, 2 * at + t], level_s[level, 2 * at + t]
            plain, swapped = two_forms(made, other, chosen)
            piece = plain.reshape(16, 8, 128) * cosine[None]
            piece = piece + swapped.reshape(16, 8, 128) * sine[None]
            end = starts[at] | t << below
            if level % 2 == 0:
                work[pl.ds(end * 128, 128), :] = piece.reshape(128, 128)
            else:
                for x in range(16):
                    work[box_rows(x, end), :] = piece[x]


def eighth_lefts(work, pair):
    lefts = []
    for h in range(HALF):
        both = [
            work[pl.ds((2 * pair + c) * HALF + h, 256, stride=8), :].astype(BF16) for c in range(2)
        ]
        lefts.append(jnp.concatenate(both, axis=1))
    return lefts


def eighth_turns(tables, out_ref, pair, h, made, other):
    eight_c, eight_s = tables[2:]
    for t in range(2):
        chosen = (slice(None), slice(t * 128, t * 128 + 128))
        plain, swapped = two_forms(made, other, chosen)
        piece = plain.reshape(16, 2, 8, 128) * eight_c[pair, t][:, None]
        piece = piece + swapped.reshape(16, 2, 8, 128) * eight_s[pair, t][:, None]
        out_ref[pair, t, h] = piece.reshape(256, 128).astype(BF16)


def inner(leaf, mats, tables):
    vmem = pl.BlockSpec(memory_space=pltpu.VMEM)
    return pl.pallas_call(
        inner_kernel,
        in_specs=[vmem] * 6,
        out_specs=[vmem] * 2,
        out_shape=[jax.ShapeDtypeStruct((2, 2, HALF, 256, 128), BF16)] * 2,
        scratch_shapes=[pltpu.VMEM((2048, 128), F32)] * 2,
        compiler_params=pltpu.CompilerParams(vmem_limit_bytes=40 * MIB),
        cost_estimate=cost(5),
        name="inner",
    )(leaf, mats, *tables[:4])


def outer_kernel(
    where_ref, mine_ref, other_ref, mats_ref, nine_c, nine_s, ten_c, ten_s, after_ref, *refs
):
    del after_ref
    outs, held = refs[:4], refs[4]
    row_y = where_ref[1]
    own = where_ref[2]
    core = row_y & 1
    table = (nine_c[...][None], nine_s[...][None])
    mats_y = jnp.concatenate([mats_ref[0, core, core], mats_ref[0, core, 1 - core]], axis=1)
    mats_y = jnp.concatenate([mats_y, swapped_parts(mats_y)], axis=0)
    mats_x = level_matrix(mats_ref, 1)
    mats_x = jnp.concatenate([mats_x, swapped_parts(mats_x)], axis=0)
    for t8 in range(2):
        tables = [(ten_c[t8, t][:, None], ten_s[t8, t][:, None]) for t in range(2)]
        for h in range(HALF):
            both = []
            for c in range(2):
                pair = jnp.concatenate([mine_ref[c, t8, h], other_ref[c, t8, h]], axis=1)
                made = matmul_nt(pair, mats_y)
                piece = made[:, :128].reshape(16, 16, 128) * table[0]
                piece = piece + made[:, 128:].reshape(16, 16, 128) * table[1]
                both.append(piece.reshape(256, 128).astype(BF16))
            made = matmul_nt(jnp.concatenate(both, axis=1), mats_x)
            for t in range(2):
                plain = made[:, t * 128 : t * 128 + 128].reshape(16, 2, 8, 128)
                other = made[:, t * 128 + 256 : t * 128 + 384].reshape(16, 2, 8, 128)
                piece = plain * tables[t][0] + other * tables[t][1]
                held[2 * t + t8, h] = piece.reshape(256, 128).astype(BF16)
    for shift in range(4):
        outs[shift][...] = held[(own + shift) & 3]


def outer(where, mine, other, mats, tables, after):
    vmem = pl.BlockSpec(memory_space=pltpu.VMEM)
    return pl.pallas_call(
        outer_kernel,
        in_specs=[pl.BlockSpec(memory_space=pltpu.SMEM)]
        + [vmem] * 7
        + [pl.BlockSpec(memory_space=pl.ANY)],
        out_specs=[vmem] * 4,
        out_shape=[jax.ShapeDtypeStruct((HALF, 256, 128), BF16)] * 4,
        scratch_shapes=[pltpu.VMEM((4, HALF, 256, 128), BF16)],
        compiler_params=pltpu.CompilerParams(vmem_limit_bytes=40 * MIB),
        cost_estimate=cost(3),
        name="outer",
    )(where, mine, other, mats, *tables[4:], after)


def finish_kernel(where_ref, *refs):
    got, out_ref, held, sems = refs[:8], *refs[8:]
    own = where_ref[2]
    row = iota((256, 256), 1)
    place = row >> 4
    group = (own - (place >> 1)) & 3
    target = (row & 15) * 16 + group * 4 + (place >> 3) * HALF + (place & 1)
    order = jnp.where(iota((256, 256), 0) == target, 1.0, 0.0).astype(BF16)

    def run(*accs):
        for number, acc in enumerate(accs):
            blocks = []
            for block in (2 * number, 2 * number + 1):
                span = slice(block * 16, block * 16 + 16)
                pieces = [got[at // 2][at % 2, span] for at in range(16)]
                blocks.append(jnp.concatenate(pieces, axis=0))
            m, register = number % 2, number // 2 % 2
            pltpu.matmul_push_rhs(jnp.concatenate(blocks, axis=1), register, m)
            pltpu.matmul_acc_lhs(acc, order, load_staged_rhs=register)
        for number, acc in enumerate(accs):
            made = pltpu.matmul_pop(acc).astype(BF16)
            for side in range(2):
                start = (2 * number + side) * 256
                held[:, start : start + 256] = made[:, side * 128 : side * 128 + 128].T
            if number % 2 == 1:
                copies[number // 2].start()

    copies = []
    for number in range(4):
        span = pl.ds(number * 1024, 1024)
        copies.append(
            pltpu.make_async_copy(held.at[:, span], out_ref.at[:, span], sems.at[number])
        )
    pl.run_scoped(run, *[pltpu.ACC(number % 2)((256, 256), F32) for number in range(8)])
    for copy in copies:
        copy.wait()


def finish(where, got):
    vmem = pl.BlockSpec(memory_space=pltpu.VMEM)
    return pl.pallas_call(
        finish_kernel,
        in_specs=[pl.BlockSpec(memory_space=pltpu.SMEM)] + [vmem] * 8,
        out_specs=pl.BlockSpec(memory_space=pltpu.HBM),
        out_shape=jax.ShapeDtypeStruct((128, 4096), BF16),
        scratch_shapes=[pltpu.VMEM((128, 4096), BF16), pltpu.SemaphoreType.DMA((4,))],
        compiler_params=pltpu.CompilerParams(vmem_limit_bytes=40 * MIB),
        cost_estimate=cost(3),
        name="finish",
    )(where, *got)


def block_matrices(translation):
    parts = translation.reshape(-1, 2, 2, 2, R, R)
    real = parts[:, :, :, 0]
    imag = parts[:, :, :, 1]
    top = jnp.concatenate([real, -imag], axis=-1)
    bottom = jnp.concatenate([imag, real], axis=-1)
    return jnp.concatenate([top, bottom], axis=-2)


def body(src_value, src_point, src_owner, translation):
    row_x = lax.axis_index("gx")
    row_y = lax.axis_index("gy")
    where = jnp.stack([row_x >> 2, row_y, row_x & 3]).astype(jnp.int32)

    send = route(src_owner.reshape(1, -1), src_point, src_value)
    got = lax.all_to_all(send, ("gx", "gy"), split_axis=0, concat_axis=0, tiled=True)
    mats = block_matrices(translation)
    inner_mats = mats[: 2 * LEVX + 1]
    outer_mats = mats[2 * LEVX + 1 :]
    leaf = leaves(got)
    cores = [(i, i ^ 1) for i in range(lax.axis_size("gy"))]
    tables = phases(where)
    last = where
    got = []
    for mine in inner(leaf, inner_mats, tables):
        other = lax.ppermute(mine, "gy", cores)
        outs = outer(where, mine, other, outer_mats, tables, last)
        last = outs[0]
        got.append(outs[0])
        for shift in range(1, 4):
            pairs = [(i, i // 4 * 4 + (i + shift) % 4) for i in range(lax.axis_size("gx"))]
            got.append(lax.ppermute(outs[shift], "gx", pairs))
    return finish(where, got).reshape(128, 1, 1, 4096)


def solution(mesh):
    return jax.shard_map(
        body,
        mesh=mesh,
        in_specs=(P(None, ("gx", "gy")), P(None, ("gx", "gy")), P(("gx", "gy"), None), P()),
        out_specs=P(None, "gx", "gy", None),
        check_vma=False,
    )
```

```python
import functools
import math

import jax
import jax.numpy as jnp
from jax import lax
from jax.experimental import pallas as pl
from jax.experimental.pallas import tpu as pltpu
from jax.sharding import PartitionSpec as P

QX = 8
R = 64
LEVX = 4
LB = 16
LAT = 16
CAP = 128

F32 = jnp.float32
BF16 = jnp.bfloat16
MODULUS = 61.0
MIB = 1024 * 1024

BLOCK = 256
HALF = 2
RANK_UNROLL = 8
ROUTE_UNROLL = 32


def matmul_nt(lhs, rhs):
    return lax.dot_general(lhs, rhs, (((1,), (1,)), ((), ())), preferred_element_type=F32)


def unit_phase(product):
    rest = product - MODULUS * jnp.floor(product * (1.0 / MODULUS) + 0.5)
    x = rest * (math.pi / MODULUS)
    x2 = x * x
    s = x * (1.0 + x2 * (-1 / 6 + x2 * (1 / 120 + x2 * (-1 / 5040 + x2 * (1 / 362880 + x2 * (-1 / 39916800))))))
    c = 1.0 + x2 * (-1 / 2 + x2 * (1 / 24 + x2 * (-1 / 720 + x2 * (1 / 40320 + x2 * (-1 / 3628800)))))
    return 1.0 - 2.0 * s * s, 2.0 * s * c


def cost(micros):
    return pl.CostEstimate(flops=int(micros * 1.0e9), bytes_accessed=0, transcendentals=0)


def iota(shape, dim):
    return lax.broadcasted_iota(jnp.int32, shape, dim)


def reversed_bits(value, bits):
    out = 0
    for bit in range(bits):
        out |= (value >> bit & 1) << (bits - 1 - bit)
    return out


def nibble_reversed(value):
    return (value & 1) << 3 | (value & 2) << 1 | value >> 1 & 2 | value >> 3 & 1


def one_hot(cells, row):
    return jnp.where(cells == row, jnp.ones((), BF16), jnp.zeros((), BF16))


def rank_sources(own_ref, point_ref, value_ref, rows_ref, charge_ref, tri, accs):
    width = BLOCK
    owners = iota((128, width), 0).astype(F32).astype(BF16)
    before_accs, whole_accs = accs[0::2], accs[1::2]

    pltpu.matmul_push_rhs(tri[...], 0, 0)
    pltpu.matmul_acc_lhs(before_accs[0], jnp.zeros((128, width), BF16), load_staged_rhs=0)
    pltpu.matmul_push_rhs(jnp.ones((width, width), BF16), 0, 1)
    pltpu.matmul_acc_lhs(whole_accs[0], jnp.zeros((128, width), BF16), load_staged_rhs=0)
    start = pltpu.matmul_pop(before_accs[0]) + pltpu.matmul_pop(whole_accs[0])

    def several(step, held):
        spans = [
            pl.ds((step * RANK_UNROLL + u) * width, width) for u in range(RANK_UNROLL)
        ]
        hits = []
        for u, span in enumerate(spans):
            own = own_ref[0:1, span]
            hits.append(one_hot(owners, own.astype(F32).astype(BF16)))
            pltpu.matmul_acc_lhs(before_accs[u], hits[u])
            pltpu.matmul_acc_lhs(whole_accs[u], hits[u])
        for u, span in enumerate(spans):
            own = own_ref[0:1, span]
            px = point_ref[0:1, span]
            py = point_ref[1:2, span]
            rows_ref[2:3, span] = ((own >> 6) * 16 + (own & 15)).astype(F32)
            box = nibble_reversed(px >> 4) * 16 + nibble_reversed(py >> 4)
            rows_ref[3:4, span] = box.astype(F32)
            rows_ref[4:5, span] = ((px & 15) * 16 + (py & 15)).astype(F32)
            big_x = (own >> 4) * (LB * LAT) + px
            big_y = (own & 15) * (LB * LAT) + py
            cosine, sine = unit_phase(big_x.astype(F32) * big_y.astype(F32))
            real = value_ref[0:16, span].astype(F32)
            imag = value_ref[16:32, span].astype(F32)
            turned_real = cosine * real - sine * imag
            turned_imag = sine * real + cosine * imag
            parts = []
            for group in range(4):
                parts.append(turned_real[4 * group : 4 * group + 4])
                parts.append(turned_imag[4 * group : 4 * group + 4])
            charge_ref[:, span] = jnp.concatenate(parts, axis=0).astype(BF16)
        for u, span in enumerate(spans):
            before = pltpu.matmul_pop(before_accs[u]) + held
            held = held + pltpu.matmul_pop(whole_accs[u])
            rank = jnp.sum(hits[u].astype(F32) * before, axis=0, keepdims=True)
            sibling = own_ref[0:1, span] >> 4 & 3
            key = rank + (128 * (sibling & 1)).astype(F32)
            rows_ref[0:1, span] = jnp.where(sibling < 2, key, -1.0)
            rows_ref[1:2, span] = jnp.where(sibling < 2, -1.0, key)
        return held

    held = start
    for step in range(own_ref.shape[1] // width // RANK_UNROLL):
        held = several(step, held)


def place_sources(high, rows_ref, charge_ref, hold, accs):
    blocks = charge_ref.shape[1] // BLOCK
    cells = iota((256, BLOCK), 0).astype(F32).astype(BF16)
    lows = (iota((16, BLOCK), 0) + 16 * high).astype(F32).astype(BF16)
    none = jnp.zeros((), BF16)

    def one(step, carried):
        for u in range(ROUTE_UNROLL):
            span = pl.ds(pl.multiple_of((step * ROUTE_UNROLL + u) * BLOCK, BLOCK), BLOCK)
            row = rows_ref[2:3, span].astype(BF16)
            low = jnp.broadcast_to(row, (32, BLOCK))
            charge = charge_ref[:, span]
            parts = [jnp.where(low == float(high * 16 + n), charge, none) for n in range(16)]
            mine = lows == row
            for kind in range(2):
                parts.append(jnp.where(mine, rows_ref[3 + kind : 4 + kind, span].astype(BF16), none))
            parts = jnp.concatenate(parts, axis=0)
            for side in range(2):
                slots = one_hot(cells, rows_ref[side : side + 1, span].astype(BF16))
                pltpu.matmul_push_rhs(slots, u % 2, side, transpose=True)
                pltpu.matmul_acc_lhs(accs[side], parts, load_staged_rhs=u % 2)
        return carried

    lax.fori_loop(0, blocks // ROUTE_UNROLL, one, 0)
    for side in range(2):
        hold[high, side] = pltpu.matmul_pop(accs[side])


def route_kernel(
    own_hbm, point_hbm, value_hbm, send_hbm, own, point, value, rows, charge, tri, hold, send, sems
):
    copies = [
        pltpu.make_async_copy(source, target, sems.at[number])
        for number, (source, target) in enumerate(
            ((own_hbm, own), (point_hbm, point), (value_hbm, value))
        )
    ]
    for copy in copies:
        copy.start()
    earlier = iota((BLOCK, BLOCK), 0) < iota((BLOCK, BLOCK), 1)
    tri[...] = jnp.where(earlier, 1.0, 0.0).astype(BF16)
    for copy in copies:
        copy.wait()
    pl.run_scoped(
        lambda *accs: rank_sources(own, point, value, rows, charge, tri, accs),
        *[pltpu.ACC(number % 2)((128, 256), F32) for number in range(2 * RANK_UNROLL)],
    )
    halves = []
    for high in range(2):
        pl.run_scoped(
            lambda *accs, high=high: place_sources(high, rows, charge, hold, accs),
            *[pltpu.ACC(number)((544, 256), F32) for number in range(2)],
        )
        for low in range(16):
            first = high * 64 + low
            for group in range(4):
                at = low * 32 + group * 8
                for y in range(4):
                    tile = hold[high, y // 2, at : at + 8, y % 2 * 128 : y % 2 * 128 + 128]
                    send[first + group * 16, y] = tile.astype(BF16)
            tile = [
                hold[high, y // 2, pl.ds(512 + 16 * kind + low, 1), y % 2 * 128 : y % 2 * 128 + 128]
                for kind in range(2)
                for y in range(4)
            ]
            tile = jnp.concatenate(tile, axis=0).astype(BF16)
            for group in range(4):
                send[first + group * 16, 4] = tile
        span = pl.ds(high * 64, 64)
        halves.append(pltpu.make_async_copy(send.at[span], send_hbm.at[span], sems.at[3 + high]))
        halves[high].start()
    for copy in halves:
        copy.wait()


def route(owner, point, value):
    sources = owner.shape[1]
    return pl.pallas_call(
        route_kernel,
        in_specs=[pl.BlockSpec(memory_space=pltpu.HBM)] * 3,
        out_specs=pl.BlockSpec(memory_space=pltpu.HBM),
        out_shape=jax.ShapeDtypeStruct((128, 5, 8, 128), BF16),
        scratch_shapes=[
            pltpu.VMEM((1, sources), jnp.int32),
            pltpu.VMEM((2, sources), jnp.int32),
            pltpu.VMEM((32, sources), BF16),
            pltpu.VMEM((8, sources), F32),
            pltpu.VMEM((32, sources), BF16),
            pltpu.VMEM((BLOCK, BLOCK), BF16),
            pltpu.VMEM((2, 2, 544, 256), F32),
            pltpu.VMEM((128, 5, 8, 128), BF16),
            pltpu.SemaphoreType.DMA((5,)),
        ],
        compiler_params=pltpu.CompilerParams(vmem_limit_bytes=60 * MIB),
        cost_estimate=cost(15),
        name="route",
    )(owner, point, value)


def level_starts(depth):
    return [(high, low) for high in range(2**depth) for low in range(2 ** (LEVX - 1 - depth))]


def phases_kernel(
    where_ref, level_c, level_s, eight_c, eight_s, nine_c, nine_s, ten_c, ten_s
):
    row_high = where_ref[0].astype(F32)
    row_y = where_ref[1]
    sign = signs((8, 128))
    row_x = row_high * 4.0 + (iota((8, 128), 0) // HALF).astype(F32)
    flat_y = jnp.full((8, 128), row_y.astype(F32))
    for depth in range(LEVX):
        below = LEVX - 1 - depth
        for axis in range(2):
            row = (row_x, flat_y)[axis]
            for place, (high, low) in enumerate(level_starts(depth)):
                parent = row * float(2**below) + float(reversed_bits(low, below))
                for t in range(2):
                    cosine, sine = unit_phase(parent * float(2 * high + t))
                    level_c[2 * depth + axis, 2 * place + t] = cosine
                    level_s[2 * depth + axis, 2 * place + t] = sine * sign

    key = iota((16, 8, 128), 0).astype(F32)
    sign = signs((16, 8, 128))
    for pair in range(2):
        for t in range(2):
            cosine, sine = unit_phase((row_high * 2.0 + float(pair)) * (2.0 * key + float(t)))
            eight_c[pair, t] = cosine
            eight_s[pair, t] = sine * sign
            cosine, sine = unit_phase(row_high * (2.0 * (2.0 * key + float(pair)) + float(t)))
            ten_c[pair, t] = cosine
            ten_s[pair, t] = sine * sign

    core = (row_y & 1).astype(F32)
    target = 2.0 * iota((16, 128), 0).astype(F32) + core
    cosine, sine = unit_phase((row_y >> 1).astype(F32) * target)
    nine_c[...] = cosine
    nine_s[...] = sine * signs((16, 128))


def phases(where):
    shapes = [(8, 16, 8, 128), (2, 2, 16, 8, 128), (16, 128), (2, 2, 16, 8, 128)]
    return pl.pallas_call(
        phases_kernel,
        in_specs=[pl.BlockSpec(memory_space=pltpu.SMEM)],
        out_specs=[pl.BlockSpec(memory_space=pltpu.VMEM)] * 8,
        out_shape=[jax.ShapeDtypeStruct(shape, F32) for shape in shapes for _ in range(2)],
        compiler_params=pltpu.CompilerParams(vmem_limit_bytes=40 * MIB),
        cost_estimate=cost(2),
        name="phases",
    )(where)


def nodes_and_scales():
    nodes = [0.5 + 0.5 * math.cos(math.pi * (2 * a + 1) / (2 * QX)) for a in range(QX)]
    scales = []
    for a in range(QX):
        scale = 1.0
        for c in range(QX):
            if c != a:
                scale /= nodes[a] - nodes[c]
        scales.append(scale)
    return nodes, scales


def column(values, shape):
    row = iota(shape, 0)
    out = jnp.full(shape, values[0], F32)
    for index in range(1, len(values)):
        out = jnp.where(row == index, values[index], out)
    return out


def interpolation(position, nodes, scales):
    gap = position - nodes
    one = pltpu.roll(gap, 7, axis=0)
    two = one * pltpu.roll(one, 7, axis=0)
    four = two * pltpu.roll(two, 6, axis=0)
    return scales * four * pltpu.roll(two, 4, axis=0) * pltpu.roll(one, 2, axis=0)


def swapped_parts(matrix):
    blocks = [matrix[row : row + 64] for row in range(0, matrix.shape[0], 64)]
    order = [number ^ 1 for number in range(len(blocks))]
    return jnp.concatenate([blocks[number] for number in order], axis=0)


def signs(shape):
    return jnp.where(iota(shape, len(shape) - 1) < 64, -1.0, 1.0)


def level_matrix(mats_ref, level):
    return jnp.concatenate(
        [
            jnp.concatenate([mats_ref[level, t, 0], mats_ref[level, t, 1]], axis=1)
            for t in range(2)
        ],
        axis=0,
    )


def leaves_kernel(got_ref, out_ref, points):
    points[...] = got_ref[:, 4].astype(F32)
    nodes, scales = nodes_and_scales()
    nodes = column(nodes, (8, 128))
    scales = column(scales, (8, 128))
    cells = iota((256, 128), 0).astype(F32).astype(BF16)

    def operands(source, y):
        charge = got_ref[source, y].astype(F32)
        box = points[source, y : y + 1, :]
        offset = points[source, 4 + y : 5 + y, :]
        coarse = jnp.floor(offset * (1.0 / LAT))
        fine = offset - LAT * coarse
        over_x = interpolation((coarse + 0.5) * (1.0 / LAT), nodes, scales)
        over_y = interpolation((fine + 0.5) * (1.0 / LAT), nodes, scales)
        both = jnp.concatenate([over_x[a : a + 1] * over_y for a in range(QX)], axis=0)
        both = both.astype(BF16)
        rows = []
        for h in range(4):
            for part in range(2):
                at = part * 4 + h
                rows.append(both * charge[at : at + 1].astype(BF16))
        return one_hot(cells, box.astype(BF16)), jnp.concatenate(rows, axis=0)

    def run(*accs):
        for y in range(4):

            for step in range(32):
                for m in range(2):
                    source = step * 4 + m * 2
                    boxes0, spread0 = operands(source, y)
                    boxes1, spread1 = operands(source + 1, y)
                    boxes = jnp.concatenate([boxes0, boxes1], axis=1)
                    spread = jnp.concatenate([spread0, spread1], axis=1)
                    pltpu.matmul_push_rhs(boxes, step % 2, m, transpose=True)
                    pltpu.matmul_acc_lhs(accs[m], spread, load_staged_rhs=step % 2)
            total = pltpu.matmul_pop(accs[0]) + pltpu.matmul_pop(accs[1])
            for h in range(4):
                rows = pl.ds(y * HALF + h % HALF, 256, stride=8)
                out_ref[h // HALF, rows, :] = total[h * 128 : (h + 1) * 128].T

    pl.run_scoped(run, pltpu.ACC(0)((512, 256), F32), pltpu.ACC(1)((512, 256), F32))


def leaves(got):
    vmem = pl.BlockSpec(memory_space=pltpu.VMEM)
    return pl.pallas_call(
        leaves_kernel,
        in_specs=[vmem],
        out_specs=vmem,
        out_shape=jax.ShapeDtypeStruct((2, 2048, 128), F32),
        scratch_shapes=[pltpu.VMEM((128, 8, 128), F32)],
        compiler_params=pltpu.CompilerParams(vmem_limit_bytes=40 * MIB),
        cost_estimate=cost(19),
        name="leaves",
    )(got)


def inner_kernel(leaf_ref, mats_ref, level_c, level_s, eight_c, eight_s, out0, out1, work0, work1):
    tables = (level_c, level_s, eight_c, eight_s)
    works, outs = (work0, work1), (out0, out1)
    stages = [
        (level, half, number)
        for level in range(2 * LEVX + 1)
        for half in range(2)
        for number in range(2)
    ]

    def run(*accs):
        def start(at):
            level, half, number = stages[at]
            work = leaf_ref.at[half] if level == 0 else works[half]
            if level < 2 * LEVX:
                lefts = level_lefts(level, work, number)
            else:
                lefts = eighth_lefts(work, number)
            own = accs[at % 2 * 4 : at % 2 * 4 + 4]
            first = half == 0 and number == 0
            if first:
                right = level_matrix(mats_ref, level)
                pltpu.matmul_push_rhs(right, level % 2, 0, transpose=True)
                pltpu.matmul_push_rhs(swapped_parts(right), level % 2, 1, transpose=True)
            for place, left in enumerate(lefts):
                for m in range(2):
                    if place == 0 or m == at % 2:
                        load = level % 2 if first and place == 0 else None
                        pltpu.matmul_acc_lhs(own[2 * place + m], left, load_staged_rhs=load)

        def finish(at):
            level, half, number = stages[at]
            own = accs[at % 2 * 4 : at % 2 * 4 + 4]
            for place in range(2):
                both = place == 0
                made = pltpu.matmul_pop(own[2 * place]) if both or at % 2 == 0 else None
                other = pltpu.matmul_pop(own[2 * place + 1]) if both or at % 2 == 1 else None
                if level < 2 * LEVX:
                    level_turns(level, tables, works[half], 2 * number + place, made, other)
                else:
                    eighth_turns(tables, outs[half], number, place, made, other)

        start(0)
        start(1)
        for at in range(len(stages)):
            finish(at)
            if at + 2 < len(stages):
                start(at + 2)

    pl.run_scoped(run, *[pltpu.ACC(number % 2)((256, 256), F32) for number in range(8)])


def box_rows(x, y):
    return pl.ds((x * 16 + y) * 8, 8)


def line(work, level, at):
    if level % 2 == 0:
        return work[pl.ds(at * 128, 128), :].astype(BF16)
    return jnp.concatenate([work[box_rows(x, at), :] for x in range(16)], axis=0).astype(BF16)


def level_lefts(level, work, half):
    below = LEVX - 1 - level // 2
    starts = [high << below + 1 | low for high, low in level_starts(level // 2)]
    lefts = []
    for number in range(2 * half, 2 * half + 2):
        first = starts[2 * number : 2 * number + 2]
        ends = [[line(work, level, s | t << below) for s in first] for t in range(2)]
        ends = [jnp.concatenate(end, axis=0) for end in ends]
        lefts.append(jnp.concatenate(ends, axis=1))
    return lefts


def two_forms(made, other, chosen):
    if made is None:
        other = other[chosen]
        return pltpu.roll(other, 64, axis=1), other
    made = made[chosen]
    return made, pltpu.roll(made, 64, axis=1) if other is None else other[chosen]


def level_turns(level, tables, work, number, made, other):
    level_c, level_s = tables[:2]
    below = LEVX - 1 - level // 2
    starts = [high << below + 1 | low for high, low in level_starts(level // 2)]
    for place in range(2):
        at = 2 * number + place
        for t in range(2):
            chosen = (slice(place * 128, place * 128 + 128), slice(t * 128, t * 128 + 128))
            cosine, sine = level_c[level, 2 * at + t], level_s[level, 2 * at + t]
            plain, swapped = two_forms(made, other, chosen)
            piece = plain.reshape(16, 8, 128) * cosine[None]
            piece = piece + swapped.reshape(16, 8, 128) * sine[None]
            end = starts[at] | t << below
            if level % 2 == 0:
                work[pl.ds(end * 128, 128), :] = piece.reshape(128, 128)
            else:
                for x in range(16):
                    work[box_rows(x, end), :] = piece[x]


def eighth_lefts(work, pair):
    lefts = []
    for h in range(HALF):
        both = [
            work[pl.ds((2 * pair + c) * HALF + h, 256, stride=8), :].astype(BF16) for c in range(2)
        ]
        lefts.append(jnp.concatenate(both, axis=1))
    return lefts


def eighth_turns(tables, out_ref, pair, h, made, other):
    eight_c, eight_s = tables[2:]
    for t in range(2):
        chosen = (slice(None), slice(t * 128, t * 128 + 128))
        plain, swapped = two_forms(made, other, chosen)
        piece = plain.reshape(16, 2, 8, 128) * eight_c[pair, t][:, None]
        piece = piece + swapped.reshape(16, 2, 8, 128) * eight_s[pair, t][:, None]
        out_ref[pair, t, h] = piece.reshape(256, 128).astype(BF16)


def inner(leaf, mats, tables):
    vmem = pl.BlockSpec(memory_space=pltpu.VMEM)
    return pl.pallas_call(
        inner_kernel,
        in_specs=[vmem] * 6,
        out_specs=[vmem] * 2,
        out_shape=[jax.ShapeDtypeStruct((2, 2, HALF, 256, 128), BF16)] * 2,
        scratch_shapes=[pltpu.VMEM((2048, 128), F32)] * 2,
        compiler_params=pltpu.CompilerParams(vmem_limit_bytes=40 * MIB),
        cost_estimate=cost(5),
        name="inner",
    )(leaf, mats, *tables[:4])


def outer_kernel(
    where_ref, mine_ref, other_ref, mats_ref, nine_c, nine_s, ten_c, ten_s, after_ref, *refs
):
    del after_ref
    outs, held = refs[:4], refs[4]
    row_y = where_ref[1]
    own = where_ref[2]
    core = row_y & 1
    table = (nine_c[...][None], nine_s[...][None])
    mats_y = jnp.concatenate([mats_ref[0, core, core], mats_ref[0, core, 1 - core]], axis=1)
    mats_y = jnp.concatenate([mats_y, swapped_parts(mats_y)], axis=0)
    mats_x = level_matrix(mats_ref, 1)
    mats_x = jnp.concatenate([mats_x, swapped_parts(mats_x)], axis=0)
    for t8 in range(2):
        tables = [(ten_c[t8, t][:, None], ten_s[t8, t][:, None]) for t in range(2)]
        for h in range(HALF):
            both = []
            for c in range(2):
                pair = jnp.concatenate([mine_ref[c, t8, h], other_ref[c, t8, h]], axis=1)
                made = matmul_nt(pair, mats_y)
                piece = made[:, :128].reshape(16, 16, 128) * table[0]
                piece = piece + made[:, 128:].reshape(16, 16, 128) * table[1]
                both.append(piece.reshape(256, 128).astype(BF16))
            made = matmul_nt(jnp.concatenate(both, axis=1), mats_x)
            for t in range(2):
                plain = made[:, t * 128 : t * 128 + 128].reshape(16, 2, 8, 128)
                other = made[:, t * 128 + 256 : t * 128 + 384].reshape(16, 2, 8, 128)
                piece = plain * tables[t][0] + other * tables[t][1]
                held[2 * t + t8, h] = piece.reshape(256, 128).astype(BF16)
    for shift in range(4):
        outs[shift][...] = held[(own + shift) & 3]


def outer(where, mine, other, mats, tables, after):
    vmem = pl.BlockSpec(memory_space=pltpu.VMEM)
    return pl.pallas_call(
        outer_kernel,
        in_specs=[pl.BlockSpec(memory_space=pltpu.SMEM)]
        + [vmem] * 7
        + [pl.BlockSpec(memory_space=pl.ANY)],
        out_specs=[vmem] * 4,
        out_shape=[jax.ShapeDtypeStruct((HALF, 256, 128), BF16)] * 4,
        scratch_shapes=[pltpu.VMEM((4, HALF, 256, 128), BF16)],
        compiler_params=pltpu.CompilerParams(vmem_limit_bytes=40 * MIB),
        cost_estimate=cost(3),
        name="outer",
    )(where, mine, other, mats, *tables[4:], after)


def finish_kernel(where_ref, *refs):
    got, out_ref, held, sems = refs[:8], *refs[8:]
    own = where_ref[2]
    row = iota((256, 256), 1)
    place = row >> 4
    group = (own - (place >> 1)) & 3
    target = (row & 15) * 16 + group * 4 + (place >> 3) * HALF + (place & 1)
    order = jnp.where(iota((256, 256), 0) == target, 1.0, 0.0).astype(BF16)

    def run(*accs):
        for number, acc in enumerate(accs):
            blocks = []
            for block in (2 * number, 2 * number + 1):
                span = slice(block * 16, block * 16 + 16)
                pieces = [got[at // 2][at % 2, span] for at in range(16)]
                blocks.append(jnp.concatenate(pieces, axis=0))
            m, register = number % 2, number // 2 % 2
            pltpu.matmul_push_rhs(jnp.concatenate(blocks, axis=1), register, m)
            pltpu.matmul_acc_lhs(acc, order, load_staged_rhs=register)
        for number, acc in enumerate(accs):
            made = pltpu.matmul_pop(acc).astype(BF16)
            for side in range(2):
                start = (2 * number + side) * 256
                held[:, start : start + 256] = made[:, side * 128 : side * 128 + 128].T
            if number % 2 == 1:
                copies[number // 2].start()

    copies = []
    for number in range(4):
        span = pl.ds(number * 1024, 1024)
        copies.append(
            pltpu.make_async_copy(held.at[:, span], out_ref.at[:, span], sems.at[number])
        )
    pl.run_scoped(run, *[pltpu.ACC(number % 2)((256, 256), F32) for number in range(8)])
    for copy in copies:
        copy.wait()


def finish(where, got):
    vmem = pl.BlockSpec(memory_space=pltpu.VMEM)
    return pl.pallas_call(
        finish_kernel,
        in_specs=[pl.BlockSpec(memory_space=pltpu.SMEM)] + [vmem] * 8,
        out_specs=pl.BlockSpec(memory_space=pltpu.HBM),
        out_shape=jax.ShapeDtypeStruct((128, 4096), BF16),
        scratch_shapes=[pltpu.VMEM((128, 4096), BF16), pltpu.SemaphoreType.DMA((4,))],
        compiler_params=pltpu.CompilerParams(vmem_limit_bytes=40 * MIB),
        cost_estimate=cost(3),
        name="finish",
    )(where, *got)


def block_matrices(translation):
    parts = translation.reshape(-1, 2, 2, 2, R, R)
    real = parts[:, :, :, 0]
    imag = parts[:, :, :, 1]
    top = jnp.concatenate([real, -imag], axis=-1)
    bottom = jnp.concatenate([imag, real], axis=-1)
    return jnp.concatenate([top, bottom], axis=-2)


def body(src_value, src_point, src_owner, translation):
    row_x = lax.axis_index("gx")
    row_y = lax.axis_index("gy")
    where = jnp.stack([row_x >> 2, row_y, row_x & 3]).astype(jnp.int32)

    send = route(src_owner.reshape(1, -1), src_point, src_value)
    got = lax.all_to_all(send, ("gx", "gy"), split_axis=0, concat_axis=0, tiled=True)
    mats = block_matrices(translation)
    inner_mats = mats[: 2 * LEVX + 1]
    outer_mats = mats[2 * LEVX + 1 :]
    leaf = leaves(got)
    cores = [(i, i ^ 1) for i in range(lax.axis_size("gy"))]
    tables = phases(where)
    last = where
    got = []
    for mine in inner(leaf, inner_mats, tables):
        other = lax.ppermute(mine, "gy", cores)
        outs = outer(where, mine, other, outer_mats, tables, last)
        last = outs[0]
        arrived = {0: outs[0]}
        for shift in (2, 1, 3):
            pairs = [(i, i // 4 * 4 + (i + shift) % 4) for i in range(lax.axis_size("gx"))]
            arrived[shift] = lax.ppermute(outs[shift], "gx", pairs)
        got += [arrived[shift] for shift in range(4)]
    return finish(where, got).reshape(128, 1, 1, 4096)


def solution(mesh):
    return jax.shard_map(
        body,
        mesh=mesh,
        in_specs=(P(None, ("gx", "gy")), P(None, ("gx", "gy")), P(("gx", "gy"), None), P()),
        out_specs=P(None, "gx", "gy", None),
        check_vma=False,
    )
```

```python
import functools
import math

import jax
import jax.numpy as jnp
from jax import lax
from jax.experimental import pallas as pl
from jax.experimental.pallas import tpu as pltpu
from jax.sharding import PartitionSpec as P

QX = 8
R = 64
LEVX = 4
LB = 16
LAT = 16
CAP = 128

F32 = jnp.float32
BF16 = jnp.bfloat16
MODULUS = 61.0
MIB = 1024 * 1024

BLOCK = 256
HALF = 2
RANK_UNROLL = 8
ROUTE_UNROLL = 32


def matmul_nt(lhs, rhs):
    return lax.dot_general(lhs, rhs, (((1,), (1,)), ((), ())), preferred_element_type=F32)


def unit_phase(product):
    rest = product - MODULUS * jnp.floor(product * (1.0 / MODULUS) + 0.5)
    x = rest * (math.pi / MODULUS)
    x2 = x * x
    s = x * (1.0 + x2 * (-1 / 6 + x2 * (1 / 120 + x2 * (-1 / 5040 + x2 * (1 / 362880 + x2 * (-1 / 39916800))))))
    c = 1.0 + x2 * (-1 / 2 + x2 * (1 / 24 + x2 * (-1 / 720 + x2 * (1 / 40320 + x2 * (-1 / 3628800)))))
    return 1.0 - 2.0 * s * s, 2.0 * s * c


def cost(micros):
    return pl.CostEstimate(flops=int(micros * 1.0e9), bytes_accessed=0, transcendentals=0)


def iota(shape, dim):
    return lax.broadcasted_iota(jnp.int32, shape, dim)


def reversed_bits(value, bits):
    out = 0
    for bit in range(bits):
        out |= (value >> bit & 1) << (bits - 1 - bit)
    return out


def nibble_reversed(value):
    return (value & 1) << 3 | (value & 2) << 1 | value >> 1 & 2 | value >> 3 & 1


def one_hot(cells, row):
    return jnp.where(cells == row, jnp.ones((), BF16), jnp.zeros((), BF16))


def rank_sources(own_ref, point_ref, value_ref, rows_ref, charge_ref, tri, accs):
    width = BLOCK
    owners = iota((128, width), 0).astype(F32).astype(BF16)
    before_accs, whole_accs = accs[0::2], accs[1::2]

    pltpu.matmul_push_rhs(tri[...], 0, 0)
    pltpu.matmul_acc_lhs(before_accs[0], jnp.zeros((128, width), BF16), load_staged_rhs=0)
    pltpu.matmul_push_rhs(jnp.ones((width, width), BF16), 0, 1)
    pltpu.matmul_acc_lhs(whole_accs[0], jnp.zeros((128, width), BF16), load_staged_rhs=0)
    start = pltpu.matmul_pop(before_accs[0]) + pltpu.matmul_pop(whole_accs[0])

    def several(step, held):
        spans = [
            pl.ds((step * RANK_UNROLL + u) * width, width) for u in range(RANK_UNROLL)
        ]
        hits = []
        for u, span in enumerate(spans):
            own = own_ref[0:1, span]
            hits.append(one_hot(owners, own.astype(F32).astype(BF16)))
            pltpu.matmul_acc_lhs(before_accs[u], hits[u])
            pltpu.matmul_acc_lhs(whole_accs[u], hits[u])
        for u, span in enumerate(spans):
            own = own_ref[0:1, span]
            px = point_ref[0:1, span]
            py = point_ref[1:2, span]
            rows_ref[2:3, span] = ((own >> 6) * 16 + (own & 15)).astype(F32)
            box = nibble_reversed(px >> 4) * 16 + nibble_reversed(py >> 4)
            rows_ref[3:4, span] = box.astype(F32)
            rows_ref[4:5, span] = ((px & 15) * 16 + (py & 15)).astype(F32)
            big_x = (own >> 4) * (LB * LAT) + px
            big_y = (own & 15) * (LB * LAT) + py
            cosine, sine = unit_phase(big_x.astype(F32) * big_y.astype(F32))
            real = value_ref[0:16, span].astype(F32)
            imag = value_ref[16:32, span].astype(F32)
            turned_real = cosine * real - sine * imag
            turned_imag = sine * real + cosine * imag
            parts = []
            for group in range(4):
                parts.append(turned_real[4 * group : 4 * group + 4])
                parts.append(turned_imag[4 * group : 4 * group + 4])
            charge_ref[:, span] = jnp.concatenate(parts, axis=0).astype(BF16)
        for u, span in enumerate(spans):
            before = pltpu.matmul_pop(before_accs[u]) + held
            held = held + pltpu.matmul_pop(whole_accs[u])
            rank = jnp.sum(hits[u].astype(F32) * before, axis=0, keepdims=True)
            sibling = own_ref[0:1, span] >> 4 & 3
            key = rank + (128 * (sibling & 1)).astype(F32)
            rows_ref[0:1, span] = jnp.where(sibling < 2, key, -1.0)
            rows_ref[1:2, span] = jnp.where(sibling < 2, -1.0, key)
        return held

    held = start
    for step in range(own_ref.shape[1] // width // RANK_UNROLL):
        held = several(step, held)


def place_sources(high, rows_ref, charge_ref, hold, accs):
    blocks = charge_ref.shape[1] // BLOCK
    cells = iota((256, BLOCK), 0).astype(F32).astype(BF16)
    lows = (iota((16, BLOCK), 0) + 16 * high).astype(F32).astype(BF16)
    none = jnp.zeros((), BF16)

    def one(step, carried):
        for u in range(ROUTE_UNROLL):
            span = pl.ds(pl.multiple_of((step * ROUTE_UNROLL + u) * BLOCK, BLOCK), BLOCK)
            row = rows_ref[2:3, span].astype(BF16)
            low = jnp.broadcast_to(row, (32, BLOCK))
            charge = charge_ref[:, span]
            parts = [jnp.where(low == float(high * 16 + n), charge, none) for n in range(16)]
            mine = lows == row
            for kind in range(2):
                parts.append(jnp.where(mine, rows_ref[3 + kind : 4 + kind, span].astype(BF16), none))
            parts = jnp.concatenate(parts, axis=0)
            for side in range(2):
                slots = one_hot(cells, rows_ref[side : side + 1, span].astype(BF16))
                pltpu.matmul_push_rhs(slots, u % 2, side, transpose=True)
                pltpu.matmul_acc_lhs(accs[side], parts, load_staged_rhs=u % 2)
        return carried

    lax.fori_loop(0, blocks // ROUTE_UNROLL, one, 0)
    for side in range(2):
        hold[high, side] = pltpu.matmul_pop(accs[side])


def route_kernel(
    own_hbm, point_hbm, value_hbm, send_hbm, own, point, value, rows, charge, tri, hold, send, sems
):
    copies = [
        pltpu.make_async_copy(source, target, sems.at[number])
        for number, (source, target) in enumerate(
            ((own_hbm, own), (point_hbm, point), (value_hbm, value))
        )
    ]
    for copy in copies:
        copy.start()
    earlier = iota((BLOCK, BLOCK), 0) < iota((BLOCK, BLOCK), 1)
    tri[...] = jnp.where(earlier, 1.0, 0.0).astype(BF16)
    for copy in copies:
        copy.wait()
    pl.run_scoped(
        lambda *accs: rank_sources(own, point, value, rows, charge, tri, accs),
        *[pltpu.ACC(number % 2)((128, 256), F32) for number in range(2 * RANK_UNROLL)],
    )
    halves = []
    for high in range(2):
        pl.run_scoped(
            lambda *accs, high=high: place_sources(high, rows, charge, hold, accs),
            *[pltpu.ACC(number)((544, 256), F32) for number in range(2)],
        )
        for low in range(16):
            first = high * 64 + low
            for group in range(4):
                at = low * 32 + group * 8
                for y in range(4):
                    tile = hold[high, y // 2, at : at + 8, y % 2 * 128 : y % 2 * 128 + 128]
                    send[first + group * 16, y] = tile.astype(BF16)
            tile = [
                hold[high, y // 2, pl.ds(512 + 16 * kind + low, 1), y % 2 * 128 : y % 2 * 128 + 128]
                for kind in range(2)
                for y in range(4)
            ]
            tile = jnp.concatenate(tile, axis=0).astype(BF16)
            for group in range(4):
                send[first + group * 16, 4] = tile
        span = pl.ds(high * 64, 64)
        halves.append(pltpu.make_async_copy(send.at[span], send_hbm.at[span], sems.at[3 + high]))
        halves[high].start()
    for copy in halves:
        copy.wait()


def route(owner, point, value):
    sources = owner.shape[1]
    return pl.pallas_call(
        route_kernel,
        in_specs=[pl.BlockSpec(memory_space=pltpu.HBM)] * 3,
        out_specs=pl.BlockSpec(memory_space=pltpu.HBM),
        out_shape=jax.ShapeDtypeStruct((128, 5, 8, 128), BF16),
        scratch_shapes=[
            pltpu.VMEM((1, sources), jnp.int32),
            pltpu.VMEM((2, sources), jnp.int32),
            pltpu.VMEM((32, sources), BF16),
            pltpu.VMEM((8, sources), F32),
            pltpu.VMEM((32, sources), BF16),
            pltpu.VMEM((BLOCK, BLOCK), BF16),
            pltpu.VMEM((2, 2, 544, 256), F32),
            pltpu.VMEM((128, 5, 8, 128), BF16),
            pltpu.SemaphoreType.DMA((5,)),
        ],
        compiler_params=pltpu.CompilerParams(vmem_limit_bytes=60 * MIB),
        cost_estimate=cost(15),
        name="route",
    )(owner, point, value)


def level_starts(depth):
    return [(high, low) for high in range(2**depth) for low in range(2 ** (LEVX - 1 - depth))]


def phases_kernel(
    where_ref, level_c, level_s, eight_c, eight_s, nine_c, nine_s, ten_c, ten_s
):
    row_high = where_ref[0].astype(F32)
    row_y = where_ref[1]
    sign = signs((8, 128))
    row_x = row_high * 4.0 + (iota((8, 128), 0) // HALF).astype(F32)
    flat_y = jnp.full((8, 128), row_y.astype(F32))
    for depth in range(LEVX):
        below = LEVX - 1 - depth
        for axis in range(2):
            row = (row_x, flat_y)[axis]
            for place, (high, low) in enumerate(level_starts(depth)):
                parent = row * float(2**below) + float(reversed_bits(low, below))
                for t in range(2):
                    cosine, sine = unit_phase(parent * float(2 * high + t))
                    level_c[2 * depth + axis, 2 * place + t] = cosine
                    level_s[2 * depth + axis, 2 * place + t] = sine * sign

    key = iota((16, 8, 128), 0).astype(F32)
    sign = signs((16, 8, 128))
    for pair in range(2):
        for t in range(2):
            cosine, sine = unit_phase((row_high * 2.0 + float(pair)) * (2.0 * key + float(t)))
            eight_c[pair, t] = cosine
            eight_s[pair, t] = sine * sign
            cosine, sine = unit_phase(row_high * (2.0 * (2.0 * key + float(pair)) + float(t)))
            ten_c[pair, t] = cosine
            ten_s[pair, t] = sine * sign

    core = (row_y & 1).astype(F32)
    target = 2.0 * iota((16, 128), 0).astype(F32) + core
    cosine, sine = unit_phase((row_y >> 1).astype(F32) * target)
    nine_c[...] = cosine
    nine_s[...] = sine * signs((16, 128))


def phases(where):
    shapes = [(8, 16, 8, 128), (2, 2, 16, 8, 128), (16, 128), (2, 2, 16, 8, 128)]
    return pl.pallas_call(
        phases_kernel,
        in_specs=[pl.BlockSpec(memory_space=pltpu.SMEM)],
        out_specs=[pl.BlockSpec(memory_space=pltpu.VMEM)] * 8,
        out_shape=[jax.ShapeDtypeStruct(shape, F32) for shape in shapes for _ in range(2)],
        compiler_params=pltpu.CompilerParams(vmem_limit_bytes=40 * MIB),
        cost_estimate=cost(2),
        name="phases",
    )(where)


def nodes_and_scales():
    nodes = [0.5 + 0.5 * math.cos(math.pi * (2 * a + 1) / (2 * QX)) for a in range(QX)]
    scales = []
    for a in range(QX):
        scale = 1.0
        for c in range(QX):
            if c != a:
                scale /= nodes[a] - nodes[c]
        scales.append(scale)
    return nodes, scales


def column(values, shape):
    row = iota(shape, 0)
    out = jnp.full(shape, values[0], F32)
    for index in range(1, len(values)):
        out = jnp.where(row == index, values[index], out)
    return out


def interpolation(position, nodes, scales):
    gap = position - nodes
    one = pltpu.roll(gap, 7, axis=0)
    two = one * pltpu.roll(one, 7, axis=0)
    four = two * pltpu.roll(two, 6, axis=0)
    return scales * four * pltpu.roll(two, 4, axis=0) * pltpu.roll(one, 2, axis=0)


def swapped_parts(matrix):
    blocks = [matrix[row : row + 64] for row in range(0, matrix.shape[0], 64)]
    order = [number ^ 1 for number in range(len(blocks))]
    return jnp.concatenate([blocks[number] for number in order], axis=0)


def signs(shape):
    return jnp.where(iota(shape, len(shape) - 1) < 64, -1.0, 1.0)


def level_matrix(mats_ref, level):
    return jnp.concatenate(
        [
            jnp.concatenate([mats_ref[level, t, 0], mats_ref[level, t, 1]], axis=1)
            for t in range(2)
        ],
        axis=0,
    )


def leaves_kernel(got_ref, out_ref, points):
    points[...] = got_ref[:, 4].astype(F32)
    nodes, scales = nodes_and_scales()
    nodes = column(nodes, (8, 128))
    scales = column(scales, (8, 128))
    cells = iota((256, 128), 0).astype(F32).astype(BF16)

    def operands(source, y):
        charge = got_ref[source, y].astype(F32)
        box = points[source, y : y + 1, :]
        offset = points[source, 4 + y : 5 + y, :]
        coarse = jnp.floor(offset * (1.0 / LAT))
        fine = offset - LAT * coarse
        over_x = interpolation((coarse + 0.5) * (1.0 / LAT), nodes, scales)
        over_y = interpolation((fine + 0.5) * (1.0 / LAT), nodes, scales)
        both = jnp.concatenate([over_x[a : a + 1] * over_y for a in range(QX)], axis=0)
        both = both.astype(BF16)
        rows = []
        for h in range(4):
            for part in range(2):
                at = part * 4 + h
                rows.append(both * charge[at : at + 1].astype(BF16))
        return one_hot(cells, box.astype(BF16)), jnp.concatenate(rows, axis=0)

    def run(*accs):
        for y in range(4):

            for step in range(32):
                for m in range(2):
                    source = step * 4 + m * 2
                    boxes0, spread0 = operands(source, y)
                    boxes1, spread1 = operands(source + 1, y)
                    boxes = jnp.concatenate([boxes0, boxes1], axis=1)
                    spread = jnp.concatenate([spread0, spread1], axis=1)
                    pltpu.matmul_push_rhs(boxes, step % 2, m, transpose=True)
                    pltpu.matmul_acc_lhs(accs[m], spread, load_staged_rhs=step % 2)
            total = pltpu.matmul_pop(accs[0]) + pltpu.matmul_pop(accs[1])
            for h in range(4):
                rows = pl.ds(y * HALF + h % HALF, 256, stride=8)
                out_ref[h // HALF, rows, :] = total[h * 128 : (h + 1) * 128].T

    pl.run_scoped(run, pltpu.ACC(0)((512, 256), F32), pltpu.ACC(1)((512, 256), F32))


def leaves(got):
    vmem = pl.BlockSpec(memory_space=pltpu.VMEM)
    return pl.pallas_call(
        leaves_kernel,
        in_specs=[vmem],
        out_specs=vmem,
        out_shape=jax.ShapeDtypeStruct((2, 2048, 128), F32),
        scratch_shapes=[pltpu.VMEM((128, 8, 128), F32)],
        compiler_params=pltpu.CompilerParams(vmem_limit_bytes=40 * MIB),
        cost_estimate=cost(19),
        name="leaves",
    )(got)


def inner_kernel(leaf_ref, mats_ref, level_c, level_s, eight_c, eight_s, out0, out1, work0, work1):
    tables = (level_c, level_s, eight_c, eight_s)
    works, outs = (work0, work1), (out0, out1)
    stages = [
        (level, half, number)
        for level in range(2 * LEVX + 1)
        for half in range(2)
        for number in range(2)
    ]

    def run(*accs):
        def start(at):
            level, half, number = stages[at]
            work = leaf_ref.at[half] if level == 0 else works[half]
            if level < 2 * LEVX:
                lefts = level_lefts(level, work, number)
            else:
                lefts = eighth_lefts(work, number)
            own = accs[at % 2 * 4 : at % 2 * 4 + 4]
            first = half == 0 and number == 0
            if first:
                right = level_matrix(mats_ref, level)
                pltpu.matmul_push_rhs(right, level % 2, 0, transpose=True)
                pltpu.matmul_push_rhs(swapped_parts(right), level % 2, 1, transpose=True)
            for place, left in enumerate(lefts):
                for m in range(2):
                    if place == 0 or m == at % 2:
                        load = level % 2 if first and place == 0 else None
                        pltpu.matmul_acc_lhs(own[2 * place + m], left, load_staged_rhs=load)

        def finish(at):
            level, half, number = stages[at]
            own = accs[at % 2 * 4 : at % 2 * 4 + 4]
            for place in range(2):
                both = place == 0
                made = pltpu.matmul_pop(own[2 * place]) if both or at % 2 == 0 else None
                other = pltpu.matmul_pop(own[2 * place + 1]) if both or at % 2 == 1 else None
                if level < 2 * LEVX:
                    level_turns(level, tables, works[half], 2 * number + place, made, other)
                else:
                    eighth_turns(tables, outs[half], number, place, made, other)

        start(0)
        start(1)
        for at in range(len(stages)):
            finish(at)
            if at + 2 < len(stages):
                start(at + 2)

    pl.run_scoped(run, *[pltpu.ACC(number % 2)((256, 256), F32) for number in range(8)])


def box_rows(x, y):
    return pl.ds((x * 16 + y) * 8, 8)


def line(work, level, at):
    if level % 2 == 0:
        return work[pl.ds(at * 128, 128), :].astype(BF16)
    return jnp.concatenate([work[box_rows(x, at), :] for x in range(16)], axis=0).astype(BF16)


def level_lefts(level, work, half):
    below = LEVX - 1 - level // 2
    starts = [high << below + 1 | low for high, low in level_starts(level // 2)]
    lefts = []
    for number in range(2 * half, 2 * half + 2):
        first = starts[2 * number : 2 * number + 2]
        ends = [[line(work, level, s | t << below) for s in first] for t in range(2)]
        ends = [jnp.concatenate(end, axis=0) for end in ends]
        lefts.append(jnp.concatenate(ends, axis=1))
    return lefts


def two_forms(made, other, chosen):
    if made is None:
        other = other[chosen]
        return pltpu.roll(other, 64, axis=1), other
    made = made[chosen]
    return made, pltpu.roll(made, 64, axis=1) if other is None else other[chosen]


def level_turns(level, tables, work, number, made, other):
    level_c, level_s = tables[:2]
    below = LEVX - 1 - level // 2
    starts = [high << below + 1 | low for high, low in level_starts(level // 2)]
    for place in range(2):
        at = 2 * number + place
        for t in range(2):
            chosen = (slice(place * 128, place * 128 + 128), slice(t * 128, t * 128 + 128))
            cosine, sine = level_c[level, 2 * at + t], level_s[level, 2 * at + t]
            plain, swapped = two_forms(made, other, chosen)
            piece = plain.reshape(16, 8, 128) * cosine[None]
            piece = piece + swapped.reshape(16, 8, 128) * sine[None]
            end = starts[at] | t << below
            if level % 2 == 0:
                work[pl.ds(end * 128, 128), :] = piece.reshape(128, 128)
            else:
                for x in range(16):
                    work[box_rows(x, end), :] = piece[x]


def eighth_lefts(work, pair):
    lefts = []
    for h in range(HALF):
        both = [
            work[pl.ds((2 * pair + c) * HALF + h, 256, stride=8), :].astype(BF16) for c in range(2)
        ]
        lefts.append(jnp.concatenate(both, axis=1))
    return lefts


def eighth_turns(tables, out_ref, pair, h, made, other):
    eight_c, eight_s = tables[2:]
    for t in range(2):
        chosen = (slice(None), slice(t * 128, t * 128 + 128))
        plain, swapped = two_forms(made, other, chosen)
        piece = plain.reshape(16, 2, 8, 128) * eight_c[pair, t][:, None]
        piece = piece + swapped.reshape(16, 2, 8, 128) * eight_s[pair, t][:, None]
        out_ref[pair, t, h] = piece.reshape(256, 128).astype(BF16)


def inner(leaf, mats, tables):
    vmem = pl.BlockSpec(memory_space=pltpu.VMEM)
    return pl.pallas_call(
        inner_kernel,
        in_specs=[vmem] * 6,
        out_specs=[vmem] * 2,
        out_shape=[jax.ShapeDtypeStruct((2, 2, HALF, 256, 128), BF16)] * 2,
        scratch_shapes=[pltpu.VMEM((2048, 128), F32)] * 2,
        compiler_params=pltpu.CompilerParams(vmem_limit_bytes=40 * MIB),
        cost_estimate=cost(5),
        name="inner",
    )(leaf, mats, *tables[:4])


def outer_kernel(
    where_ref, mine_ref, other_ref, mats_ref, nine_c, nine_s, ten_c, ten_s, after_ref, *refs
):
    del after_ref
    outs, held = refs[:4], refs[4]
    row_y = where_ref[1]
    own = where_ref[2]
    core = row_y & 1
    table = (nine_c[...][None], nine_s[...][None])
    mats_y = jnp.concatenate([mats_ref[0, core, core], mats_ref[0, core, 1 - core]], axis=1)
    mats_y = jnp.concatenate([mats_y, swapped_parts(mats_y)], axis=0)
    mats_x = level_matrix(mats_ref, 1)
    mats_x = jnp.concatenate([mats_x, swapped_parts(mats_x)], axis=0)
    for t8 in range(2):
        tables = [(ten_c[t8, t][:, None], ten_s[t8, t][:, None]) for t in range(2)]
        for h in range(HALF):
            both = []
            for c in range(2):
                pair = jnp.concatenate([mine_ref[c, t8, h], other_ref[c, t8, h]], axis=1)
                made = matmul_nt(pair, mats_y)
                piece = made[:, :128].reshape(16, 16, 128) * table[0]
                piece = piece + made[:, 128:].reshape(16, 16, 128) * table[1]
                both.append(piece.reshape(256, 128).astype(BF16))
            made = matmul_nt(jnp.concatenate(both, axis=1), mats_x)
            for t in range(2):
                plain = made[:, t * 128 : t * 128 + 128].reshape(16, 2, 8, 128)
                other = made[:, t * 128 + 256 : t * 128 + 384].reshape(16, 2, 8, 128)
                piece = plain * tables[t][0] + other * tables[t][1]
                held[2 * t + t8, h] = piece.reshape(256, 128).astype(BF16)
    for shift in range(4):
        outs[shift][...] = held[(own + shift) & 3]


def outer(where, mine, other, mats, tables, after):
    vmem = pl.BlockSpec(memory_space=pltpu.VMEM)
    return pl.pallas_call(
        outer_kernel,
        in_specs=[pl.BlockSpec(memory_space=pltpu.SMEM)]
        + [vmem] * 7
        + [pl.BlockSpec(memory_space=pl.ANY)],
        out_specs=[vmem] * 4,
        out_shape=[jax.ShapeDtypeStruct((HALF, 256, 128), BF16)] * 4,
        scratch_shapes=[pltpu.VMEM((4, HALF, 256, 128), BF16)],
        compiler_params=pltpu.CompilerParams(vmem_limit_bytes=40 * MIB),
        cost_estimate=cost(3),
        name="outer",
    )(where, mine, other, mats, *tables[4:], after)


def finish_kernel(where_ref, *refs):
    got, out_ref, held, sems = refs[:8], *refs[8:]
    own = where_ref[2]
    row = iota((256, 256), 1)
    place = row >> 4
    group = (own - (place >> 1)) & 3
    target = (row & 15) * 16 + group * 4 + (place >> 3) * HALF + (place & 1)
    order = jnp.where(iota((256, 256), 0) == target, 1.0, 0.0).astype(BF16)

    def run(*accs):
        for number, acc in enumerate(accs):
            blocks = []
            for block in (2 * number, 2 * number + 1):
                span = slice(block * 16, block * 16 + 16)
                pieces = [got[at // 2][at % 2, span] for at in range(16)]
                blocks.append(jnp.concatenate(pieces, axis=0))
            m, register = number % 2, number // 2 % 2
            pltpu.matmul_push_rhs(jnp.concatenate(blocks, axis=1), register, m)
            pltpu.matmul_acc_lhs(acc, order, load_staged_rhs=register)
        for number, acc in enumerate(accs):
            made = pltpu.matmul_pop(acc).astype(BF16)
            for side in range(2):
                start = (2 * number + side) * 256
                held[:, start : start + 256] = made[:, side * 128 : side * 128 + 128].T
            copies[number].start()

    copies = []
    for number in range(8):
        span = pl.ds(number * 512, 512)
        copies.append(
            pltpu.make_async_copy(held.at[:, span], out_ref.at[:, span], sems.at[number])
        )
    pl.run_scoped(run, *[pltpu.ACC(number % 2)((256, 256), F32) for number in range(8)])
    for copy in copies:
        copy.wait()


def finish(where, got):
    vmem = pl.BlockSpec(memory_space=pltpu.VMEM)
    return pl.pallas_call(
        finish_kernel,
        in_specs=[pl.BlockSpec(memory_space=pltpu.SMEM)] + [vmem] * 8,
        out_specs=pl.BlockSpec(memory_space=pltpu.HBM),
        out_shape=jax.ShapeDtypeStruct((128, 4096), BF16),
        scratch_shapes=[pltpu.VMEM((128, 4096), BF16), pltpu.SemaphoreType.DMA((8,))],
        compiler_params=pltpu.CompilerParams(vmem_limit_bytes=40 * MIB),
        cost_estimate=cost(3),
        name="finish",
    )(where, *got)


def block_matrices(translation):
    parts = translation.reshape(-1, 2, 2, 2, R, R)
    real = parts[:, :, :, 0]
    imag = parts[:, :, :, 1]
    top = jnp.concatenate([real, -imag], axis=-1)
    bottom = jnp.concatenate([imag, real], axis=-1)
    return jnp.concatenate([top, bottom], axis=-2)


def body(src_value, src_point, src_owner, translation):
    row_x = lax.axis_index("gx")
    row_y = lax.axis_index("gy")
    where = jnp.stack([row_x >> 2, row_y, row_x & 3]).astype(jnp.int32)

    send = route(src_owner.reshape(1, -1), src_point, src_value)
    got = lax.all_to_all(send, ("gx", "gy"), split_axis=0, concat_axis=0, tiled=True)
    mats = block_matrices(translation)
    inner_mats = mats[: 2 * LEVX + 1]
    outer_mats = mats[2 * LEVX + 1 :]
    leaf = leaves(got)
    cores = [(i, i ^ 1) for i in range(lax.axis_size("gy"))]
    tables = phases(where)
    last = where
    got = []
    for mine in inner(leaf, inner_mats, tables):
        other = lax.ppermute(mine, "gy", cores)
        outs = outer(where, mine, other, outer_mats, tables, last)
        last = outs[0]
        arrived = {0: outs[0]}
        for shift in (2, 1, 3):
            pairs = [(i, i // 4 * 4 + (i + shift) % 4) for i in range(lax.axis_size("gx"))]
            arrived[shift] = lax.ppermute(outs[shift], "gx", pairs)
        got += [arrived[shift] for shift in range(4)]
    return finish(where, got).reshape(128, 1, 1, 4096)


def solution(mesh):
    return jax.shard_map(
        body,
        mesh=mesh,
        in_specs=(P(None, ("gx", "gy")), P(None, ("gx", "gy")), P(("gx", "gy"), None), P()),
        out_specs=P(None, "gx", "gy", None),
        check_vma=False,
    )
```
